32 devices in a mesh: row: 4 (over y, x), col: 8 (over z, core).
Axes of the slice: x: 2, y: 2, z: 4, core: 2. Of those that a mesh axis runs over, the one named last changes fastest.
Arguments:
- factor_tiles: float32 [8, 512, 4, 1024], P(None, 'row', None, 'col'), may hold values from -40 to 40, as said below
Outputs:
- rotated: float32 [4096, 4096], P(None, ('row', 'col'))
The draws below stay inside these ranges and needn't reach their ends.
Inputs may be any that keep to these rules, and one draw needn't show every extreme that they name: `factor_tiles`: upper triangular: entries below the diagonal are zero, entries on it are positive.
All inputs are finite; a program needn't handle non-finite values.
Results may differ from the reference program's by a relative error of at most 0.0003.
Values sent between devices are 32-bit elements; how exact they have to be, the bound alone decides.
No kernel may reach another device: no remote copies, remote signals or barrier semaphores. Data moves between devices by JAX's collectives and lax.ppermute only.
A program may use at most 128 MiB of HBM per device.

```python
import math
import jax
import jax.numpy as jnp
from jax import lax

LOGB = 7
OUTER = 4
INNER = 8
BLK = 128
NMAT = 4096
TILE_ROWS = 512
TILE_COLS = 1024


def draw_factor_tiles(key, part):
    keys = jax.random.split(jax.random.fold_in(key, 11), 5)
    order = NMAT
    rough = jnp.clip(jax.random.normal(keys[0], (order, order), jnp.float32), -6.0, 6.0)
    common = jnp.clip(jax.random.normal(keys[1], (order, 1), jnp.float32), -4.0, 4.0)
    row_scale = jnp.exp(jax.random.uniform(keys[2], (order, 1), jnp.float32, math.log(0.5), math.log(2.0)))
    col_scale = jnp.exp(jax.random.uniform(keys[3], (1, order), jnp.float32, math.log(0.5), math.log(5.0)))
    leading = 0.5 + jax.random.uniform(keys[4], (1, order), jnp.float32)
    row_ids = jnp.arange(order)[:, None]
    col_ids = jnp.arange(order)[None, :]
    upper_part = (rough + common) * math.sqrt(2.0 / order)
    core = jnp.where(row_ids < col_ids, upper_part, jnp.where(row_ids == col_ids, leading, 0.0))
    full_matrix = row_scale * col_scale * core
    return full_matrix.reshape(order // TILE_ROWS, TILE_ROWS, order // TILE_COLS, TILE_COLS).astype(jnp.float32)


def setup_inputs(seed: int = 0) -> dict:
    splits = jax.random.split(jax.random.key(seed), 2)
    return {
        "factor_tiles": draw_factor_tiles(jax.random.fold_in(splits[1], 71), 0),
    }


damping_ratio = 0.01


def pair_turn(matrix_in, cosine, sine_val, stride):
    orig_shape = matrix_in.shape
    groups = orig_shape[-1] // (2 * stride)
    split_view = matrix_in.reshape(orig_shape[:-1] + (groups, 2, stride))
    lead_part = split_view[..., 0, :]
    tail_part = split_view[..., 1, :]
    combined = jnp.stack([cosine * lead_part - sine_val * tail_part, sine_val * lead_part + cosine * tail_part], axis=-2)
    return combined.reshape(orig_shape)


def pair_angles(gram_matrix, stride):
    lead_dims = gram_matrix.shape[:-2]
    order = gram_matrix.shape[-1]
    groups = order // (2 * stride)
    diagonal = jnp.diagonal(gram_matrix, axis1=-2, axis2=-1).reshape(lead_dims + (groups, 2, stride))
    diag_p = diagonal[..., 0, :]
    diag_q = diagonal[..., 1, :]
    pair_rows = gram_matrix.reshape(lead_dims + (groups, 2, stride, order))[..., 0, :, :]
    target = jnp.arange(groups)[:, None] * (2 * stride) + stride + jnp.arange(stride)[None, :]
    selector = jnp.arange(order)[None, None, :] == target[:, :, None]
    cross = jnp.sum(jnp.where(selector, pair_rows, 0.0), axis=-1)
    diag_gap = diag_q - diag_p
    diag_sum = diag_p + diag_q
    rot_angle = 0.5 * jnp.arctan2(2.0 * cross * diag_gap, diag_gap * diag_gap + damping_ratio * diag_sum * diag_sum)
    return jnp.cos(rot_angle), jnp.sin(rot_angle)


def inner_solve(gram_matrix):
    order = gram_matrix.shape[-1]
    accum = jnp.broadcast_to(jnp.eye(order, dtype=gram_matrix.dtype), gram_matrix.shape)
    for inner_step in range(INNER):
        bit_index = (LOGB - 1 - inner_step) % LOGB
        stride = 2 ** bit_index
        cosine, sine_val = pair_angles(gram_matrix, stride)
        cos_wide = cosine[..., None, :, :]
        sin_wide = sine_val[..., None, :, :]
        gram_matrix = pair_turn(gram_matrix, cos_wide, sin_wide, stride)
        gram_matrix = jnp.swapaxes(pair_turn(jnp.swapaxes(gram_matrix, -1, -2), cos_wide, sin_wide, stride), -1, -2)
        accum = pair_turn(accum, cos_wide, sin_wide, stride)
    return accum


def reference(factor_tiles):
    order = NMAT
    slots_total = order // BLK
    half_width = BLK // 2
    full_matrix = factor_tiles.reshape(order, order)
    slot_columns = jnp.transpose(full_matrix.reshape(order, slots_total, BLK), (1, 0, 2))
    for round_index in range(OUTER):
        gram_matrix = jnp.einsum("pni,pnj->pij", slot_columns, slot_columns, precision=lax.Precision.HIGHEST)
        rotation = inner_solve(gram_matrix)
        slot_columns = jnp.einsum("pni,pij->pnj", slot_columns, rotation, precision=lax.Precision.HIGHEST)
        if round_index + 1 < OUTER:
            top_half = slot_columns[:, :, :half_width]
            bottom_half = slot_columns[:, :, half_width:]
            outgoing = jnp.concatenate([bottom_half[:1], top_half[1:]], axis=0)
            new_top = jnp.concatenate([top_half[:1], outgoing[:-1]], axis=0)
            new_bottom = jnp.concatenate([bottom_half[1:], top_half[-1:]], axis=0)
            slot_columns = jnp.concatenate([new_top, new_bottom], axis=2)
    return jnp.transpose(slot_columns, (1, 0, 2)).reshape(order, order)
```

```python
import functools

import jax
import jax.numpy as jnp
from jax import lax
from jax.experimental import pallas as pl
from jax.experimental.pallas import tpu as pltpu
from jax.sharding import PartitionSpec as P

LOGB = 7
OUTER = 4
INNER = 8
LANES = 128
SPAN = 512
DEPTH = 2048
PARTS = 4

damping_ratio = 0.01
vmem_bytes = 40 * 1024 * 1024


def partner_columns(value, stride):
    order = value.shape[-1]
    if 2 * stride == order:
        return pltpu.roll(value, stride, 1)
    column = lax.broadcasted_iota(jnp.int32, value.shape, 1)
    is_tail = jnp.bitwise_and(column, stride) != 0
    return jnp.where(is_tail, pltpu.roll(value, stride, 1), pltpu.roll(value, order - stride, 1))


def partner_rows(value, stride):
    order = value.shape[0]
    if stride >= 8:
        pieces = [value[start : start + stride] for start in range(0, order, stride)]
        return jnp.concatenate([pieces[place ^ 1] for place in range(len(pieces))], axis=0)
    row = lax.broadcasted_iota(jnp.int32, value.shape, 0)
    is_tail = jnp.bitwise_and(row, stride) != 0
    return jnp.where(is_tail, pltpu.roll(value, stride, 0), pltpu.roll(value, order - stride, 0))


def turn_of(own, other, cross):
    gap = own - other
    total = own + other
    base = gap * gap + damping_ratio * total * total
    tangent = jnp.where(base > 0.0, 2.0 * cross * gap / jnp.where(base > 0.0, base, 1.0), 0.0)
    inverse = lax.rsqrt(1.0 + tangent * tangent)
    square = 0.5 + 0.5 * inverse
    root = lax.rsqrt(square)
    return square * root, 0.5 * tangent * inverse * root


def inner_solve(gram):
    order = gram.shape[0]
    row = lax.broadcasted_iota(jnp.int32, gram.shape, 0)
    column = lax.broadcasted_iota(jnp.int32, gram.shape, 1)
    identity = row == column
    turned = jnp.where(identity, 1.0, 0.0).astype(jnp.float32)
    for step in range(INNER):
        stride = 2 ** ((LOGB - 1 - step) % LOGB)
        paired = jnp.bitwise_xor(row, stride) == column
        on_diagonal = jnp.where(identity, gram, 0.0)
        on_pair = jnp.where(paired, gram, 0.0)
        own_row = jnp.sum(on_diagonal, axis=0, keepdims=True)
        cross_row = jnp.sum(on_pair, axis=0, keepdims=True)
        own_col = jnp.sum(on_diagonal, axis=1, keepdims=True)
        cross_col = jnp.sum(on_pair, axis=1, keepdims=True)
        cos_row, sin_row = turn_of(own_row, partner_columns(own_row, stride), cross_row)
        cos_col, sin_col = turn_of(own_col, partner_rows(own_col, stride), cross_col)
        gram = gram * cos_row + partner_columns(gram, stride) * sin_row
        gram = gram * cos_col + partner_rows(gram, stride) * sin_col
        turned = turned * cos_col + partner_rows(turned, stride) * sin_col
    return turned


def three_parts(value):
    high = value.astype(jnp.bfloat16)
    rest = value - high.astype(jnp.float32)
    middle = rest.astype(jnp.bfloat16)
    return high, middle, (rest - middle.astype(jnp.float32)).astype(jnp.bfloat16)


def split_store(split_ref, value, start, lane):
    order = split_ref.shape[0] // 3
    rows, lanes = value.shape
    for place, part in enumerate(three_parts(value)):
        split_ref[pl.ds(place * order + start, rows), pl.ds(lane, lanes)] = part


def gram_of(split_ref):
    order = split_ref.shape[0] // 3
    total = split_ref.shape[1]

    def body(place, acc):
        lanes = pl.ds(pl.multiple_of(place * DEPTH, DEPTH), DEPTH)
        return acc + lax.dot_general(
            split_ref[:, lanes],
            split_ref[: 2 * order, lanes],
            (((1,), (1,)), ((), ())),
            preferred_element_type=jnp.float32,
        )

    acc = lax.fori_loop(0, total // DEPTH, body, jnp.zeros((3 * order, 2 * order), jnp.float32))
    outer = acc[2 * order :, :order]
    inner = acc[:order, order:] + acc[order : 2 * order, :order] + acc[order : 2 * order, order:]
    return acc[:order, :order] + (inner + (outer + outer.T))


def product(turned, split_ref, lane):
    order = split_ref.shape[0] // 3
    parts = three_parts(turned)
    lanes = pl.ds(lane, SPAN)
    weights = jnp.concatenate([jnp.concatenate([part, part], axis=1) for part in parts], axis=0)
    both = lax.dot_general(
        weights,
        split_ref[: 2 * order, lanes],
        (((1,), (0,)), ((), ())),
        preferred_element_type=jnp.float32,
    )
    small = lax.dot_general(
        parts[0],
        split_ref[2 * order :, lanes],
        (((1,), (0,)), ((), ())),
        preferred_element_type=jnp.float32,
    )
    return both[:order] + (both[order : 2 * order] + (both[2 * order :] + small))


def send_out(turned, split_ref, off_refs, on_refs, swap):
    order = split_ref.shape[0] // 3
    half = order // 2
    swapped = jnp.concatenate([turned[half:], turned[:half]], axis=0)
    arranged = jnp.where(swap, swapped, turned)
    length = off_refs[0].shape[1]
    for chunk, (off_ref, on_ref) in enumerate(zip(off_refs, on_refs)):

        def body(place, carry):
            lane = pl.multiple_of(place * SPAN, SPAN)
            lines = product(arranged, split_ref, pl.multiple_of(chunk * length + lane, SPAN))
            off_ref[:, pl.ds(lane, SPAN)] = lines[:half]
            on_ref[:, pl.ds(lane, SPAN)] = lines[half:]
            return carry

        lax.fori_loop(0, length // SPAN, body, 0)


def run_of(column, row, row_count, column_count):
    first = row_count - 1 - row
    last = jnp.where(row == row_count - 1, row, row_count - 2 - row)
    return jnp.where(column == 0, first, jnp.where(column == column_count - 1, last, row))


def prepare_kernel(in_ref, *out_refs):
    count = len(out_refs)
    rows = in_ref.shape[1] // count
    me = lax.axis_index("row")
    column, columns = lax.axis_index("col"), lax.axis_size("col")
    for offset in range(count):
        tile = run_of(column, jnp.bitwise_xor(me, offset), count, columns)
        out_refs[offset][...] = in_ref[0, pl.ds(tile, rows, stride=count), :].T


def off_is_bottom():
    column, columns = lax.axis_index("col"), lax.axis_size("col")
    run = run_of(column, lax.axis_index("row"), lax.axis_size("row"), columns)
    slot = run * columns + column
    return jnp.logical_and(jnp.bitwise_and(slot, 1) == 0, slot != 0)


def first_kernel(count, *refs):
    chunk_refs, out_refs, split_ref = refs[:count], refs[count:-1], refs[-1]
    parts = len(out_refs) // 2
    me = lax.axis_index("row")
    width = chunk_refs[0].shape[1] // parts
    for offset in range(count):
        lane = jnp.bitwise_xor(me, offset) * width
        for part in range(parts):
            split_store(
                split_ref,
                chunk_refs[offset][:, part * width : (part + 1) * width],
                0,
                pl.multiple_of(lane + part * count * width, width),
            )
    turned = inner_solve(gram_of(split_ref))
    send_out(turned, split_ref, out_refs[:parts], out_refs[parts:], off_is_bottom())


def load_halves(off_refs, on_refs, split_ref):
    half, length = off_refs[0].shape
    odd = jnp.bitwise_and(lax.axis_index("col"), 1)
    off_start = pl.multiple_of(odd * half, half)
    on_start = pl.multiple_of((1 - odd) * half, half)
    for chunk, (off_ref, on_ref) in enumerate(zip(off_refs, on_refs)):

        def body(place, carry):
            lane = pl.multiple_of(place * SPAN, SPAN)
            there = pl.multiple_of(chunk * length + lane, SPAN)
            split_store(split_ref, off_ref[:, pl.ds(lane, SPAN)], off_start, there)
            split_store(split_ref, on_ref[:, pl.ds(lane, SPAN)], on_start, there)
            return carry

        lax.fori_loop(0, length // SPAN, body, 0)


def middle_kernel(*refs):
    split_ref = refs[-1]
    parts = len(refs) // 4
    off_in, on_in, off_out, on_out = (refs[place * parts : (place + 1) * parts] for place in range(4))
    load_halves(off_in, on_in, split_ref)
    turned = inner_solve(gram_of(split_ref))
    send_out(turned, split_ref, off_out, on_out, off_is_bottom())


def last_kernel(count, *refs):
    out_ref, split_ref = refs[-2:]
    parts = len(refs) // 2 - 1
    load_halves(refs[:parts], refs[parts : 2 * parts], split_ref)
    turned = inner_solve(gram_of(split_ref))
    total = split_ref.shape[1]
    per_part = total // (parts * LANES)
    cycles = per_part // count
    per_span = SPAN // LANES

    def body(place, carry):
        lines = product(turned, split_ref, pl.multiple_of(place * SPAN, SPAN))
        for piece in range(per_span):
            block = place * per_span + piece
            part, inside = block // per_part, block % per_part
            source, cycle = inside // cycles, inside % cycles
            start = pl.multiple_of(((part * cycles + cycle) * count + source) * LANES, LANES)
            out_ref[pl.ds(start, LANES), :] = lines[:, piece * LANES : (piece + 1) * LANES].T
        return carry

    lax.fori_loop(0, total // SPAN, body, 0)


def in_vmem(count):
    return [pl.BlockSpec(memory_space=pltpu.VMEM)] * count


def mixed_place(slot, row_count, column_count):
    run, column = divmod(slot, column_count)
    if column == 0:
        run = row_count - 1 - run
    elif column == column_count - 1 and run != row_count - 1:
        run = row_count - 2 - run
    return run * column_count + column


def move_pairs(move, chunk, chunk_rows, width, row_count, column_count):
    slots = row_count * column_count
    off_pairs, on_pairs = [], []
    for slot in range(slots):
        if (slot + move + 1) * width <= chunk * chunk_rows:
            continue
        source = mixed_place(slot, row_count, column_count)
        off_target = slot + 1 if slot % 2 else slot - 1
        if not 0 <= off_target < slots:
            off_target = slot
        on_target = slot ^ 1
        if move < OUTER - 2:
            off_target = mixed_place(off_target, row_count, column_count)
            on_target = mixed_place(on_target, row_count, column_count)
        off_pairs.append((source, off_target))
        on_pairs.append((source, on_target))
    return off_pairs, on_pairs


def per_device(factor_tiles):
    cycles, rows, tiles, width = factor_tiles.shape
    count, columns = lax.axis_size("row"), lax.axis_size("col")
    half = width // 2
    length = cycles * rows * count
    parts = PARTS
    params = pltpu.CompilerParams(vmem_limit_bytes=vmem_bytes)
    halves = [jax.ShapeDtypeStruct((half, length // parts), jnp.float32)] * (2 * parts)
    scratch = [pltpu.VMEM((3 * width, length), jnp.bfloat16)]

    chunks = pl.pallas_call(
        prepare_kernel,
        grid=(cycles,),
        in_specs=[pl.BlockSpec((1, rows * tiles, width), lambda i: (i, 0, 0))],
        out_specs=[pl.BlockSpec((width, rows), lambda i: (0, i))] * tiles,
        out_shape=[jax.ShapeDtypeStruct((width, cycles * rows), jnp.float32)] * tiles,
        compiler_params=params,
        name="prepare",
    )(factor_tiles.reshape(cycles, rows * tiles, width))
    received = [chunks[0]] + [None] * (tiles - 1)
    for offset in range(tiles - 1, 0, -1):
        received[offset] = lax.ppermute(
            chunks[offset], "row", [(source, source ^ offset) for source in range(count)]
        )

    moved = pl.pallas_call(
        functools.partial(first_kernel, tiles),
        in_specs=in_vmem(tiles),
        out_specs=in_vmem(2 * parts),
        out_shape=halves,
        scratch_shapes=scratch,
        compiler_params=params,
        name="first_round",
    )(*received)
    for round_index in range(1, OUTER):
        off_halves, on_halves = list(moved[:parts]), list(moved[parts:])
        for part in range(parts):
            off_pairs, on_pairs = move_pairs(
                round_index - 1, part, length // parts, width, count, columns
            )
            off_halves[part] = lax.ppermute(off_halves[part], ("row", "col"), off_pairs)
            on_halves[part] = lax.ppermute(on_halves[part], ("row", "col"), on_pairs)
        if round_index + 1 < OUTER:
            moved = pl.pallas_call(
                middle_kernel,
                in_specs=in_vmem(2 * parts),
                out_specs=in_vmem(2 * parts),
                out_shape=halves,
                scratch_shapes=scratch,
                compiler_params=params,
                name="middle_round",
            )(*off_halves, *on_halves)
    return pl.pallas_call(
        functools.partial(last_kernel, count),
        in_specs=in_vmem(2 * parts),
        out_specs=pl.BlockSpec(memory_space=pltpu.VMEM),
        out_shape=jax.ShapeDtypeStruct((length, width), jnp.float32),
        scratch_shapes=scratch,
        compiler_params=params,
        name="last_round",
    )(*off_halves, *on_halves)


def solution(mesh):
    return jax.shard_map(
        per_device,
        mesh=mesh,
        in_specs=(P(None, "row", None, "col"),),
        out_specs=P(None, ("row", "col")),
        check_vma=False,
    )
```

```python
import functools

import jax
import jax.numpy as jnp
from jax import lax
from jax.experimental import pallas as pl
from jax.experimental.pallas import tpu as pltpu
from jax.sharding import PartitionSpec as P

LOGB = 7
OUTER = 4
INNER = 8
LANES = 128
SPAN = 512
DEPTH = 2048
PARTS = 4

damping_ratio = 0.01
spare_bytes = 2048


def partner_columns(value, stride):
    order = value.shape[-1]
    if 2 * stride == order:
        return pltpu.roll(value, stride, 1)
    column = lax.broadcasted_iota(jnp.int32, value.shape, 1)
    is_tail = jnp.bitwise_and(column, stride) != 0
    return jnp.where(is_tail, pltpu.roll(value, stride, 1), pltpu.roll(value, order - stride, 1))


def partner_rows(value, stride):
    order = value.shape[0]
    if stride >= 8:
        pieces = [value[start : start + stride] for start in range(0, order, stride)]
        return jnp.concatenate([pieces[place ^ 1] for place in range(len(pieces))], axis=0)
    row = lax.broadcasted_iota(jnp.int32, value.shape, 0)
    is_tail = jnp.bitwise_and(row, stride) != 0
    return jnp.where(is_tail, pltpu.roll(value, stride, 0), pltpu.roll(value, order - stride, 0))


def turn_of(own, other, cross):
    gap = own - other
    total = own + other
    base = gap * gap + damping_ratio * total * total
    tangent = jnp.where(base > 0.0, 2.0 * cross * gap / jnp.where(base > 0.0, base, 1.0), 0.0)
    inverse = lax.rsqrt(1.0 + tangent * tangent)
    square = 0.5 + 0.5 * inverse
    root = lax.rsqrt(square)
    return square * root, 0.5 * tangent * inverse * root


def inner_solve(*grams):
    shape = grams[0].shape
    row = lax.broadcasted_iota(jnp.int32, shape, 0)
    column = lax.broadcasted_iota(jnp.int32, shape, 1)
    identity = row == column
    state = [(gram, jnp.where(identity, 1.0, 0.0).astype(jnp.float32)) for gram in grams]
    for step in range(INNER):
        stride = 2 ** ((LOGB - 1 - step) % LOGB)
        paired = jnp.bitwise_xor(row, stride) == column
        after = []
        for gram, turned in state:
            on_diagonal = jnp.where(identity, gram, 0.0)
            on_pair = jnp.where(paired, gram, 0.0)
            own_row = jnp.sum(on_diagonal, axis=0, keepdims=True)
            cross_row = jnp.sum(on_pair, axis=0, keepdims=True)
            own_col = jnp.sum(on_diagonal, axis=1, keepdims=True)
            cross_col = jnp.sum(on_pair, axis=1, keepdims=True)
            cos_row, sin_row = turn_of(own_row, partner_columns(own_row, stride), cross_row)
            cos_col, sin_col = turn_of(own_col, partner_rows(own_col, stride), cross_col)
            if step + 1 < INNER:
                gram = gram * cos_row + partner_columns(gram, stride) * sin_row
                gram = gram * cos_col + partner_rows(gram, stride) * sin_col
            after.append((gram, turned * cos_col + partner_rows(turned, stride) * sin_col))
        state = after
    return [turned for _, turned in state]


def three_parts(value):
    high = value.astype(jnp.bfloat16)
    rest = value - high.astype(jnp.float32)
    middle = rest.astype(jnp.bfloat16)
    return high, middle, (rest - middle.astype(jnp.float32)).astype(jnp.bfloat16)


def split_store(split_ref, value, start, lane):
    order = split_ref.shape[0] // 3
    rows, lanes = value.shape
    for place, part in enumerate(three_parts(value)):
        split_ref[pl.ds(place * order + start, rows), pl.ds(lane, lanes)] = part


def gram_of(split_ref):
    order = split_ref.shape[0] // 3
    total = split_ref.shape[1]

    def body(place, acc):
        lanes = pl.ds(pl.multiple_of(place * DEPTH, DEPTH), DEPTH)
        return acc + lax.dot_general(
            split_ref[:, lanes],
            split_ref[: 2 * order, lanes],
            (((1,), (1,)), ((), ())),
            preferred_element_type=jnp.float32,
        )

    acc = lax.fori_loop(0, total // DEPTH, body, jnp.zeros((3 * order, 2 * order), jnp.float32))
    outer = acc[2 * order :, :order]
    inner = acc[:order, order:] + acc[order : 2 * order, :order] + acc[order : 2 * order, order:]
    return acc[:order, :order] + (inner + (outer + outer.T))


def product(turned, split_ref, lane):
    order = split_ref.shape[0] // 3
    rows = turned.shape[0]
    parts = three_parts(turned)
    lanes = pl.ds(lane, SPAN)
    weights = jnp.concatenate([jnp.concatenate([part, part], axis=1) for part in parts], axis=0)
    both = lax.dot_general(
        weights,
        split_ref[: 2 * order, lanes],
        (((1,), (0,)), ((), ())),
        preferred_element_type=jnp.float32,
    )
    small = lax.dot_general(
        parts[0],
        split_ref[2 * order :, lanes],
        (((1,), (0,)), ((), ())),
        preferred_element_type=jnp.float32,
    )
    return both[:rows] + (both[rows : 2 * rows] + (both[2 * rows :] + small))


def spans(length, body):
    def step(place, carry):
        body(pl.multiple_of(place * SPAN, SPAN))
        return carry

    lax.fori_loop(0, length // SPAN, step, 0)


def load_rows(split_ref, refs, start):
    length = refs[0].shape[1]
    for chunk, ref in enumerate(refs):

        def body(lane):
            split_store(
                split_ref,
                ref[:, pl.ds(lane, SPAN)],
                start,
                pl.multiple_of(chunk * length + lane, SPAN),
            )

        spans(length, body)


def send_out(turned, split_ref, first_refs, second_refs, swap):
    half = split_ref.shape[0] // 6
    swapped = jnp.concatenate([turned[half:], turned[:half]], axis=0)
    arranged = jnp.where(swap, swapped, turned)
    length = first_refs[0].shape[1]
    for chunk, (first_ref, second_ref) in enumerate(zip(first_refs, second_refs)):

        def body(lane):
            lines = product(arranged, split_ref, pl.multiple_of(chunk * length + lane, SPAN))
            first_ref[:, pl.ds(lane, SPAN)] = lines[:half]
            second_ref[:, pl.ds(lane, SPAN)] = lines[half:]

        spans(length, body)


def run_of(column, row, row_count):
    return jnp.where(jnp.bitwise_and(column, 1) == 0, row, row_count - 1 - row)


def hosted_slot():
    column = lax.axis_index("col")
    run = run_of(column, lax.axis_index("row"), lax.axis_size("row"))
    return run * lax.axis_size("col") + column


def slot_count():
    return lax.axis_size("row") * lax.axis_size("col")


def prepare_kernel(in_ref, *out_refs):
    count = len(out_refs)
    rows = in_ref.shape[1] // count
    me = lax.axis_index("row")
    for offset in range(count):
        tile = run_of(lax.axis_index("col"), jnp.bitwise_xor(me, offset), count)
        out_refs[offset][...] = in_ref[0, pl.ds(tile, rows, stride=count), :].T


def first_kernel(count, *refs):
    chunk_refs, out_refs, edge_ref, split_ref = refs[:count], refs[count:-2], refs[-2], refs[-1]
    parts = len(out_refs) // 2
    tops, bottoms = out_refs[:parts], out_refs[parts:]
    me = lax.axis_index("row")
    width = chunk_refs[0].shape[1] // parts
    for offset in range(count):
        lane = jnp.bitwise_xor(me, offset) * width
        for part in range(parts):
            split_store(
                split_ref,
                chunk_refs[offset][:, part * width : (part + 1) * width],
                0,
                pl.multiple_of(lane + part * count * width, width),
            )
    (turned,) = inner_solve(gram_of(split_ref))
    slot, slots = hosted_slot(), slot_count()
    send_out(turned, split_ref, tops, bottoms, slot == 0)
    length = tops[0].shape[1]

    def edge_from(refs):
        for part, ref in enumerate(refs):
            edge_ref[:, part * length : (part + 1) * length] = ref[...]

    pl.when(slot <= 1)(lambda: edge_from(bottoms))
    pl.when(slot >= slots - 2)(lambda: edge_from(tops))


def middle_kernel(*refs):
    off_out, on_out, left_ref, right_ref = refs[-4:]
    edge = refs[-5:-4]
    parts = (len(refs) - 5) // 4
    from_left, from_right, tops, bottoms = (
        refs[place * parts : (place + 1) * parts] for place in range(4)
    )
    slot, slots = hosted_slot(), slot_count()
    half = off_out.shape[0]
    load_rows(left_ref, from_left, 0)
    load_rows(left_ref, bottoms, half)
    load_rows(right_ref, tops, 0)
    load_rows(right_ref, from_right, half)

    @pl.when(slot == 0)
    def _():
        load_rows(left_ref, bottoms, 0)
        load_rows(left_ref, edge, half)

    @pl.when(slot == 1)
    def _():
        load_rows(left_ref, edge, 0)

    @pl.when(slot == slots - 2)
    def _():
        load_rows(right_ref, edge, half)

    @pl.when(slot == slots - 1)
    def _():
        load_rows(right_ref, edge, 0)
        load_rows(right_ref, tops, half)

    left, right = inner_solve(gram_of(left_ref), gram_of(right_ref))
    to_top = jnp.where(slot == 1, left[half:], left[:half])
    to_bottom = jnp.where(slot == slots - 1, right[:half], right[half:])

    def body(lane):
        top = product(to_top, left_ref, lane)
        bottom = product(to_bottom, right_ref, lane)
        split_store(left_ref, top, 0, lane)
        split_store(left_ref, bottom, half, lane)

    spans(left_ref.shape[1], body)
    (turned,) = inner_solve(gram_of(left_ref))
    swap = jnp.logical_and(jnp.bitwise_and(slot, 1) == 0, slot != 0)
    send_out(turned, left_ref, [off_out], [on_out], swap)


def last_kernel(count, parts, off_in, on_in, out_ref, split_ref):
    half = off_in.shape[0]
    odd = jnp.bitwise_and(lax.axis_index("col"), 1)
    load_rows(split_ref, [off_in], pl.multiple_of(odd * half, half))
    load_rows(split_ref, [on_in], pl.multiple_of((1 - odd) * half, half))
    (turned,) = inner_solve(gram_of(split_ref))
    total = split_ref.shape[1]
    per_part = total // (parts * LANES)
    cycles = per_part // count

    def body(lane):
        lines = product(turned, split_ref, lane)
        for piece in range(SPAN // LANES):
            block = lane // LANES + piece
            part, inside = block // per_part, block % per_part
            source, cycle = inside // cycles, inside % cycles
            start = pl.multiple_of(((part * cycles + cycle) * count + source) * LANES, LANES)
            out_ref[pl.ds(start, LANES), :] = lines[:, piece * LANES : (piece + 1) * LANES].T

    spans(total, body)


def in_vmem(count):
    return [pl.BlockSpec(memory_space=pltpu.VMEM)] * count


def host_of(slot, row_count, column_count):
    run, column = divmod(slot, column_count)
    row = row_count - 1 - run if column % 2 else run
    return row * column_count + column


def far_pairs(step, first_row, width, row_count, column_count):
    slots = row_count * column_count
    return [
        (host_of(slot, row_count, column_count), host_of(slot + step, row_count, column_count))
        for slot in range(slots)
        if 0 <= slot + step < slots and (slot + 1) * width > first_row
    ]


def per_device(factor_tiles):
    cycles, rows, tiles, width = factor_tiles.shape
    count, columns = lax.axis_size("row"), lax.axis_size("col")
    slots = count * columns
    half = width // 2
    length = cycles * rows * count
    parts = PARTS
    axes = ("row", "col")
    split_bytes, spare = 6 * width * length, spare_bytes * length
    params = pltpu.CompilerParams(vmem_limit_bytes=split_bytes + spare)
    more_params = pltpu.CompilerParams(vmem_limit_bytes=2 * split_bytes + spare)
    whole_half = jax.ShapeDtypeStruct((half, length), jnp.float32)
    part_half = jax.ShapeDtypeStruct((half, length // parts), jnp.float32)
    split = pltpu.VMEM((3 * width, length), jnp.bfloat16)

    chunks = pl.pallas_call(
        prepare_kernel,
        grid=(cycles,),
        in_specs=[pl.BlockSpec((1, rows * tiles, width), lambda i: (i, 0, 0))],
        out_specs=[pl.BlockSpec((width, rows), lambda i: (0, i))] * tiles,
        out_shape=[jax.ShapeDtypeStruct((width, cycles * rows), jnp.float32)] * tiles,
        compiler_params=params,
        name="prepare",
    )(factor_tiles.reshape(cycles, rows * tiles, width))
    received = [chunks[0]] + [None] * (tiles - 1)
    for offset in range(tiles - 1, 0, -1):
        received[offset] = lax.ppermute(
            chunks[offset], "row", [(source, source ^ offset) for source in range(count)]
        )

    *halves, edge = pl.pallas_call(
        functools.partial(first_kernel, tiles),
        in_specs=in_vmem(tiles),
        out_specs=in_vmem(2 * parts + 1),
        out_shape=[part_half] * (2 * parts) + [whole_half],
        scratch_shapes=[split],
        compiler_params=params,
        name="first_round",
    )(*received)
    tops, bottoms = halves[:parts], halves[parts:]

    from_left, from_right = [], []
    for part in range(parts):
        first_row = part * (length // parts)
        from_left.append(
            lax.ppermute(tops[part], axes, far_pairs(2, first_row, width, count, columns))
        )
        from_right.append(
            lax.ppermute(bottoms[part], axes, far_pairs(-2, first_row, width, count, columns))
        )
    ends = [(0, 1), (1, 0), (slots - 2, slots - 1), (slots - 1, slots - 2)]
    edge = lax.ppermute(
        edge, axes, [tuple(host_of(slot, count, columns) for slot in pair) for pair in ends]
    )
    off, on = pl.pallas_call(
        middle_kernel,
        in_specs=in_vmem(4 * parts + 1),
        out_specs=in_vmem(2),
        out_shape=[whole_half] * 2,
        scratch_shapes=[split] * 2,
        compiler_params=more_params,
        name="middle_rounds",
    )(*from_left, *from_right, *tops, *bottoms, edge)

    off_pairs, on_pairs = [], []
    for slot in range(slots):
        target = slot + 1 if slot % 2 else slot - 1
        source = host_of(slot, count, columns)
        off_pairs.append((source, target if 0 <= target < slots else slot))
        on_pairs.append((source, slot ^ 1))
    off = lax.ppermute(off, axes, off_pairs)
    on = lax.ppermute(on, axes, on_pairs)
    return pl.pallas_call(
        functools.partial(last_kernel, count, parts),
        in_specs=in_vmem(2),
        out_specs=pl.BlockSpec(memory_space=pltpu.VMEM),
        out_shape=jax.ShapeDtypeStruct((length, width), jnp.float32),
        scratch_shapes=[split],
        compiler_params=params,
        name="last_round",
    )(off, on)


def solution(mesh):
    return jax.shard_map(
        per_device,
        mesh=mesh,
        in_specs=(P(None, "row", None, "col"),),
        out_specs=P(None, ("row", "col")),
        check_vma=False,
    )
```

```python
import functools

import jax
import jax.numpy as jnp
from jax import lax
from jax.experimental import pallas as pl
from jax.experimental.pallas import tpu as pltpu
from jax.sharding import PartitionSpec as P

LOGB = 7
OUTER = 4
INNER = 8
LANES = 128
SPAN = 512
DEPTH = 2048
PARTS = 4

damping_ratio = 0.01
spare_bytes = 2048


def partner_columns(value, stride):
    order = value.shape[-1]
    if 2 * stride == order:
        return pltpu.roll(value, stride, 1)
    column = lax.broadcasted_iota(jnp.int32, value.shape, 1)
    is_tail = jnp.bitwise_and(column, stride) != 0
    return jnp.where(is_tail, pltpu.roll(value, stride, 1), pltpu.roll(value, order - stride, 1))


def partner_rows(value, stride):
    order = value.shape[0]
    if stride >= 8:
        pieces = [value[start : start + stride] for start in range(0, order, stride)]
        return jnp.concatenate([pieces[place ^ 1] for place in range(len(pieces))], axis=0)
    row = lax.broadcasted_iota(jnp.int32, value.shape, 0)
    is_tail = jnp.bitwise_and(row, stride) != 0
    return jnp.where(is_tail, pltpu.roll(value, stride, 0), pltpu.roll(value, order - stride, 0))


def turn_of(own, other, cross):
    gap = own - other
    total = own + other
    base = gap * gap + damping_ratio * total * total
    tangent = jnp.where(base > 0.0, 2.0 * cross * gap / jnp.where(base > 0.0, base, 1.0), 0.0)
    inverse = lax.rsqrt(1.0 + tangent * tangent)
    square = 0.5 + 0.5 * inverse
    root = lax.rsqrt(square)
    return square * root, 0.5 * tangent * inverse * root


def inner_solve(*grams):
    shape = grams[0].shape
    row = lax.broadcasted_iota(jnp.int32, shape, 0)
    column = lax.broadcasted_iota(jnp.int32, shape, 1)
    identity = row == column
    state = [(gram, jnp.where(identity, 1.0, 0.0).astype(jnp.float32)) for gram in grams]
    for step in range(INNER):
        stride = 2 ** ((LOGB - 1 - step) % LOGB)
        paired = jnp.bitwise_xor(row, stride) == column
        after = []
        for gram, turned in state:
            on_diagonal = jnp.where(identity, gram, 0.0)
            on_pair = jnp.where(paired, gram, 0.0)
            own_row = jnp.sum(on_diagonal, axis=0, keepdims=True)
            cross_row = jnp.sum(on_pair, axis=0, keepdims=True)
            cos_row, sin_row = turn_of(own_row, partner_columns(own_row, stride), cross_row)
            cos_col = jnp.sum(jnp.where(identity, cos_row, 0.0), axis=1, keepdims=True)
            sin_col = jnp.sum(jnp.where(identity, sin_row, 0.0), axis=1, keepdims=True)
            if step + 1 < INNER:
                gram = gram * cos_row + partner_columns(gram, stride) * sin_row
                gram = gram * cos_col + partner_rows(gram, stride) * sin_col
            after.append((gram, turned * cos_col + partner_rows(turned, stride) * sin_col))
        state = after
    return [turned for _, turned in state]


def three_parts(value):
    high = value.astype(jnp.bfloat16)
    rest = value - high.astype(jnp.float32)
    middle = rest.astype(jnp.bfloat16)
    return high, middle, (rest - middle.astype(jnp.float32)).astype(jnp.bfloat16)


def split_store(split_ref, value, start, lane):
    order = split_ref.shape[0] // 3
    rows, lanes = value.shape
    for place, part in enumerate(three_parts(value)):
        split_ref[pl.ds(place * order + start, rows), pl.ds(lane, lanes)] = part


def gram_of(split_ref):
    order = split_ref.shape[0] // 3
    total = split_ref.shape[1]

    def body(place, acc):
        lanes = pl.ds(pl.multiple_of(place * DEPTH, DEPTH), DEPTH)
        return acc + lax.dot_general(
            split_ref[:, lanes],
            split_ref[: 2 * order, lanes],
            (((1,), (1,)), ((), ())),
            preferred_element_type=jnp.float32,
        )

    acc = lax.fori_loop(0, total // DEPTH, body, jnp.zeros((3 * order, 2 * order), jnp.float32))
    outer = acc[2 * order :, :order]
    inner = acc[:order, order:] + acc[order : 2 * order, :order] + acc[order : 2 * order, order:]
    return acc[:order, :order] + (inner + (outer + outer.T))


def product(turned, split_ref, lane):
    order = split_ref.shape[0] // 3
    rows = turned.shape[0]
    parts = three_parts(turned)
    lanes = pl.ds(lane, SPAN)
    weights = jnp.concatenate([jnp.concatenate([part, part], axis=1) for part in parts], axis=0)
    both = lax.dot_general(
        weights,
        split_ref[: 2 * order, lanes],
        (((1,), (0,)), ((), ())),
        preferred_element_type=jnp.float32,
    )
    small = lax.dot_general(
        parts[0],
        split_ref[2 * order :, lanes],
        (((1,), (0,)), ((), ())),
        preferred_element_type=jnp.float32,
    )
    return both[:rows] + (both[rows : 2 * rows] + (both[2 * rows :] + small))


def spans(length, body):
    def step(place, carry):
        body(pl.multiple_of(place * SPAN, SPAN))
        return carry

    lax.fori_loop(0, length // SPAN, step, 0)


def load_rows(split_ref, refs, start):
    done = 0
    for ref in refs:

        def body(lane):
            split_store(
                split_ref, ref[:, pl.ds(lane, SPAN)], start, pl.multiple_of(done + lane, SPAN)
            )

        spans(ref.shape[1], body)
        done += ref.shape[1]


def send_out(turned, split_ref, first_refs, second_refs, swap):
    half = split_ref.shape[0] // 6
    swapped = jnp.concatenate([turned[half:], turned[:half]], axis=0)
    arranged = jnp.where(swap, swapped, turned)
    done = 0
    for first_ref, second_ref in zip(first_refs, second_refs):

        def body(lane):
            lines = product(arranged, split_ref, pl.multiple_of(done + lane, SPAN))
            first_ref[:, pl.ds(lane, SPAN)] = lines[:half]
            second_ref[:, pl.ds(lane, SPAN)] = lines[half:]

        spans(first_ref.shape[1], body)
        done += first_ref.shape[1]


def run_of(column, row, row_count):
    return jnp.where(jnp.bitwise_and(column, 1) == 0, row, row_count - 1 - row)


def hosted_slot():
    column = lax.axis_index("col")
    run = run_of(column, lax.axis_index("row"), lax.axis_size("row"))
    return run * lax.axis_size("col") + column


def slot_count():
    return lax.axis_size("row") * lax.axis_size("col")


def prepare_kernel(in_ref, *out_refs):
    count = len(out_refs)
    rows = in_ref.shape[1] // count
    me = lax.axis_index("row")
    for offset in range(count):
        tile = run_of(lax.axis_index("col"), jnp.bitwise_xor(me, offset), count)
        out_refs[offset][...] = in_ref[0, pl.ds(tile, rows, stride=count), :].T


def odd_chip(slot):
    return jnp.bitwise_and(slot // 2, 1)


def first_kernel(count, *refs):
    chunk_refs, out_refs, split_ref = refs[:count], refs[count:-1], refs[-1]
    sizes = len(out_refs) // 2
    me = lax.axis_index("row")
    width = chunk_refs[0].shape[1] // PARTS
    for offset in range(count):
        lane = jnp.bitwise_xor(me, offset) * width
        for part in range(PARTS):
            split_store(
                split_ref,
                chunk_refs[offset][:, part * width : (part + 1) * width],
                0,
                pl.multiple_of(lane + part * count * width, width),
            )
    (turned,) = inner_solve(gram_of(split_ref))
    slot = hosted_slot()
    bottom_first = jnp.logical_or(odd_chip(slot) == 1, slot == 0)
    send_out(turned, split_ref, out_refs[:sizes], out_refs[sizes:], bottom_first)


def middle_kernel(*refs):
    off_out, on_out, near_ref, far_ref = refs[-4:]
    sizes = (len(refs) - 4) // 4
    near_in, far_in, first, second = (
        refs[place * sizes : (place + 1) * sizes] for place in range(4)
    )
    slot, slots = hosted_slot(), slot_count()
    half = off_out.shape[0]
    odd = odd_chip(slot)
    at_end = jnp.logical_or(slot == 0, slot == slots - 1).astype(jnp.int32)
    near_own = pl.multiple_of(odd * half, half)
    near_other = pl.multiple_of((1 - odd) * half, half)
    far_own = pl.multiple_of(jnp.bitwise_xor(1 - odd, at_end) * half, half)
    far_other = pl.multiple_of(jnp.bitwise_xor(odd, at_end) * half, half)
    load_rows(near_ref, first, near_own)
    load_rows(near_ref, near_in, near_other)
    load_rows(far_ref, second, far_own)
    load_rows(far_ref, far_in, far_other)
    near, far = inner_solve(gram_of(near_ref), gram_of(far_ref))
    near_half = jnp.where(odd == 0, near[half:], near[:half])
    flipped = jnp.logical_or(slot == 1, slot == slots - 1)
    far_bottom = jnp.logical_xor(odd == 1, flipped)
    far_half = jnp.where(far_bottom, far[half:], far[:half])

    def body(lane):
        near_lines = product(near_half, near_ref, lane)
        far_lines = product(far_half, far_ref, lane)
        split_store(near_ref, near_lines, near_other, lane)
        split_store(near_ref, far_lines, near_own, lane)

    spans(near_ref.shape[1], body)
    (turned,) = inner_solve(gram_of(near_ref))
    swap = jnp.logical_and(jnp.bitwise_and(slot, 1) == 0, slot != 0)
    send_out(turned, near_ref, [off_out], [on_out], swap)


def last_kernel(count, off_in, on_in, out_ref, split_ref):
    half = off_in.shape[0]
    odd = jnp.bitwise_and(lax.axis_index("col"), 1)
    load_rows(split_ref, [off_in], pl.multiple_of(odd * half, half))
    load_rows(split_ref, [on_in], pl.multiple_of((1 - odd) * half, half))
    (turned,) = inner_solve(gram_of(split_ref))
    total = split_ref.shape[1]
    per_part = total // (PARTS * LANES)
    cycles = per_part // count

    def body(lane):
        lines = product(turned, split_ref, lane)
        for piece in range(SPAN // LANES):
            block = lane // LANES + piece
            part, inside = block // per_part, block % per_part
            source, cycle = inside // cycles, inside % cycles
            start = pl.multiple_of(((part * cycles + cycle) * count + source) * LANES, LANES)
            out_ref[pl.ds(start, LANES), :] = lines[:, piece * LANES : (piece + 1) * LANES].T

    spans(total, body)


def in_vmem(count):
    return [pl.BlockSpec(memory_space=pltpu.VMEM)] * count


def host_of(slot, row_count, column_count):
    run, column = divmod(slot, column_count)
    row = row_count - 1 - run if column % 2 else run
    return row * column_count + column


def swap_pairs(first_row, width, row_count, column_count):
    slots = row_count * column_count
    near_pairs, far_pairs = [], []
    for slot in range(slots):
        if (slot + 1) * width <= first_row:
            continue
        source = host_of(slot, row_count, column_count)
        step = -2 if slot // 2 % 2 else 2
        near_pairs.append((source, host_of(slot + step, row_count, column_count)))
        target = slot - step if 0 <= slot - step < slots else slot ^ 1
        far_pairs.append((source, host_of(target, row_count, column_count)))
    return near_pairs, far_pairs


def per_device(factor_tiles):
    cycles, rows, tiles, width = factor_tiles.shape
    count, columns = lax.axis_size("row"), lax.axis_size("col")
    slots = count * columns
    half = width // 2
    length = cycles * rows * count
    axes = ("row", "col")
    split_bytes, spare = 6 * width * length, spare_bytes * length
    params = pltpu.CompilerParams(vmem_limit_bytes=split_bytes + spare)
    more_params = pltpu.CompilerParams(vmem_limit_bytes=2 * split_bytes + spare)
    whole_half = jax.ShapeDtypeStruct((half, length), jnp.float32)
    split = pltpu.VMEM((3 * width, length), jnp.bfloat16)

    chunks = pl.pallas_call(
        prepare_kernel,
        grid=(cycles,),
        in_specs=[pl.BlockSpec((1, rows * tiles, width), lambda i: (i, 0, 0))],
        out_specs=[pl.BlockSpec((width, rows), lambda i: (0, i))] * tiles,
        out_shape=[jax.ShapeDtypeStruct((width, cycles * rows), jnp.float32)] * tiles,
        compiler_params=params,
        name="prepare",
    )(factor_tiles.reshape(cycles, rows * tiles, width))
    received = [chunks[0]] + [None] * (tiles - 1)
    for offset in range(tiles - 1, 0, -1):
        received[offset] = lax.ppermute(
            chunks[offset], "row", [(source, source ^ offset) for source in range(count)]
        )

    part = length // PARTS
    starts = [0, 2 * part] + [place * part for place in range(3, PARTS)]
    ends = starts[1:] + [length]
    sizes = len(starts)
    halves = [
        jax.ShapeDtypeStruct((half, end - start), jnp.float32) for start, end in zip(starts, ends)
    ]
    moved = pl.pallas_call(
        functools.partial(first_kernel, tiles),
        in_specs=in_vmem(tiles),
        out_specs=in_vmem(2 * sizes),
        out_shape=halves * 2,
        scratch_shapes=[split],
        compiler_params=params,
        name="first_round",
    )(*received)
    near, far = list(moved[:sizes]), list(moved[sizes:])
    for place in reversed(range(sizes)):
        near_pairs, far_pairs = swap_pairs(starts[place], width, count, columns)
        near[place] = lax.ppermute(near[place], axes, near_pairs)
        far[place] = lax.ppermute(far[place], axes, far_pairs)
    off, on = pl.pallas_call(
        middle_kernel,
        in_specs=in_vmem(4 * sizes),
        out_specs=in_vmem(2),
        out_shape=[whole_half] * 2,
        scratch_shapes=[split] * 2,
        compiler_params=more_params,
        name="middle_rounds",
    )(*near, *far, *moved)

    off_pairs, on_pairs = [], []
    for slot in range(slots):
        target = slot + 1 if slot % 2 else slot - 1
        source = host_of(slot, count, columns)
        off_pairs.append((source, target if 0 <= target < slots else slot))
        on_pairs.append((source, slot ^ 1))
    off = lax.ppermute(off, axes, off_pairs)
    on = lax.ppermute(on, axes, on_pairs)
    return pl.pallas_call(
        functools.partial(last_kernel, count),
        in_specs=in_vmem(2),
        out_specs=pl.BlockSpec(memory_space=pltpu.VMEM),
        out_shape=jax.ShapeDtypeStruct((length, width), jnp.float32),
        scratch_shapes=[split],
        compiler_params=params,
        name="last_round",
    )(off, on)


def solution(mesh):
    return jax.shard_map(
        per_device,
        mesh=mesh,
        in_specs=(P(None, "row", None, "col"),),
        out_specs=P(None, ("row", "col")),
        check_vma=False,
    )
```

```python
import functools

import jax
import jax.numpy as jnp
from jax import lax
from jax.experimental import pallas as pl
from jax.experimental.pallas import tpu as pltpu
from jax.sharding import PartitionSpec as P

LOGB = 7
OUTER = 4
INNER = 8
LANES = 128
SPAN = 512
DEPTH = 2048
PARTS = 4

damping_ratio = 0.01
spare_bytes = 2048


def partner_columns(value, stride):
    order = value.shape[-1]
    if 2 * stride == order:
        return pltpu.roll(value, stride, 1)
    column = lax.broadcasted_iota(jnp.int32, value.shape, 1)
    is_tail = jnp.bitwise_and(column, stride) != 0
    return jnp.where(is_tail, pltpu.roll(value, stride, 1), pltpu.roll(value, order - stride, 1))


def partner_rows(value, stride):
    order = value.shape[0]
    if stride >= 8:
        pieces = [value[start : start + stride] for start in range(0, order, stride)]
        return jnp.concatenate([pieces[place ^ 1] for place in range(len(pieces))], axis=0)
    row = lax.broadcasted_iota(jnp.int32, value.shape, 0)
    is_tail = jnp.bitwise_and(row, stride) != 0
    return jnp.where(is_tail, pltpu.roll(value, stride, 0), pltpu.roll(value, order - stride, 0))


def turn_of(own, other, cross):
    gap = own - other
    total = own + other
    base = gap * gap + damping_ratio * total * total
    tangent = jnp.where(base > 0.0, 2.0 * cross * gap / jnp.where(base > 0.0, base, 1.0), 0.0)
    inverse = lax.rsqrt(1.0 + tangent * tangent)
    square = 0.5 + 0.5 * inverse
    root = lax.rsqrt(square)
    return square * root, 0.5 * tangent * inverse * root


def inner_solve(*grams):
    shape = grams[0].shape
    row = lax.broadcasted_iota(jnp.int32, shape, 0)
    column = lax.broadcasted_iota(jnp.int32, shape, 1)
    identity = row == column
    state = [(gram, jnp.where(identity, 1.0, 0.0).astype(jnp.float32)) for gram in grams]
    for step in range(INNER):
        stride = 2 ** ((LOGB - 1 - step) % LOGB)
        paired = jnp.bitwise_xor(row, stride) == column
        after = []
        for gram, turned in state:
            on_diagonal = jnp.where(identity, gram, 0.0)
            on_pair = jnp.where(paired, gram, 0.0)
            own_row = jnp.sum(on_diagonal, axis=0, keepdims=True)
            cross_row = jnp.sum(on_pair, axis=0, keepdims=True)
            own_col = jnp.sum(on_diagonal, axis=1, keepdims=True)
            cross_col = jnp.sum(on_pair, axis=1, keepdims=True)
            cos_row, sin_row = turn_of(own_row, partner_columns(own_row, stride), cross_row)
            cos_col, sin_col = turn_of(own_col, partner_rows(own_col, stride), cross_col)
            if step + 1 < INNER:
                gram = gram * cos_row + partner_columns(gram, stride) * sin_row
                gram = gram * cos_col + partner_rows(gram, stride) * sin_col
            after.append((gram, turned * cos_col + partner_rows(turned, stride) * sin_col))
        state = after
    return [turned for _, turned in state]


def three_parts(value):
    high = value.astype(jnp.bfloat16)
    rest = value - high.astype(jnp.float32)
    middle = rest.astype(jnp.bfloat16)
    return high, middle, (rest - middle.astype(jnp.float32)).astype(jnp.bfloat16)


def split_store(split_ref, value, start, lane):
    order = split_ref.shape[0] // 3
    rows, lanes = value.shape
    for place, part in enumerate(three_parts(value)):
        split_ref[pl.ds(place * order + start, rows), pl.ds(lane, lanes)] = part


def gram_of(split_ref):
    order = split_ref.shape[0] // 3
    total = split_ref.shape[1]

    def body(place, acc):
        lanes = pl.ds(pl.multiple_of(place * DEPTH, DEPTH), DEPTH)
        return acc + lax.dot_general(
            split_ref[:, lanes],
            split_ref[: 2 * order, lanes],
            (((1,), (1,)), ((), ())),
            preferred_element_type=jnp.float32,
        )

    acc = lax.fori_loop(0, total // DEPTH, body, jnp.zeros((3 * order, 2 * order), jnp.float32))
    outer = acc[2 * order :, :order]
    inner = acc[:order, order:] + acc[order : 2 * order, :order] + acc[order : 2 * order, order:]
    return acc[:order, :order] + (inner + (outer + outer.T))


def product(turned, split_ref, lane):
    order = split_ref.shape[0] // 3
    rows = turned.shape[0]
    parts = three_parts(turned)
    lanes = pl.ds(lane, SPAN)
    weights = jnp.concatenate([jnp.concatenate([part, part], axis=1) for part in parts], axis=0)
    both = lax.dot_general(
        weights,
        split_ref[: 2 * order, lanes],
        (((1,), (0,)), ((), ())),
        preferred_element_type=jnp.float32,
    )
    small = lax.dot_general(
        parts[0],
        split_ref[2 * order :, lanes],
        (((1,), (0,)), ((), ())),
        preferred_element_type=jnp.float32,
    )
    return both[:rows] + (both[rows : 2 * rows] + (both[2 * rows :] + small))


def spans(length, body):
    def step(place, carry):
        body(pl.multiple_of(place * SPAN, SPAN))
        return carry

    lax.fori_loop(0, length // SPAN, step, 0)


def load_rows(split_ref, refs, start):
    done = 0
    for ref in refs:

        def body(lane):
            split_store(
                split_ref, ref[:, pl.ds(lane, SPAN)], start, pl.multiple_of(done + lane, SPAN)
            )

        spans(ref.shape[1], body)
        done += ref.shape[1]


def send_out(turned, split_ref, first_refs, second_refs, swap):
    half = split_ref.shape[0] // 6
    swapped = jnp.concatenate([turned[half:], turned[:half]], axis=0)
    arranged = jnp.where(swap, swapped, turned)
    done = 0
    for first_ref, second_ref in zip(first_refs, second_refs):

        def body(lane):
            lines = product(arranged, split_ref, pl.multiple_of(done + lane, SPAN))
            first_ref[:, pl.ds(lane, SPAN)] = lines[:half]
            second_ref[:, pl.ds(lane, SPAN)] = lines[half:]

        spans(first_ref.shape[1], body)
        done += first_ref.shape[1]


def run_of(column, row, row_count, column_count):
    last = jnp.where(row == row_count - 1, row, row_count - 2 - row)
    odd = jnp.where(column == column_count - 1, last, row_count - 1 - row)
    return jnp.where(jnp.bitwise_and(column, 1) == 0, row, odd)


def hosted_slot():
    column, columns = lax.axis_index("col"), lax.axis_size("col")
    run = run_of(column, lax.axis_index("row"), lax.axis_size("row"), columns)
    return run * columns + column


def slot_count():
    return lax.axis_size("row") * lax.axis_size("col")


def prepare_kernel(in_ref, *out_refs):
    count = len(out_refs)
    rows = in_ref.shape[1] // count
    me = lax.axis_index("row")
    column, columns = lax.axis_index("col"), lax.axis_size("col")
    for offset in range(count):
        tile = run_of(column, jnp.bitwise_xor(me, offset), count, columns)
        out_refs[offset][...] = in_ref[0, pl.ds(tile, rows, stride=count), :].T


def odd_chip(slot):
    return jnp.bitwise_and(slot // 2, 1)


def first_kernel(count, *refs):
    chunk_refs, out_refs, split_ref = refs[:count], refs[count:-1], refs[-1]
    sizes = len(out_refs) // 2
    me = lax.axis_index("row")
    width = chunk_refs[0].shape[1] // PARTS
    for offset in range(count):
        lane = jnp.bitwise_xor(me, offset) * width
        for part in range(PARTS):
            split_store(
                split_ref,
                chunk_refs[offset][:, part * width : (part + 1) * width],
                0,
                pl.multiple_of(lane + part * count * width, width),
            )
    (turned,) = inner_solve(gram_of(split_ref))
    slot = hosted_slot()
    bottom_first = jnp.logical_or(odd_chip(slot) == 1, slot == 0)
    send_out(turned, split_ref, out_refs[:sizes], out_refs[sizes:], bottom_first)


def middle_kernel(*refs):
    off_out, on_out, near_ref, far_ref = refs[-4:]
    sizes = (len(refs) - 4) // 4
    near_in, far_in, first, second = (
        refs[place * sizes : (place + 1) * sizes] for place in range(4)
    )
    slot, slots = hosted_slot(), slot_count()
    half = off_out.shape[0]
    odd = odd_chip(slot)
    at_end = jnp.logical_or(slot == 0, slot == slots - 1).astype(jnp.int32)
    near_own = pl.multiple_of(odd * half, half)
    near_other = pl.multiple_of((1 - odd) * half, half)
    far_own = pl.multiple_of(jnp.bitwise_xor(1 - odd, at_end) * half, half)
    far_other = pl.multiple_of(jnp.bitwise_xor(odd, at_end) * half, half)
    load_rows(near_ref, first, near_own)
    load_rows(near_ref, near_in, near_other)
    load_rows(far_ref, second, far_own)
    load_rows(far_ref, far_in, far_other)
    near, far = inner_solve(gram_of(near_ref), gram_of(far_ref))
    near_half = jnp.where(odd == 0, near[half:], near[:half])
    flipped = jnp.logical_or(slot == 1, slot == slots - 1)
    far_bottom = jnp.logical_xor(odd == 1, flipped)
    far_half = jnp.where(far_bottom, far[half:], far[:half])

    def body(lane):
        near_lines = product(near_half, near_ref, lane)
        far_lines = product(far_half, far_ref, lane)
        split_store(near_ref, near_lines, near_other, lane)
        split_store(near_ref, far_lines, near_own, lane)

    spans(near_ref.shape[1], body)
    (turned,) = inner_solve(gram_of(near_ref))
    swap = jnp.logical_and(jnp.bitwise_and(slot, 1) == 0, slot != 0)
    send_out(turned, near_ref, [off_out], [on_out], swap)


def last_kernel(count, off_in, on_in, out_ref, split_ref):
    half = off_in.shape[0]
    odd = jnp.bitwise_and(lax.axis_index("col"), 1)
    load_rows(split_ref, [off_in], pl.multiple_of(odd * half, half))
    load_rows(split_ref, [on_in], pl.multiple_of((1 - odd) * half, half))
    (turned,) = inner_solve(gram_of(split_ref))
    total = split_ref.shape[1]
    per_part = total // (PARTS * LANES)
    cycles = per_part // count

    def body(lane):
        lines = product(turned, split_ref, lane)
        for piece in range(SPAN // LANES):
            block = lane // LANES + piece
            part, inside = block // per_part, block % per_part
            source, cycle = inside // cycles, inside % cycles
            start = pl.multiple_of(((part * cycles + cycle) * count + source) * LANES, LANES)
            out_ref[pl.ds(start, LANES), :] = lines[:, piece * LANES : (piece + 1) * LANES].T

    spans(total, body)


def in_vmem(count):
    return [pl.BlockSpec(memory_space=pltpu.VMEM)] * count


def host_of(slot, row_count, column_count):
    run, column = divmod(slot, column_count)
    row = run
    if column == column_count - 1:
        row = run if run == row_count - 1 else row_count - 2 - run
    elif column % 2:
        row = row_count - 1 - run
    return row * column_count + column


def swap_pairs(first_row, width, row_count, column_count):
    slots = row_count * column_count
    near_pairs, far_pairs = [], []
    for slot in range(slots):
        if (slot + 1) * width <= first_row:
            continue
        source = host_of(slot, row_count, column_count)
        step = -2 if slot // 2 % 2 else 2
        near_pairs.append((source, host_of(slot + step, row_count, column_count)))
        target = slot - step if 0 <= slot - step < slots else slot ^ 1
        far_pairs.append((source, host_of(target, row_count, column_count)))
    return near_pairs, far_pairs


def per_device(factor_tiles):
    cycles, rows, tiles, width = factor_tiles.shape
    count, columns = lax.axis_size("row"), lax.axis_size("col")
    slots = count * columns
    half = width // 2
    length = cycles * rows * count
    axes = ("row", "col")
    split_bytes, spare = 6 * width * length, spare_bytes * length
    params = pltpu.CompilerParams(vmem_limit_bytes=split_bytes + spare)
    more_params = pltpu.CompilerParams(vmem_limit_bytes=2 * split_bytes + spare)
    whole_half = jax.ShapeDtypeStruct((half, length), jnp.float32)
    split = pltpu.VMEM((3 * width, length), jnp.bfloat16)

    chunks = pl.pallas_call(
        prepare_kernel,
        grid=(cycles,),
        in_specs=[pl.BlockSpec((1, rows * tiles, width), lambda i: (i, 0, 0))],
        out_specs=[pl.BlockSpec((width, rows), lambda i: (0, i))] * tiles,
        out_shape=[jax.ShapeDtypeStruct((width, cycles * rows), jnp.float32)] * tiles,
        compiler_params=params,
        name="prepare",
    )(factor_tiles.reshape(cycles, rows * tiles, width))
    received = [chunks[0]] + [None] * (tiles - 1)
    for offset in range(tiles - 1, 0, -1):
        received[offset] = lax.ppermute(
            chunks[offset], "row", [(source, source ^ offset) for source in range(count)]
        )

    part = length // PARTS
    starts = [0, 2 * part] + [place * part for place in range(3, PARTS)]
    ends = starts[1:] + [length]
    sizes = len(starts)
    halves = [
        jax.ShapeDtypeStruct((half, end - start), jnp.float32) for start, end in zip(starts, ends)
    ]
    moved = pl.pallas_call(
        functools.partial(first_kernel, tiles),
        in_specs=in_vmem(tiles),
        out_specs=in_vmem(2 * sizes),
        out_shape=halves * 2,
        scratch_shapes=[split],
        compiler_params=params,
        name="first_round",
    )(*received)
    near, far = list(moved[:sizes]), list(moved[sizes:])
    for place in reversed(range(sizes)):
        near_pairs, far_pairs = swap_pairs(starts[place], width, count, columns)
        near[place] = lax.ppermute(near[place], axes, near_pairs)
        far[place] = lax.ppermute(far[place], axes, far_pairs)
    off, on = pl.pallas_call(
        middle_kernel,
        in_specs=in_vmem(4 * sizes),
        out_specs=in_vmem(2),
        out_shape=[whole_half] * 2,
        scratch_shapes=[split] * 2,
        compiler_params=more_params,
        name="middle_rounds",
    )(*near, *far, *moved)

    off_pairs, on_pairs = [], []
    for slot in range(slots):
        target = slot + 1 if slot % 2 else slot - 1
        source = host_of(slot, count, columns)
        off_pairs.append((source, target if 0 <= target < slots else slot))
        on_pairs.append((source, slot ^ 1))
    off = lax.ppermute(off, axes, off_pairs)
    on = lax.ppermute(on, axes, on_pairs)
    return pl.pallas_call(
        functools.partial(last_kernel, count),
        in_specs=in_vmem(2),
        out_specs=pl.BlockSpec(memory_space=pltpu.VMEM),
        out_shape=jax.ShapeDtypeStruct((length, width), jnp.float32),
        scratch_shapes=[split],
        compiler_params=params,
        name="last_round",
    )(off, on)


def solution(mesh):
    return jax.shard_map(
        per_device,
        mesh=mesh,
        in_specs=(P(None, "row", None, "col"),),
        out_specs=P(None, ("row", "col")),
        check_vma=False,
    )
```

```python
import functools

import jax
import jax.numpy as jnp
from jax import lax
from jax.experimental import pallas as pl
from jax.experimental.pallas import tpu as pltpu
from jax.sharding import PartitionSpec as P

LOGB = 7
OUTER = 4
INNER = 8
LANES = 128
SPAN = 512
DEPTH = 2048
PARTS = 4

damping_ratio = 0.01
spare_bytes = 2048


def partner_columns(value, stride):
    order = value.shape[-1]
    if 2 * stride == order:
        return pltpu.roll(value, stride, 1)
    column = lax.broadcasted_iota(jnp.int32, value.shape, 1)
    is_tail = jnp.bitwise_and(column, stride) != 0
    return jnp.where(is_tail, pltpu.roll(value, stride, 1), pltpu.roll(value, order - stride, 1))


def partner_rows(value, stride):
    order = value.shape[0]
    if stride >= 8:
        pieces = [value[start : start + stride] for start in range(0, order, stride)]
        return jnp.concatenate([pieces[place ^ 1] for place in range(len(pieces))], axis=0)
    row = lax.broadcasted_iota(jnp.int32, value.shape, 0)
    is_tail = jnp.bitwise_and(row, stride) != 0
    return jnp.where(is_tail, pltpu.roll(value, stride, 0), pltpu.roll(value, order - stride, 0))


def turn_of(own, other, cross):
    gap = own - other
    total = own + other
    base = gap * gap + damping_ratio * total * total
    tangent = jnp.where(base > 0.0, 2.0 * cross * gap / jnp.where(base > 0.0, base, 1.0), 0.0)
    inverse = lax.rsqrt(1.0 + tangent * tangent)
    square = 0.5 + 0.5 * inverse
    root = lax.rsqrt(square)
    return square * root, 0.5 * tangent * inverse * root


def inner_solve(*grams):
    shape = grams[0].shape
    row = lax.broadcasted_iota(jnp.int32, shape, 0)
    column = lax.broadcasted_iota(jnp.int32, shape, 1)
    mixed = jnp.bitwise_xor(row, column)
    state = []
    for gram in grams:
        lines = gram
        for bit in range(LOGB):
            is_set = jnp.bitwise_and(column, 2**bit) != 0
            lines = jnp.where(is_set, partner_rows(lines, 2**bit), lines)
        state.append((lines, lines[:1], jnp.where(row == column, 1.0, 0.0).astype(jnp.float32)))
    for step in range(INNER):
        stride = 2 ** ((LOGB - 1 - step) % LOGB)
        after = []
        for lines, own, turned in state:
            other = partner_columns(own, stride)
            cross = lines[stride : stride + 1]
            cosine, sine = turn_of(own, other, cross)
            turned = turned * cosine + partner_columns(turned, stride) * sine
            own = cosine * (cosine * own + 2.0 * sine * cross) + sine * sine * other
            if step + 1 < INNER:
                across = partner_rows(partner_columns(lines, stride), stride)
                lines = lines * cosine + across * sine
                cos_mixed = jnp.take_along_axis(jnp.broadcast_to(cosine, shape), mixed, axis=1)
                sin_mixed = jnp.take_along_axis(jnp.broadcast_to(sine, shape), mixed, axis=1)
                lines = lines * cos_mixed + partner_rows(lines, stride) * sin_mixed
            after.append((lines, own, turned))
        state = after
    return [turned.T for _, _, turned in state]


def three_parts(value):
    high = value.astype(jnp.bfloat16)
    rest = value - high.astype(jnp.float32)
    middle = rest.astype(jnp.bfloat16)
    return high, middle, (rest - middle.astype(jnp.float32)).astype(jnp.bfloat16)


def split_store(split_ref, value, start, lane):
    order = split_ref.shape[0] // 3
    rows, lanes = value.shape
    for place, part in enumerate(three_parts(value)):
        split_ref[pl.ds(place * order + start, rows), pl.ds(lane, lanes)] = part


def gram_of(split_ref):
    order = split_ref.shape[0] // 3
    total = split_ref.shape[1]

    def body(place, acc):
        lanes = pl.ds(pl.multiple_of(place * DEPTH, DEPTH), DEPTH)
        return acc + lax.dot_general(
            split_ref[:, lanes],
            split_ref[: 2 * order, lanes],
            (((1,), (1,)), ((), ())),
            preferred_element_type=jnp.float32,
        )

    acc = lax.fori_loop(0, total // DEPTH, body, jnp.zeros((3 * order, 2 * order), jnp.float32))
    outer = acc[2 * order :, :order]
    inner = acc[:order, order:] + acc[order : 2 * order, :order] + acc[order : 2 * order, order:]
    return acc[:order, :order] + (inner + (outer + outer.T))


def product(turned, split_ref, lane):
    order = split_ref.shape[0] // 3
    rows = turned.shape[0]
    parts = three_parts(turned)
    lanes = pl.ds(lane, SPAN)
    weights = jnp.concatenate([jnp.concatenate([part, part], axis=1) for part in parts], axis=0)
    both = lax.dot_general(
        weights,
        split_ref[: 2 * order, lanes],
        (((1,), (0,)), ((), ())),
        preferred_element_type=jnp.float32,
    )
    small = lax.dot_general(
        parts[0],
        split_ref[2 * order :, lanes],
        (((1,), (0,)), ((), ())),
        preferred_element_type=jnp.float32,
    )
    return both[:rows] + (both[rows : 2 * rows] + (both[2 * rows :] + small))


def spans(length, body):
    def step(place, carry):
        body(pl.multiple_of(place * SPAN, SPAN))
        return carry

    lax.fori_loop(0, length // SPAN, step, 0)


def load_rows(split_ref, refs, start):
    done = 0
    for ref in refs:

        def body(lane):
            split_store(
                split_ref, ref[:, pl.ds(lane, SPAN)], start, pl.multiple_of(done + lane, SPAN)
            )

        spans(ref.shape[1], body)
        done += ref.shape[1]


def send_out(turned, split_ref, first_refs, second_refs, swap):
    half = split_ref.shape[0] // 6
    swapped = jnp.concatenate([turned[half:], turned[:half]], axis=0)
    arranged = jnp.where(swap, swapped, turned)
    done = 0
    for first_ref, second_ref in zip(first_refs, second_refs):

        def body(lane):
            lines = product(arranged, split_ref, pl.multiple_of(done + lane, SPAN))
            first_ref[:, pl.ds(lane, SPAN)] = lines[:half]
            second_ref[:, pl.ds(lane, SPAN)] = lines[half:]

        spans(first_ref.shape[1], body)
        done += first_ref.shape[1]


def run_of(column, row, row_count, column_count):
    last = jnp.where(row == row_count - 1, row, row_count - 2 - row)
    odd = jnp.where(column == column_count - 1, last, row_count - 1 - row)
    return jnp.where(jnp.bitwise_and(column, 1) == 0, row, odd)


def hosted_slot():
    column, columns = lax.axis_index("col"), lax.axis_size("col")
    run = run_of(column, lax.axis_index("row"), lax.axis_size("row"), columns)
    return run * columns + column


def slot_count():
    return lax.axis_size("row") * lax.axis_size("col")


def prepare_kernel(in_ref, *out_refs):
    count = len(out_refs)
    rows = in_ref.shape[1] // count
    me = lax.axis_index("row")
    column, columns = lax.axis_index("col"), lax.axis_size("col")
    for offset in range(count):
        tile = run_of(column, jnp.bitwise_xor(me, offset), count, columns)
        out_refs[offset][...] = in_ref[0, pl.ds(tile, rows, stride=count), :].T


def odd_chip(slot):
    return jnp.bitwise_and(slot // 2, 1)


def first_kernel(count, *refs):
    chunk_refs, out_refs, split_ref = refs[:count], refs[count:-1], refs[-1]
    sizes = len(out_refs) // 2
    me = lax.axis_index("row")
    width = chunk_refs[0].shape[1] // PARTS
    for offset in range(count):
        lane = jnp.bitwise_xor(me, offset) * width
        for part in range(PARTS):
            split_store(
                split_ref,
                chunk_refs[offset][:, part * width : (part + 1) * width],
                0,
                pl.multiple_of(lane + part * count * width, width),
            )
    (turned,) = inner_solve(gram_of(split_ref))
    slot = hosted_slot()
    bottom_first = jnp.logical_or(odd_chip(slot) == 1, slot == 0)
    send_out(turned, split_ref, out_refs[:sizes], out_refs[sizes:], bottom_first)


def middle_kernel(*refs):
    off_out, on_out, near_ref, far_ref = refs[-4:]
    sizes = (len(refs) - 4) // 4
    near_in, far_in, first, second = (
        refs[place * sizes : (place + 1) * sizes] for place in range(4)
    )
    slot, slots = hosted_slot(), slot_count()
    half = off_out.shape[0]
    odd = odd_chip(slot)
    at_end = jnp.logical_or(slot == 0, slot == slots - 1).astype(jnp.int32)
    near_own = pl.multiple_of(odd * half, half)
    near_other = pl.multiple_of((1 - odd) * half, half)
    far_own = pl.multiple_of(jnp.bitwise_xor(1 - odd, at_end) * half, half)
    far_other = pl.multiple_of(jnp.bitwise_xor(odd, at_end) * half, half)
    load_rows(near_ref, first, near_own)
    load_rows(near_ref, near_in, near_other)
    load_rows(far_ref, second, far_own)
    load_rows(far_ref, far_in, far_other)
    near, far = inner_solve(gram_of(near_ref), gram_of(far_ref))
    near_half = jnp.where(odd == 0, near[half:], near[:half])
    flipped = jnp.logical_or(slot == 1, slot == slots - 1)
    far_bottom = jnp.logical_xor(odd == 1, flipped)
    far_half = jnp.where(far_bottom, far[half:], far[:half])

    def body(lane):
        near_lines = product(near_half, near_ref, lane)
        far_lines = product(far_half, far_ref, lane)
        split_store(near_ref, near_lines, near_other, lane)
        split_store(near_ref, far_lines, near_own, lane)

    spans(near_ref.shape[1], body)
    (turned,) = inner_solve(gram_of(near_ref))
    swap = jnp.logical_and(jnp.bitwise_and(slot, 1) == 0, slot != 0)
    send_out(turned, near_ref, [off_out], [on_out], swap)


def last_kernel(count, off_in, on_in, out_ref, split_ref):
    half = off_in.shape[0]
    odd = jnp.bitwise_and(lax.axis_index("col"), 1)
    load_rows(split_ref, [off_in], pl.multiple_of(odd * half, half))
    load_rows(split_ref, [on_in], pl.multiple_of((1 - odd) * half, half))
    (turned,) = inner_solve(gram_of(split_ref))
    total = split_ref.shape[1]
    per_part = total // (PARTS * LANES)
    cycles = per_part // count

    def body(lane):
        lines = product(turned, split_ref, lane)
        for piece in range(SPAN // LANES):
            block = lane // LANES + piece
            part, inside = block // per_part, block % per_part
            source, cycle = inside // cycles, inside % cycles
            start = pl.multiple_of(((part * cycles + cycle) * count + source) * LANES, LANES)
            out_ref[pl.ds(start, LANES), :] = lines[:, piece * LANES : (piece + 1) * LANES].T

    spans(total, body)


def in_vmem(count):
    return [pl.BlockSpec(memory_space=pltpu.VMEM)] * count


def host_of(slot, row_count, column_count):
    run, column = divmod(slot, column_count)
    row = run
    if column == column_count - 1:
        row = run if run == row_count - 1 else row_count - 2 - run
    elif column % 2:
        row = row_count - 1 - run
    return row * column_count + column


def swap_pairs(first_row, width, row_count, column_count):
    slots = row_count * column_count
    near_pairs, far_pairs = [], []
    for slot in range(slots):
        if (slot + 1) * width <= first_row:
            continue
        source = host_of(slot, row_count, column_count)
        step = -2 if slot // 2 % 2 else 2
        near_pairs.append((source, host_of(slot + step, row_count, column_count)))
        target = slot - step if 0 <= slot - step < slots else slot ^ 1
        far_pairs.append((source, host_of(target, row_count, column_count)))
    return near_pairs, far_pairs


def per_device(factor_tiles):
    cycles, rows, tiles, width = factor_tiles.shape
    count, columns = lax.axis_size("row"), lax.axis_size("col")
    slots = count * columns
    half = width // 2
    length = cycles * rows * count
    axes = ("row", "col")
    split_bytes, spare = 6 * width * length, spare_bytes * length
    params = pltpu.CompilerParams(vmem_limit_bytes=split_bytes + spare)
    more_params = pltpu.CompilerParams(vmem_limit_bytes=2 * split_bytes + spare)
    whole_half = jax.ShapeDtypeStruct((half, length), jnp.float32)
    split = pltpu.VMEM((3 * width, length), jnp.bfloat16)

    chunks = pl.pallas_call(
        prepare_kernel,
        grid=(cycles,),
        in_specs=[pl.BlockSpec((1, rows * tiles, width), lambda i: (i, 0, 0))],
        out_specs=[pl.BlockSpec((width, rows), lambda i: (0, i))] * tiles,
        out_shape=[jax.ShapeDtypeStruct((width, cycles * rows), jnp.float32)] * tiles,
        compiler_params=params,
        name="prepare",
    )(factor_tiles.reshape(cycles, rows * tiles, width))
    received = [chunks[0]] + [None] * (tiles - 1)
    for offset in range(tiles - 1, 0, -1):
        received[offset] = lax.ppermute(
            chunks[offset], "row", [(source, source ^ offset) for source in range(count)]
        )

    part = length // PARTS
    starts = [0, 2 * part] + [place * part for place in range(3, PARTS)]
    ends = starts[1:] + [length]
    sizes = len(starts)
    halves = [
        jax.ShapeDtypeStruct((half, end - start), jnp.float32) for start, end in zip(starts, ends)
    ]
    moved = pl.pallas_call(
        functools.partial(first_kernel, tiles),
        in_specs=in_vmem(tiles),
        out_specs=in_vmem(2 * sizes),
        out_shape=halves * 2,
        scratch_shapes=[split],
        compiler_params=params,
        name="first_round",
    )(*received)
    near, far = list(moved[:sizes]), list(moved[sizes:])
    for place in reversed(range(sizes)):
        near_pairs, far_pairs = swap_pairs(starts[place], width, count, columns)
        near[place] = lax.ppermute(near[place], axes, near_pairs)
        far[place] = lax.ppermute(far[place], axes, far_pairs)
    off, on = pl.pallas_call(
        middle_kernel,
        in_specs=in_vmem(4 * sizes),
        out_specs=in_vmem(2),
        out_shape=[whole_half] * 2,
        scratch_shapes=[split] * 2,
        compiler_params=more_params,
        name="middle_rounds",
    )(*near, *far, *moved)

    off_pairs, on_pairs = [], []
    for slot in range(slots):
        target = slot + 1 if slot % 2 else slot - 1
        source = host_of(slot, count, columns)
        off_pairs.append((source, target if 0 <= target < slots else slot))
        on_pairs.append((source, slot ^ 1))
    off = lax.ppermute(off, axes, off_pairs)
    on = lax.ppermute(on, axes, on_pairs)
    return pl.pallas_call(
        functools.partial(last_kernel, count),
        in_specs=in_vmem(2),
        out_specs=pl.BlockSpec(memory_space=pltpu.VMEM),
        out_shape=jax.ShapeDtypeStruct((length, width), jnp.float32),
        scratch_shapes=[split],
        compiler_params=params,
        name="last_round",
    )(off, on)


def solution(mesh):
    return jax.shard_map(
        per_device,
        mesh=mesh,
        in_specs=(P(None, "row", None, "col"),),
        out_specs=P(None, ("row", "col")),
        check_vma=False,
    )
```

```python
import functools

import jax
import jax.numpy as jnp
from jax import lax
from jax.experimental import pallas as pl
from jax.experimental.pallas import tpu as pltpu
from jax.sharding import PartitionSpec as P

LOGB = 7
OUTER = 4
INNER = 8
LANES = 128
SPAN = 512
DEPTH = 2048
PARTS = 4
PIECES = 2

damping_ratio = 0.01
spare_bytes = 2048


def partner_columns(value, stride):
    order = value.shape[-1]
    if 2 * stride == order:
        return pltpu.roll(value, stride, 1)
    column = lax.broadcasted_iota(jnp.int32, value.shape, 1)
    if value.shape[0] > 1:
        return jnp.take_along_axis(value, jnp.bitwise_xor(column, stride), axis=1)
    is_tail = jnp.bitwise_and(column, stride) != 0
    return jnp.where(is_tail, pltpu.roll(value, stride, 1), pltpu.roll(value, order - stride, 1))


def partner_rows(value, stride):
    order = value.shape[0]
    if stride >= 8:
        pieces = [value[start : start + stride] for start in range(0, order, stride)]
        return jnp.concatenate([pieces[place ^ 1] for place in range(len(pieces))], axis=0)
    row = lax.broadcasted_iota(jnp.int32, value.shape, 0)
    is_tail = jnp.bitwise_and(row, stride) != 0
    return jnp.where(is_tail, pltpu.roll(value, stride, 0), pltpu.roll(value, order - stride, 0))


def turn_of(own, other, cross):
    gap = own - other
    total = own + other
    base = gap * gap + damping_ratio * total * total
    tangent = jnp.where(base > 0.0, 2.0 * cross * gap / jnp.where(base > 0.0, base, 1.0), 0.0)
    inverse = lax.rsqrt(1.0 + tangent * tangent)
    square = 0.5 + 0.5 * inverse
    root = lax.rsqrt(square)
    return square * root, 0.5 * tangent * inverse * root


def inner_solve(*grams):
    shape = grams[0].shape
    row = lax.broadcasted_iota(jnp.int32, shape, 0)
    column = lax.broadcasted_iota(jnp.int32, shape, 1)
    mixed = jnp.bitwise_xor(row, column)
    state = []
    for gram in grams:
        lines = gram
        for bit in range(LOGB):
            is_set = jnp.bitwise_and(column, 2**bit) != 0
            lines = jnp.where(is_set, partner_rows(lines, 2**bit), lines)
        state.append((lines, lines[:1], jnp.where(row == column, 1.0, 0.0).astype(jnp.float32)))
    for step in range(INNER):
        stride = 2 ** ((LOGB - 1 - step) % LOGB)
        after = []
        for lines, own, turned in state:
            other = partner_columns(own, stride)
            cross = lines[stride : stride + 1]
            cosine, sine = turn_of(own, other, cross)
            turned = turned * cosine + partner_columns(turned, stride) * sine
            own = cosine * (cosine * own + 2.0 * sine * cross) + sine * sine * other
            if step + 1 < INNER:
                across = partner_rows(partner_columns(lines, stride), stride)
                lines = lines * cosine + across * sine
                cos_mixed = jnp.take_along_axis(jnp.broadcast_to(cosine, shape), mixed, axis=1)
                sin_mixed = jnp.take_along_axis(jnp.broadcast_to(sine, shape), mixed, axis=1)
                lines = lines * cos_mixed + partner_rows(lines, stride) * sin_mixed
            after.append((lines, own, turned))
        state = after
    return [turned.T for _, _, turned in state]


def three_parts(value):
    high = value.astype(jnp.bfloat16)
    rest = value - high.astype(jnp.float32)
    middle = rest.astype(jnp.bfloat16)
    return high, middle, (rest - middle.astype(jnp.float32)).astype(jnp.bfloat16)


def split_store(split_ref, value, start, lane):
    order = split_ref.shape[0] // 3
    rows, lanes = value.shape
    for place, part in enumerate(three_parts(value)):
        split_ref[pl.ds(place * order + start, rows), pl.ds(lane, lanes)] = part


def gram_of(split_ref):
    order = split_ref.shape[0] // 3
    total = split_ref.shape[1]

    def body(place, acc):
        lanes = pl.ds(pl.multiple_of(place * DEPTH, DEPTH), DEPTH)
        return acc + lax.dot_general(
            split_ref[:, lanes],
            split_ref[: 2 * order, lanes],
            (((1,), (1,)), ((), ())),
            preferred_element_type=jnp.float32,
        )

    acc = lax.fori_loop(0, total // DEPTH, body, jnp.zeros((3 * order, 2 * order), jnp.float32))
    outer = acc[2 * order :, :order]
    inner = acc[:order, order:] + acc[order : 2 * order, :order] + acc[order : 2 * order, order:]
    return acc[:order, :order] + (inner + (outer + outer.T))


def product(turned, split_ref, lane):
    order = split_ref.shape[0] // 3
    rows = turned.shape[0]
    parts = three_parts(turned)
    lanes = pl.ds(lane, SPAN)
    weights = jnp.concatenate([jnp.concatenate([part, part], axis=1) for part in parts], axis=0)
    both = lax.dot_general(
        weights,
        split_ref[: 2 * order, lanes],
        (((1,), (0,)), ((), ())),
        preferred_element_type=jnp.float32,
    )
    small = lax.dot_general(
        parts[0],
        split_ref[2 * order :, lanes],
        (((1,), (0,)), ((), ())),
        preferred_element_type=jnp.float32,
    )
    return both[:rows] + (both[rows : 2 * rows] + (both[2 * rows :] + small))


def spans(length, body):
    def step(place, carry):
        body(pl.multiple_of(place * SPAN, SPAN))
        return carry

    lax.fori_loop(0, length // SPAN, step, 0)


def load_rows(split_ref, refs, start):
    done = 0
    for ref in refs:

        def body(lane):
            split_store(
                split_ref, ref[:, pl.ds(lane, SPAN)], start, pl.multiple_of(done + lane, SPAN)
            )

        spans(ref.shape[1], body)
        done += ref.shape[1]


def send_out(turned, split_ref, first_refs, second_refs, swap):
    half = split_ref.shape[0] // 6
    swapped = jnp.concatenate([turned[half:], turned[:half]], axis=0)
    arranged = jnp.where(swap, swapped, turned)
    done = 0
    for first_ref, second_ref in zip(first_refs, second_refs):

        def body(lane):
            lines = product(arranged, split_ref, pl.multiple_of(done + lane, SPAN))
            first_ref[:, pl.ds(lane, SPAN)] = lines[:half]
            second_ref[:, pl.ds(lane, SPAN)] = lines[half:]

        spans(first_ref.shape[1], body)
        done += first_ref.shape[1]


def run_of(column, row, row_count, column_count):
    last = jnp.where(row == row_count - 1, row, row_count - 2 - row)
    odd = jnp.where(column == column_count - 1, last, row_count - 1 - row)
    return jnp.where(jnp.bitwise_and(column, 1) == 0, row, odd)


def hosted_slot():
    column, columns = lax.axis_index("col"), lax.axis_size("col")
    run = run_of(column, lax.axis_index("row"), lax.axis_size("row"), columns)
    return run * columns + column


def slot_count():
    return lax.axis_size("row") * lax.axis_size("col")


def prepare_kernel(count, in_ref, *refs):
    out_refs, buffer, ready = refs[:-2], refs[-2], refs[-1]
    cycles, rows = in_ref.shape[0], in_ref.shape[1] // count
    copies = [
        pltpu.make_async_copy(in_ref.at[cycle], buffer.at[cycle], ready.at[cycle])
        for cycle in range(cycles)
    ]
    for copy in copies:
        copy.start()
    me = lax.axis_index("row")
    column, columns = lax.axis_index("col"), lax.axis_size("col")
    per_piece = cycles // PIECES
    for cycle, copy in enumerate(copies):
        copy.wait()
        piece, place = divmod(cycle, per_piece)
        for offset in range(count):
            tile = run_of(column, jnp.bitwise_xor(me, offset), count, columns)
            out_refs[offset * PIECES + piece][:, place * rows : (place + 1) * rows] = buffer[
                cycle, pl.ds(tile, rows, stride=count), :
            ].T


def odd_chip(slot):
    return jnp.bitwise_and(slot // 2, 1)


def first_kernel(count, *refs):
    chunk_refs, out_refs, split_ref = refs[: count * PIECES], refs[count * PIECES : -1], refs[-1]
    sizes = len(out_refs) // 2
    me = lax.axis_index("row")
    per_piece = PARTS // PIECES
    width = chunk_refs[0].shape[1] // per_piece
    for offset in range(count):
        lane = jnp.bitwise_xor(me, offset) * width
        for part in range(PARTS):
            piece, place = divmod(part, per_piece)
            split_store(
                split_ref,
                chunk_refs[offset * PIECES + piece][:, place * width : (place + 1) * width],
                0,
                pl.multiple_of(lane + part * count * width, width),
            )
    (turned,) = inner_solve(gram_of(split_ref))
    slot = hosted_slot()
    bottom_first = jnp.logical_or(odd_chip(slot) == 1, slot == 0)
    send_out(turned, split_ref, out_refs[:sizes], out_refs[sizes:], bottom_first)


def middle_kernel(*refs):
    off_out, on_out, near_ref, far_ref = refs[-4:]
    sizes = (len(refs) - 4) // 4
    near_in, far_in, first, second = (
        refs[place * sizes : (place + 1) * sizes] for place in range(4)
    )
    slot, slots = hosted_slot(), slot_count()
    half = off_out.shape[0]
    odd = odd_chip(slot)
    at_end = jnp.logical_or(slot == 0, slot == slots - 1).astype(jnp.int32)
    near_own = pl.multiple_of(odd * half, half)
    near_other = pl.multiple_of((1 - odd) * half, half)
    far_own = pl.multiple_of(jnp.bitwise_xor(1 - odd, at_end) * half, half)
    far_other = pl.multiple_of(jnp.bitwise_xor(odd, at_end) * half, half)
    load_rows(near_ref, first, near_own)
    load_rows(near_ref, near_in, near_other)
    load_rows(far_ref, second, far_own)
    load_rows(far_ref, far_in, far_other)
    near, far = inner_solve(gram_of(near_ref), gram_of(far_ref))
    near_half = jnp.where(odd == 0, near[half:], near[:half])
    flipped = jnp.logical_or(slot == 1, slot == slots - 1)
    far_bottom = jnp.logical_xor(odd == 1, flipped)
    far_half = jnp.where(far_bottom, far[half:], far[:half])

    def body(lane):
        near_lines = product(near_half, near_ref, lane)
        far_lines = product(far_half, far_ref, lane)
        split_store(near_ref, near_lines, near_other, lane)
        split_store(near_ref, far_lines, near_own, lane)

    spans(near_ref.shape[1], body)
    (turned,) = inner_solve(gram_of(near_ref))
    swap = jnp.logical_and(jnp.bitwise_and(slot, 1) == 0, slot != 0)
    send_out(turned, near_ref, [off_out], [on_out], swap)


def last_kernel(count, off_in, on_in, out_ref, split_ref, buffer, done):
    half = off_in.shape[0]
    odd = jnp.bitwise_and(lax.axis_index("col"), 1)
    load_rows(split_ref, [off_in], pl.multiple_of(odd * half, half))
    load_rows(split_ref, [on_in], pl.multiple_of((1 - odd) * half, half))
    (turned,) = inner_solve(gram_of(split_ref))
    total = split_ref.shape[1]
    per_part = total // (PARTS * LANES)
    cycles = per_part // count

    def rows_of(block):
        part, inside = block // per_part, block % per_part
        source, cycle = inside // cycles, inside % cycles
        place = (part * cycles + cycle) * count + source
        return pl.ds(pl.multiple_of(place * LANES, LANES), LANES)

    def copy_of(block):
        rows = rows_of(block)
        return pltpu.make_async_copy(buffer.at[rows], out_ref.at[rows], done.at[block])

    def body(lane):
        lines = product(turned, split_ref, lane)
        for piece in range(SPAN // LANES):
            block = lane // LANES + piece
            buffer[rows_of(block), :] = lines[:, piece * LANES : (piece + 1) * LANES].T
            copy_of(block).start()

    spans(total, body)

    def finish(block, carry):
        copy_of(block).wait()
        return carry

    lax.fori_loop(0, total // LANES, finish, 0)


def in_vmem(count):
    return [pl.BlockSpec(memory_space=pltpu.VMEM)] * count


def host_of(slot, row_count, column_count):
    run, column = divmod(slot, column_count)
    row = run
    if column == column_count - 1:
        row = run if run == row_count - 1 else row_count - 2 - run
    elif column % 2:
        row = row_count - 1 - run
    return row * column_count + column


def peer_pairs(offset, first_row, width, row_count, column_count):
    pairs = []
    for row in range(row_count):
        for column in range(column_count):
            peer = (row ^ offset) * column_count + column
            slot = host_of(peer, row_count, column_count)
            if (slot + 1) * width > first_row:
                pairs.append((row * column_count + column, peer))
    return pairs


def swap_pairs(first_row, width, row_count, column_count):
    slots = row_count * column_count
    near_pairs, far_pairs = [], []
    for slot in range(slots):
        if (slot + 1) * width <= first_row:
            continue
        source = host_of(slot, row_count, column_count)
        step = -2 if slot // 2 % 2 else 2
        near_pairs.append((source, host_of(slot + step, row_count, column_count)))
        target = slot - step if 0 <= slot - step < slots else slot ^ 1
        far_pairs.append((source, host_of(target, row_count, column_count)))
    return near_pairs, far_pairs


def per_device(factor_tiles):
    cycles, rows, tiles, width = factor_tiles.shape
    count, columns = lax.axis_size("row"), lax.axis_size("col")
    slots = count * columns
    half = width // 2
    length = cycles * rows * count
    axes = ("row", "col")
    split_bytes, spare = 6 * width * length, spare_bytes * length
    params = pltpu.CompilerParams(vmem_limit_bytes=split_bytes + spare)
    more_params = pltpu.CompilerParams(vmem_limit_bytes=2 * split_bytes + spare)
    whole_half = jax.ShapeDtypeStruct((half, length), jnp.float32)
    split = pltpu.VMEM((3 * width, length), jnp.bfloat16)

    pieces = tiles * PIECES
    chunks = pl.pallas_call(
        functools.partial(prepare_kernel, tiles),
        in_specs=[pl.BlockSpec(memory_space=pltpu.HBM)],
        out_specs=in_vmem(pieces),
        out_shape=[jax.ShapeDtypeStruct((width, cycles * rows // PIECES), jnp.float32)] * pieces,
        scratch_shapes=[
            pltpu.VMEM((cycles, rows * tiles, width), jnp.float32),
            pltpu.SemaphoreType.DMA((cycles,)),
        ],
        compiler_params=params,
        name="prepare",
    )(factor_tiles.reshape(cycles, rows * tiles, width))
    received = list(chunks)
    for offset in range(tiles - 1, 0, -1):
        for piece in reversed(range(PIECES)):
            place = offset * PIECES + piece
            first_row = piece * (length // PIECES)
            pairs = peer_pairs(offset, first_row, width, count, columns)
            received[place] = lax.ppermute(chunks[place], axes, pairs)

    part = length // PARTS
    starts = [0, 2 * part] + [place * part for place in range(3, PARTS)]
    ends = starts[1:] + [length]
    sizes = len(starts)
    halves = [
        jax.ShapeDtypeStruct((half, end - start), jnp.float32) for start, end in zip(starts, ends)
    ]
    moved = pl.pallas_call(
        functools.partial(first_kernel, tiles),
        in_specs=in_vmem(pieces),
        out_specs=in_vmem(2 * sizes),
        out_shape=halves * 2,
        scratch_shapes=[split],
        compiler_params=params,
        name="first_round",
    )(*received)
    near, far = list(moved[:sizes]), list(moved[sizes:])
    for place in range(sizes):
        near_pairs, far_pairs = swap_pairs(starts[place], width, count, columns)
        if place == sizes - 1:
            near[place], near[place - 1] = lax.optimization_barrier((near[place], near[place - 1]))
        far[place] = lax.ppermute(far[place], axes, far_pairs)
        near[place] = lax.ppermute(near[place], axes, near_pairs)
    off, on = pl.pallas_call(
        middle_kernel,
        in_specs=in_vmem(4 * sizes),
        out_specs=in_vmem(2),
        out_shape=[whole_half] * 2,
        scratch_shapes=[split] * 2,
        compiler_params=more_params,
        name="middle_rounds",
    )(*near, *far, *moved)

    off_pairs, on_pairs = [], []
    for slot in range(slots):
        target = slot + 1 if slot % 2 else slot - 1
        source = host_of(slot, count, columns)
        off_pairs.append((source, target if 0 <= target < slots else slot))
        on_pairs.append((source, slot ^ 1))
    off = lax.ppermute(off, axes, off_pairs)
    on = lax.ppermute(on, axes, on_pairs)
    return pl.pallas_call(
        functools.partial(last_kernel, count),
        in_specs=in_vmem(2),
        out_specs=pl.BlockSpec(memory_space=pltpu.HBM),
        out_shape=jax.ShapeDtypeStruct((length, width), jnp.float32),
        scratch_shapes=[
            split,
            pltpu.VMEM((length, width), jnp.float32),
            pltpu.SemaphoreType.DMA((length // LANES,)),
        ],
        compiler_params=params,
        name="last_round",
    )(off, on)


def solution(mesh):
    return jax.shard_map(
        per_device,
        mesh=mesh,
        in_specs=(P(None, "row", None, "col"),),
        out_specs=P(None, ("row", "col")),
        check_vma=False,
    )
```

```python
import functools

import jax
import jax.numpy as jnp
from jax import lax
from jax.experimental import pallas as pl
from jax.experimental.pallas import tpu as pltpu
from jax.sharding import PartitionSpec as P

LOGB = 7
OUTER = 4
INNER = 8
LANES = 128
SPAN = 512
DEPTH = 2048
UNROLLED = 4096
UNITS = 32
NEAR_CUTS = (16,)
FAR_CUTS = (10, 16, 24)
PIECES = 2

damping_ratio = 0.01
spare_bytes = 2048


def partner_columns(value, stride):
    order = value.shape[-1]
    if 2 * stride == order:
        return pltpu.roll(value, stride, 1)
    column = lax.broadcasted_iota(jnp.int32, value.shape, 1)
    if value.shape[0] > 1:
        return jnp.take_along_axis(value, jnp.bitwise_xor(column, stride), axis=1)
    is_tail = jnp.bitwise_and(column, stride) != 0
    return jnp.where(is_tail, pltpu.roll(value, stride, 1), pltpu.roll(value, order - stride, 1))


def partner_rows(value, stride):
    order = value.shape[0]
    if stride >= 8:
        pieces = [value[start : start + stride] for start in range(0, order, stride)]
        return jnp.concatenate([pieces[place ^ 1] for place in range(len(pieces))], axis=0)
    row = lax.broadcasted_iota(jnp.int32, value.shape, 0)
    is_tail = jnp.bitwise_and(row, stride) != 0
    return jnp.where(is_tail, pltpu.roll(value, stride, 0), pltpu.roll(value, order - stride, 0))


def turn_of(own, other, cross):
    gap = own - other
    total = own + other
    base = gap * gap + damping_ratio * total * total
    tangent = jnp.where(base > 0.0, 2.0 * cross * gap / jnp.where(base > 0.0, base, 1.0), 0.0)
    inverse = lax.rsqrt(1.0 + tangent * tangent)
    square = 0.5 + 0.5 * inverse
    root = lax.rsqrt(square)
    return square * root, 0.5 * tangent * inverse * root


def inner_solve(*grams):
    shape = grams[0].shape
    row = lax.broadcasted_iota(jnp.int32, shape, 0)
    column = lax.broadcasted_iota(jnp.int32, shape, 1)
    mixed = jnp.bitwise_xor(row, column)
    state = []
    for gram in grams:
        lines = gram
        for bit in range(LOGB):
            is_set = jnp.bitwise_and(column, 2**bit) != 0
            lines = jnp.where(is_set, partner_rows(lines, 2**bit), lines)
        state.append((lines, lines[:1], jnp.where(row == column, 1.0, 0.0).astype(jnp.float32)))
    for step in range(INNER):
        stride = 2 ** ((LOGB - 1 - step) % LOGB)
        after = []
        for lines, own, turned in state:
            other = partner_columns(own, stride)
            cross = lines[stride : stride + 1]
            cosine, sine = turn_of(own, other, cross)
            turned = turned * cosine + partner_columns(turned, stride) * sine
            own = cosine * (cosine * own + 2.0 * sine * cross) + sine * sine * other
            if step + 1 < INNER:
                across = partner_rows(partner_columns(lines, stride), stride)
                lines = lines * cosine + across * sine
                cos_mixed = jnp.take_along_axis(jnp.broadcast_to(cosine, shape), mixed, axis=1)
                sin_mixed = jnp.take_along_axis(jnp.broadcast_to(sine, shape), mixed, axis=1)
                lines = lines * cos_mixed + partner_rows(lines, stride) * sin_mixed
            after.append((lines, own, turned))
        state = after
    return [turned.T for _, _, turned in state]


def three_parts(value):
    high = value.astype(jnp.bfloat16)
    rest = value - high.astype(jnp.float32)
    middle = rest.astype(jnp.bfloat16)
    return high, middle, (rest - middle.astype(jnp.float32)).astype(jnp.bfloat16)


def split_store(split_ref, value, start, lane):
    order = split_ref.shape[0] // 3
    rows, lanes = value.shape
    for place, part in enumerate(three_parts(value)):
        split_ref[pl.ds(place * order + start, rows), pl.ds(lane, lanes)] = part


def gram_of(split_ref):
    order = split_ref.shape[0] // 3
    total = split_ref.shape[1]

    def body(place, acc):
        lanes = pl.ds(pl.multiple_of(place * DEPTH, DEPTH), DEPTH)
        return acc + lax.dot_general(
            split_ref[:, lanes],
            split_ref[: 2 * order, lanes],
            (((1,), (1,)), ((), ())),
            preferred_element_type=jnp.float32,
        )

    acc = lax.fori_loop(0, total // DEPTH, body, jnp.zeros((3 * order, 2 * order), jnp.float32))
    outer = acc[2 * order :, :order]
    inner = acc[:order, order:] + acc[order : 2 * order, :order] + acc[order : 2 * order, order:]
    return acc[:order, :order] + (inner + (outer + outer.T))


def product(turned, split_ref, lanes, terms=3):
    order = split_ref.shape[0] // 3
    rows = turned.shape[0]
    parts = three_parts(turned)[:terms]
    weights = jnp.concatenate([jnp.concatenate([part, part], axis=1) for part in parts], axis=0)
    both = lax.dot_general(
        weights,
        split_ref[: 2 * order, lanes],
        (((1,), (0,)), ((), ())),
        preferred_element_type=jnp.float32,
    )
    if terms == 2:
        return both[:rows] + both[rows:]
    small = lax.dot_general(
        parts[0],
        split_ref[2 * order :, lanes],
        (((1,), (0,)), ((), ())),
        preferred_element_type=jnp.float32,
    )
    return both[:rows] + (both[rows : 2 * rows] + (both[2 * rows :] + small))


def spans(length, body):
    whole = length // SPAN * SPAN
    if length <= UNROLLED:
        for lane in range(0, whole, SPAN):
            body(lane, SPAN)
    else:

        def step(place, carry):
            body(pl.multiple_of(place * SPAN, SPAN), SPAN)
            return carry

        lax.fori_loop(0, length // SPAN, step, 0)
    if whole < length:
        body(whole, length - whole)


def load_rows(split_ref, refs, start):
    done = 0
    for ref in refs:

        def body(lane, size):
            split_store(split_ref, ref[:, pl.ds(lane, size)], start, done + lane)

        spans(ref.shape[1], body)
        done += ref.shape[1]


def cuts_of(refs):
    cuts = [0]
    for ref in refs:
        cuts.append(cuts[-1] + ref.shape[1])
    return cuts


def send_out(turned, split_ref, first_refs, second_refs, swap):
    half = split_ref.shape[0] // 6
    swapped = jnp.concatenate([turned[half:], turned[:half]], axis=0)
    arranged = jnp.where(swap, swapped, turned)
    first_cuts, second_cuts = cuts_of(first_refs), cuts_of(second_refs)
    cuts = sorted(set(first_cuts + second_cuts))
    for begin, end in zip(cuts[:-1], cuts[1:]):
        first = max(place for place, cut in enumerate(first_cuts) if cut <= begin)
        second = max(place for place, cut in enumerate(second_cuts) if cut <= begin)
        first_lane, second_lane = begin - first_cuts[first], begin - second_cuts[second]

        def body(lane, size):
            lines = product(arranged, split_ref, pl.ds(begin + lane, size))
            first_refs[first][:, pl.ds(first_lane + lane, size)] = lines[:half]
            second_refs[second][:, pl.ds(second_lane + lane, size)] = lines[half:]

        spans(end - begin, body)


def run_of(column, row, row_count, column_count):
    last = jnp.where(row == row_count - 1, row, row_count - 2 - row)
    odd = jnp.where(column == column_count - 1, last, row_count - 1 - row)
    return jnp.where(jnp.bitwise_and(column, 1) == 0, row, odd)


def hosted_slot():
    column, columns = lax.axis_index("col"), lax.axis_size("col")
    run = run_of(column, lax.axis_index("row"), lax.axis_size("row"), columns)
    return run * columns + column


def slot_count():
    return lax.axis_size("row") * lax.axis_size("col")


def prepare_kernel(count, in_ref, *refs):
    out_refs, buffer, ready = refs[:-2], refs[-2], refs[-1]
    cycles, rows = in_ref.shape[0], in_ref.shape[1] // count
    copies = [
        pltpu.make_async_copy(in_ref.at[cycle], buffer.at[cycle], ready.at[cycle])
        for cycle in range(cycles)
    ]
    for copy in copies:
        copy.start()
    me = lax.axis_index("row")
    column, columns = lax.axis_index("col"), lax.axis_size("col")
    per_piece = cycles // PIECES
    for cycle, copy in enumerate(copies):
        copy.wait()
        piece, place = divmod(cycle, per_piece)
        for offset in range(count):
            tile = run_of(column, jnp.bitwise_xor(me, offset), count, columns)
            out_refs[offset * PIECES + piece][:, place * rows : (place + 1) * rows] = buffer[
                cycle, pl.ds(tile, rows, stride=count), :
            ].T


def odd_chip(slot):
    return jnp.bitwise_and(slot // 2, 1)


def first_kernel(count, near_count, *refs):
    chunk_refs, out_refs, split_ref = refs[: count * PIECES], refs[count * PIECES : -1], refs[-1]
    me = lax.axis_index("row")
    total = split_ref.shape[1]
    rows = split_ref.shape[0] // 3
    per_piece = total // (PIECES * count * rows)
    for offset in range(count):
        peer = jnp.bitwise_xor(me, offset)
        for piece in range(PIECES):
            for place in range(per_piece):
                lane = ((piece * per_piece + place) * count + peer) * rows
                split_store(
                    split_ref,
                    chunk_refs[offset * PIECES + piece][:, place * rows : (place + 1) * rows],
                    0,
                    pl.multiple_of(lane, rows),
                )
    (turned,) = inner_solve(gram_of(split_ref))
    slot = hosted_slot()
    bottom_first = jnp.logical_or(odd_chip(slot) == 1, slot == 0)
    send_out(turned, split_ref, out_refs[:near_count], out_refs[near_count:], bottom_first)


def middle_kernel(near_count, *refs):
    off_out, on_out, near_ref, far_ref = refs[-4:]
    in_refs, own_refs = refs[: (len(refs) - 4) // 2], refs[(len(refs) - 4) // 2 : -4]
    near_in, far_in = in_refs[:near_count], in_refs[near_count:]
    first, second = own_refs[:near_count], own_refs[near_count:]
    slot, slots = hosted_slot(), slot_count()
    half = off_out.shape[0]
    odd = odd_chip(slot)
    at_end = jnp.logical_or(slot == 0, slot == slots - 1).astype(jnp.int32)
    near_own = pl.multiple_of(odd * half, half)
    near_other = pl.multiple_of((1 - odd) * half, half)
    far_own = pl.multiple_of(jnp.bitwise_xor(1 - odd, at_end) * half, half)
    far_other = pl.multiple_of(jnp.bitwise_xor(odd, at_end) * half, half)
    load_rows(near_ref, first, near_own)
    load_rows(near_ref, near_in, near_other)
    load_rows(far_ref, second, far_own)
    load_rows(far_ref, far_in, far_other)
    near, far = inner_solve(gram_of(near_ref), gram_of(far_ref))
    near_half = jnp.where(odd == 0, near[half:], near[:half])
    flipped = jnp.logical_or(slot == 1, slot == slots - 1)
    far_bottom = jnp.logical_xor(odd == 1, flipped)
    far_half = jnp.where(far_bottom, far[half:], far[:half])

    def body(lane, size):
        near_lines = product(near_half, near_ref, pl.ds(lane, size))
        far_lines = product(far_half, far_ref, pl.ds(lane, size))
        split_store(near_ref, near_lines, near_other, lane)
        split_store(near_ref, far_lines, near_own, lane)

    spans(near_ref.shape[1], body)
    (turned,) = inner_solve(gram_of(near_ref))
    swap = jnp.logical_and(jnp.bitwise_and(slot, 1) == 0, slot != 0)
    send_out(turned, near_ref, [off_out], [on_out], swap)


def last_kernel(off_in, on_in, out_ref, split_ref, buffer, done):
    half = off_in.shape[0]
    odd = jnp.bitwise_and(lax.axis_index("col"), 1)
    load_rows(split_ref, [off_in], pl.multiple_of(odd * half, half))
    load_rows(split_ref, [on_in], pl.multiple_of((1 - odd) * half, half))
    (turned,) = inner_solve(gram_of(split_ref))
    total = split_ref.shape[1]

    def copy_of(lane):
        rows = pl.ds(lane, SPAN)
        return pltpu.make_async_copy(buffer.at[rows], out_ref.at[rows], done.at[lane // SPAN])

    def body(lane, size):
        lines = product(turned, split_ref, pl.ds(lane, size), terms=2)
        for place in range(0, size, LANES):
            buffer[pl.ds(lane + place, LANES), :] = lines[:, place : place + LANES].T
        copy_of(lane).start()

    spans(total, body)
    spans(total, lambda lane, size: copy_of(lane).wait())


def in_vmem(count):
    return [pl.BlockSpec(memory_space=pltpu.VMEM)] * count


def host_of(slot, row_count, column_count):
    run, column = divmod(slot, column_count)
    row = run
    if column == column_count - 1:
        row = run if run == row_count - 1 else row_count - 2 - run
    elif column % 2:
        row = row_count - 1 - run
    return row * column_count + column


def peer_pairs(offset, first_row, width, row_count, column_count):
    pairs = []
    for row in range(row_count):
        for column in range(column_count):
            peer = (row ^ offset) * column_count + column
            slot = host_of(peer, row_count, column_count)
            if (slot + 1) * width > first_row:
                pairs.append((row * column_count + column, peer))
    return pairs


def swap_pairs(first_row, width, row_count, column_count):
    slots = row_count * column_count
    near_pairs, far_pairs = [], []
    for slot in range(slots):
        if (slot + 1) * width <= first_row:
            continue
        source = host_of(slot, row_count, column_count)
        step = -2 if slot // 2 % 2 else 2
        near_pairs.append((source, host_of(slot + step, row_count, column_count)))
        target = slot - step if 0 <= slot - step < slots else slot ^ 1
        far_pairs.append((source, host_of(target, row_count, column_count)))
    return near_pairs, far_pairs


def per_device(factor_tiles):
    cycles, rows, tiles, width = factor_tiles.shape
    count, columns = lax.axis_size("row"), lax.axis_size("col")
    slots = count * columns
    half = width // 2
    length = cycles * rows * count
    axes = ("row", "col")
    split_bytes, spare = 6 * width * length, spare_bytes * length
    params = pltpu.CompilerParams(vmem_limit_bytes=split_bytes + spare)
    more_params = pltpu.CompilerParams(vmem_limit_bytes=2 * split_bytes + spare)
    whole_half = jax.ShapeDtypeStruct((half, length), jnp.float32)
    split = pltpu.VMEM((3 * width, length), jnp.bfloat16)

    pieces = tiles * PIECES
    chunks = pl.pallas_call(
        functools.partial(prepare_kernel, tiles),
        in_specs=[pl.BlockSpec(memory_space=pltpu.HBM)],
        out_specs=in_vmem(pieces),
        out_shape=[jax.ShapeDtypeStruct((width, cycles * rows // PIECES), jnp.float32)] * pieces,
        scratch_shapes=[
            pltpu.VMEM((cycles, rows * tiles, width), jnp.float32),
            pltpu.SemaphoreType.DMA((cycles,)),
        ],
        compiler_params=params,
        name="prepare",
    )(factor_tiles.reshape(cycles, rows * tiles, width))
    received = list(chunks)
    for offset in range(tiles - 1, 0, -1):
        for piece in reversed(range(PIECES)):
            place = offset * PIECES + piece
            first_row = piece * (length // PIECES)
            pairs = peer_pairs(offset, first_row, width, count, columns)
            received[place] = lax.ppermute(chunks[place], axes, pairs)

    unit = length // UNITS
    near_starts = [0] + [cut * unit for cut in NEAR_CUTS]
    far_starts = [0] + [cut * unit for cut in FAR_CUTS]
    near_count = len(near_starts)
    halves = [
        jax.ShapeDtypeStruct((half, end - start), jnp.float32)
        for starts in (near_starts, far_starts)
        for start, end in zip(starts, starts[1:] + [length])
    ]
    moved = pl.pallas_call(
        functools.partial(first_kernel, tiles, near_count),
        in_specs=in_vmem(pieces),
        out_specs=in_vmem(len(halves)),
        out_shape=halves,
        scratch_shapes=[split],
        compiler_params=params,
        name="first_round",
    )(*received)
    near, far = list(moved[:near_count]), list(moved[near_count:])

    def swapped(value, first_row, side):
        return lax.ppermute(value, axes, swap_pairs(first_row, width, count, columns)[side])

    for place, start in enumerate(far_starts):
        far[place] = swapped(far[place], start, 1)
        if place < near_count:
            near[place] = swapped(near[place], near_starts[place], 0)
    off, on = pl.pallas_call(
        functools.partial(middle_kernel, near_count),
        in_specs=in_vmem(2 * len(halves)),
        out_specs=in_vmem(2),
        out_shape=[whole_half] * 2,
        scratch_shapes=[split] * 2,
        compiler_params=more_params,
        name="middle_rounds",
    )(*near, *far, *moved)

    off_pairs, on_pairs = [], []
    for slot in range(slots):
        target = slot + 1 if slot % 2 else slot - 1
        source = host_of(slot, count, columns)
        off_pairs.append((source, target if 0 <= target < slots else slot))
        on_pairs.append((source, slot ^ 1))
    off = lax.ppermute(off, axes, off_pairs)
    on = lax.ppermute(on, axes, on_pairs)
    return pl.pallas_call(
        last_kernel,
        in_specs=in_vmem(2),
        out_specs=pl.BlockSpec(memory_space=pltpu.HBM),
        out_shape=jax.ShapeDtypeStruct((length, width), jnp.float32),
        scratch_shapes=[
            split,
            pltpu.VMEM((length, width), jnp.float32),
            pltpu.SemaphoreType.DMA((length // SPAN,)),
        ],
        compiler_params=params,
        name="last_round",
    )(off, on)


def solution(mesh):
    return jax.shard_map(
        per_device,
        mesh=mesh,
        in_specs=(P(None, "row", None, "col"),),
        out_specs=P(None, ("row", "col")),
        check_vma=False,
    )
```

```python
import functools

import jax
import jax.numpy as jnp
from jax import lax
from jax.experimental import pallas as pl
from jax.experimental.pallas import tpu as pltpu
from jax.sharding import PartitionSpec as P

LOGB = 7
OUTER = 4
INNER = 8
LANES = 128
SPAN = 512
DEPTH = 2048
UNROLLED = 4096
UNITS = 32
NEAR_CUTS = (10, 22)
FAR_CUTS = (16, 24)
PIECES = 2

damping_ratio = 0.01
spare_bytes = 2048


def partner_columns(value, stride):
    order = value.shape[-1]
    if 2 * stride == order:
        return pltpu.roll(value, stride, 1)
    column = lax.broadcasted_iota(jnp.int32, value.shape, 1)
    if value.shape[0] > 1:
        return jnp.take_along_axis(value, jnp.bitwise_xor(column, stride), axis=1)
    is_tail = jnp.bitwise_and(column, stride) != 0
    return jnp.where(is_tail, pltpu.roll(value, stride, 1), pltpu.roll(value, order - stride, 1))


def partner_rows(value, stride):
    order = value.shape[0]
    if stride >= 8:
        pieces = [value[start : start + stride] for start in range(0, order, stride)]
        return jnp.concatenate([pieces[place ^ 1] for place in range(len(pieces))], axis=0)
    row = lax.broadcasted_iota(jnp.int32, value.shape, 0)
    is_tail = jnp.bitwise_and(row, stride) != 0
    return jnp.where(is_tail, pltpu.roll(value, stride, 0), pltpu.roll(value, order - stride, 0))


def turn_of(own, other, cross):
    gap = own - other
    total = own + other
    base = gap * gap + damping_ratio * total * total
    tangent = jnp.where(base > 0.0, 2.0 * cross * gap / jnp.where(base > 0.0, base, 1.0), 0.0)
    inverse = lax.rsqrt(1.0 + tangent * tangent)
    square = 0.5 + 0.5 * inverse
    root = lax.rsqrt(square)
    return square * root, 0.5 * tangent * inverse * root


def inner_solve(*grams):
    shape = grams[0].shape
    row = lax.broadcasted_iota(jnp.int32, shape, 0)
    column = lax.broadcasted_iota(jnp.int32, shape, 1)
    mixed = jnp.bitwise_xor(row, column)
    state = []
    for gram in grams:
        lines = gram
        for bit in range(LOGB):
            is_set = jnp.bitwise_and(column, 2**bit) != 0
            lines = jnp.where(is_set, partner_rows(lines, 2**bit), lines)
        state.append((lines, lines[:1], jnp.where(row == column, 1.0, 0.0).astype(jnp.float32)))
    for step in range(INNER):
        stride = 2 ** ((LOGB - 1 - step) % LOGB)
        after = []
        for lines, own, turned in state:
            other = partner_columns(own, stride)
            cross = lines[stride : stride + 1]
            cosine, sine = turn_of(own, other, cross)
            turned = turned * cosine + partner_columns(turned, stride) * sine
            own = cosine * (cosine * own + 2.0 * sine * cross) + sine * sine * other
            if step + 1 < INNER:
                across = partner_rows(partner_columns(lines, stride), stride)
                lines = lines * cosine + across * sine
                cos_mixed = jnp.take_along_axis(jnp.broadcast_to(cosine, shape), mixed, axis=1)
                sin_mixed = jnp.take_along_axis(jnp.broadcast_to(sine, shape), mixed, axis=1)
                lines = lines * cos_mixed + partner_rows(lines, stride) * sin_mixed
            after.append((lines, own, turned))
        state = after
    return [turned.T for _, _, turned in state]


def three_parts(value):
    high = value.astype(jnp.bfloat16)
    rest = value - high.astype(jnp.float32)
    middle = rest.astype(jnp.bfloat16)
    return high, middle, (rest - middle.astype(jnp.float32)).astype(jnp.bfloat16)


def split_store(split_ref, value, start, lane):
    order = split_ref.shape[0] // 3
    rows, lanes = value.shape
    for place, part in enumerate(three_parts(value)):
        split_ref[pl.ds(place * order + start, rows), pl.ds(lane, lanes)] = part


def gram_of(split_ref):
    order = split_ref.shape[0] // 3
    total = split_ref.shape[1]

    def body(place, acc):
        lanes = pl.ds(pl.multiple_of(place * DEPTH, DEPTH), DEPTH)
        return acc + lax.dot_general(
            split_ref[:, lanes],
            split_ref[: 2 * order, lanes],
            (((1,), (1,)), ((), ())),
            preferred_element_type=jnp.float32,
        )

    acc = lax.fori_loop(0, total // DEPTH, body, jnp.zeros((3 * order, 2 * order), jnp.float32))
    outer = acc[2 * order :, :order]
    inner = acc[:order, order:] + acc[order : 2 * order, :order] + acc[order : 2 * order, order:]
    return acc[:order, :order] + (inner + (outer + outer.T))


def product(turned, split_ref, lanes, terms=3):
    order = split_ref.shape[0] // 3
    rows = turned.shape[0]
    parts = three_parts(turned)[:terms]
    weights = jnp.concatenate([jnp.concatenate([part, part], axis=1) for part in parts], axis=0)
    both = lax.dot_general(
        weights,
        split_ref[: 2 * order, lanes],
        (((1,), (0,)), ((), ())),
        preferred_element_type=jnp.float32,
    )
    if terms == 2:
        return both[:rows] + both[rows:]
    small = lax.dot_general(
        parts[0],
        split_ref[2 * order :, lanes],
        (((1,), (0,)), ((), ())),
        preferred_element_type=jnp.float32,
    )
    return both[:rows] + (both[rows : 2 * rows] + (both[2 * rows :] + small))


def spans(length, body):
    whole = length // SPAN * SPAN
    if length <= UNROLLED:
        for lane in range(0, whole, SPAN):
            body(lane, SPAN)
    else:

        def step(place, carry):
            body(pl.multiple_of(place * SPAN, SPAN), SPAN)
            return carry

        lax.fori_loop(0, length // SPAN, step, 0)
    if whole < length:
        body(whole, length - whole)


def load_rows(split_ref, refs, start):
    done = 0
    for ref in refs:

        def body(lane, size):
            split_store(split_ref, ref[:, pl.ds(lane, size)], start, done + lane)

        spans(ref.shape[1], body)
        done += ref.shape[1]


def cuts_of(refs):
    cuts = [0]
    for ref in refs:
        cuts.append(cuts[-1] + ref.shape[1])
    return cuts


def send_out(turned, split_ref, first_refs, second_refs, swap):
    half = split_ref.shape[0] // 6
    swapped = jnp.concatenate([turned[half:], turned[:half]], axis=0)
    arranged = jnp.where(swap, swapped, turned)
    first_cuts, second_cuts = cuts_of(first_refs), cuts_of(second_refs)
    cuts = sorted(set(first_cuts + second_cuts))
    for begin, end in zip(cuts[:-1], cuts[1:]):
        first = max(place for place, cut in enumerate(first_cuts) if cut <= begin)
        second = max(place for place, cut in enumerate(second_cuts) if cut <= begin)
        first_lane, second_lane = begin - first_cuts[first], begin - second_cuts[second]

        def body(lane, size):
            lines = product(arranged, split_ref, pl.ds(begin + lane, size))
            first_refs[first][:, pl.ds(first_lane + lane, size)] = lines[:half]
            second_refs[second][:, pl.ds(second_lane + lane, size)] = lines[half:]

        spans(end - begin, body)


def run_of(column, row, row_count, column_count):
    last = jnp.where(row == row_count - 1, row, row_count - 2 - row)
    odd = jnp.where(column == column_count - 1, last, row_count - 1 - row)
    return jnp.where(jnp.bitwise_and(column, 1) == 0, row, odd)


def hosted_slot():
    column, columns = lax.axis_index("col"), lax.axis_size("col")
    run = run_of(column, lax.axis_index("row"), lax.axis_size("row"), columns)
    return run * columns + column


def slot_count():
    return lax.axis_size("row") * lax.axis_size("col")


def prepare_kernel(order, in_ref, *refs):
    count = lax.axis_size("row")
    out_refs, buffer, ready = refs[:-2], refs[-2], refs[-1]
    cycles, rows = in_ref.shape[0], in_ref.shape[1] // count
    copies = [
        pltpu.make_async_copy(in_ref.at[cycle], buffer.at[cycle], ready.at[cycle])
        for cycle in range(cycles)
    ]
    for copy in copies:
        copy.start()
    me = lax.axis_index("row")
    column, columns = lax.axis_index("col"), lax.axis_size("col")
    per_piece = cycles // PIECES
    for cycle, copy in enumerate(copies):
        copy.wait()
        piece, place = divmod(cycle, per_piece)
        for offset in range(count):
            tile = run_of(column, jnp.bitwise_xor(me, offset), count, columns)
            out_ref = out_refs[order.index((offset, piece))]
            out_ref[:, place * rows : (place + 1) * rows] = buffer[
                cycle, pl.ds(tile, rows, stride=count), :
            ].T


def odd_chip(slot):
    return jnp.bitwise_and(slot // 2, 1)


def first_kernel(order, near_count, *refs):
    chunk_refs, out_refs, split_ref = refs[: len(order)], refs[len(order) : -1], refs[-1]
    me, count = lax.axis_index("row"), lax.axis_size("row")
    total = split_ref.shape[1]
    rows = split_ref.shape[0] // 3
    per_piece = total // (PIECES * count * rows)
    for (offset, piece), chunk_ref in zip(order, chunk_refs):
        peer = jnp.bitwise_xor(me, offset)
        for place in range(per_piece):
            lane = ((piece * per_piece + place) * count + peer) * rows
            split_store(
                split_ref,
                chunk_ref[:, place * rows : (place + 1) * rows],
                0,
                pl.multiple_of(lane, rows),
            )
    (turned,) = inner_solve(gram_of(split_ref))
    slot = hosted_slot()
    bottom_first = jnp.logical_or(odd_chip(slot) == 1, slot == 0)
    send_out(turned, split_ref, out_refs[-near_count:], out_refs[:-near_count], bottom_first)


def middle_kernel(near_count, *refs):
    off_out, on_out, near_ref, far_ref = refs[-4:]
    in_refs, own_refs = refs[: (len(refs) - 4) // 2], refs[(len(refs) - 4) // 2 : -4]
    far_in, near_in = in_refs[:-near_count], in_refs[-near_count:]
    second, first = own_refs[:-near_count], own_refs[-near_count:]
    slot, slots = hosted_slot(), slot_count()
    half = off_out.shape[0]
    odd = odd_chip(slot)
    at_end = jnp.logical_or(slot == 0, slot == slots - 1).astype(jnp.int32)
    near_own = pl.multiple_of(odd * half, half)
    near_other = pl.multiple_of((1 - odd) * half, half)
    far_own = pl.multiple_of(jnp.bitwise_xor(1 - odd, at_end) * half, half)
    far_other = pl.multiple_of(jnp.bitwise_xor(odd, at_end) * half, half)
    load_rows(near_ref, first, near_own)
    load_rows(near_ref, near_in, near_other)
    load_rows(far_ref, second, far_own)
    load_rows(far_ref, far_in, far_other)
    near, far = inner_solve(gram_of(near_ref), gram_of(far_ref))
    near_half = jnp.where(odd == 0, near[half:], near[:half])
    flipped = jnp.logical_or(slot == 1, slot == slots - 1)
    far_bottom = jnp.logical_xor(odd == 1, flipped)
    far_half = jnp.where(far_bottom, far[half:], far[:half])

    def body(lane, size):
        near_lines = product(near_half, near_ref, pl.ds(lane, size))
        far_lines = product(far_half, far_ref, pl.ds(lane, size))
        split_store(near_ref, near_lines, near_other, lane)
        split_store(near_ref, far_lines, near_own, lane)

    spans(near_ref.shape[1], body)
    (turned,) = inner_solve(gram_of(near_ref))
    swap = jnp.logical_and(jnp.bitwise_and(slot, 1) == 0, slot != 0)
    send_out(turned, near_ref, [off_out], [on_out], swap)


def last_kernel(off_in, on_in, out_ref, split_ref, buffer, done):
    half = off_in.shape[0]
    odd = jnp.bitwise_and(lax.axis_index("col"), 1)
    load_rows(split_ref, [off_in], pl.multiple_of(odd * half, half))
    load_rows(split_ref, [on_in], pl.multiple_of((1 - odd) * half, half))
    (turned,) = inner_solve(gram_of(split_ref))
    total = split_ref.shape[1]

    def copy_of(lane):
        rows = pl.ds(lane, SPAN)
        return pltpu.make_async_copy(buffer.at[rows], out_ref.at[rows], done.at[lane // SPAN])

    def body(lane, size):
        lines = product(turned, split_ref, pl.ds(lane, size), terms=2)
        for place in range(0, size, LANES):
            buffer[pl.ds(lane + place, LANES), :] = lines[:, place : place + LANES].T
        copy_of(lane).start()

    spans(total, body)
    spans(total, lambda lane, size: copy_of(lane).wait())


def in_vmem(count):
    return [pl.BlockSpec(memory_space=pltpu.VMEM)] * count


def host_of(slot, row_count, column_count):
    run, column = divmod(slot, column_count)
    row = run
    if column == column_count - 1:
        row = run if run == row_count - 1 else row_count - 2 - run
    elif column % 2:
        row = row_count - 1 - run
    return row * column_count + column


def peer_pairs(offset, first_row, width, row_count, column_count):
    pairs = []
    for row in range(row_count):
        for column in range(column_count):
            peer = (row ^ offset) * column_count + column
            slot = host_of(peer, row_count, column_count)
            if (slot + 1) * width > first_row:
                pairs.append((row * column_count + column, peer))
    return pairs


def swap_pairs(first_row, width, row_count, column_count):
    slots = row_count * column_count
    near_pairs, far_pairs = [], []
    for slot in range(slots):
        if (slot + 1) * width <= first_row:
            continue
        source = host_of(slot, row_count, column_count)
        step = -2 if slot // 2 % 2 else 2
        near_pairs.append((source, host_of(slot + step, row_count, column_count)))
        target = slot - step if 0 <= slot - step < slots else slot ^ 1
        far_pairs.append((source, host_of(target, row_count, column_count)))
    return near_pairs, far_pairs


def per_device(factor_tiles):
    cycles, rows, tiles, width = factor_tiles.shape
    count, columns = lax.axis_size("row"), lax.axis_size("col")
    slots = count * columns
    half = width // 2
    length = cycles * rows * count
    axes = ("row", "col")
    split_bytes, spare = 6 * width * length, spare_bytes * length
    params = pltpu.CompilerParams(vmem_limit_bytes=split_bytes + spare)
    more_params = pltpu.CompilerParams(vmem_limit_bytes=2 * split_bytes + spare)
    whole_half = jax.ShapeDtypeStruct((half, length), jnp.float32)
    split = pltpu.VMEM((3 * width, length), jnp.bfloat16)

    order = [(peer, part) for peer in range(tiles - 1, -1, -1) for part in range(PIECES - 1, -1, -1)]
    pieces = len(order)
    chunks = pl.pallas_call(
        functools.partial(prepare_kernel, order),
        in_specs=[pl.BlockSpec(memory_space=pltpu.HBM)],
        out_specs=in_vmem(pieces),
        out_shape=[jax.ShapeDtypeStruct((width, cycles * rows // PIECES), jnp.float32)] * pieces,
        scratch_shapes=[
            pltpu.VMEM((cycles, rows * tiles, width), jnp.float32),
            pltpu.SemaphoreType.DMA((cycles,)),
        ],
        compiler_params=params,
        name="prepare",
    )(factor_tiles.reshape(cycles, rows * tiles, width))
    received = list(chunks)
    for place, (offset, piece) in enumerate(order):
        if offset:
            pairs = peer_pairs(offset, piece * (length // PIECES), width, count, columns)
            received[place] = lax.ppermute(chunks[place], axes, pairs)

    unit = length // UNITS
    near_starts = [0] + [cut * unit for cut in NEAR_CUTS]
    far_starts = [0] + [cut * unit for cut in FAR_CUTS]
    near_count = len(near_starts)
    halves = [
        jax.ShapeDtypeStruct((half, end - start), jnp.float32)
        for starts in (far_starts, near_starts)
        for start, end in zip(starts, starts[1:] + [length])
    ]
    moved = pl.pallas_call(
        functools.partial(first_kernel, order, near_count),
        in_specs=in_vmem(pieces),
        out_specs=in_vmem(len(halves)),
        out_shape=halves,
        scratch_shapes=[split],
        compiler_params=params,
        name="first_round",
    )(*received)
    far, near = list(moved[:-near_count]), list(moved[-near_count:])

    def swapped(value, first_row, side):
        return lax.ppermute(value, axes, swap_pairs(first_row, width, count, columns)[side])

    far = [swapped(value, start, 1) for value, start in zip(far, far_starts)]
    near = [swapped(value, start, 0) for value, start in zip(near, near_starts)]
    off, on = pl.pallas_call(
        functools.partial(middle_kernel, near_count),
        in_specs=in_vmem(2 * len(halves)),
        out_specs=in_vmem(2),
        out_shape=[whole_half] * 2,
        scratch_shapes=[split] * 2,
        compiler_params=more_params,
        name="middle_rounds",
    )(*far, *near, *moved)

    off_pairs, on_pairs = [], []
    for slot in range(slots):
        target = slot + 1 if slot % 2 else slot - 1
        source = host_of(slot, count, columns)
        off_pairs.append((source, target if 0 <= target < slots else slot))
        on_pairs.append((source, slot ^ 1))
    off = lax.ppermute(off, axes, off_pairs)
    on = lax.ppermute(on, axes, on_pairs)
    return pl.pallas_call(
        last_kernel,
        in_specs=in_vmem(2),
        out_specs=pl.BlockSpec(memory_space=pltpu.HBM),
        out_shape=jax.ShapeDtypeStruct((length, width), jnp.float32),
        scratch_shapes=[
            split,
            pltpu.VMEM((length, width), jnp.float32),
            pltpu.SemaphoreType.DMA((length // SPAN,)),
        ],
        compiler_params=params,
        name="last_round",
    )(off, on)


def solution(mesh):
    return jax.shard_map(
        per_device,
        mesh=mesh,
        in_specs=(P(None, "row", None, "col"),),
        out_specs=P(None, ("row", "col")),
        check_vma=False,
    )
```

```python
import functools

import jax
import jax.numpy as jnp
from jax import lax
from jax.experimental import pallas as pl
from jax.experimental.pallas import tpu as pltpu
from jax.sharding import PartitionSpec as P

LOGB = 7
OUTER = 4
INNER = 8
LANES = 128
SUBLANES = 8
SPAN = 512
DEPTH = 2048
UNROLLED = 4096
UNITS = 32
NEAR_CUTS = (10, 22)
FAR_CUTS = (16, 24)
PIECES = 2

damping_ratio = 0.01
spare_bytes = 2048


def partner_columns(value, stride):
    if 2 * stride == value.shape[-1]:
        return pltpu.roll(value, stride, 1)
    column = lax.broadcasted_iota(jnp.int32, value.shape, 1)
    return jnp.take_along_axis(value, jnp.bitwise_xor(column, stride), axis=1)


def partner_rows(value, stride):
    order = value.shape[0]
    if stride >= 8:
        pieces = [value[start : start + stride] for start in range(0, order, stride)]
        return jnp.concatenate([pieces[place ^ 1] for place in range(len(pieces))], axis=0)
    row = lax.broadcasted_iota(jnp.int32, value.shape, 0)
    is_tail = jnp.bitwise_and(row, stride) != 0
    return jnp.where(is_tail, pltpu.roll(value, stride, 0), pltpu.roll(value, order - stride, 0))


def turn_of(own, other, cross):
    gap = own - other
    total = own + other
    base = gap * gap + damping_ratio * total * total
    tangent = jnp.where(base > 0.0, 2.0 * cross * gap / jnp.where(base > 0.0, base, 1.0), 0.0)
    inverse = lax.rsqrt(1.0 + tangent * tangent)
    square = 0.5 + 0.5 * inverse
    root = lax.rsqrt(square)
    return square * root, 0.5 * tangent * inverse * root


def inner_solve(*grams):
    shape = grams[0].shape
    row = lax.broadcasted_iota(jnp.int32, shape, 0)
    column = lax.broadcasted_iota(jnp.int32, shape, 1)
    mixed = jnp.bitwise_xor(row, column)

    def line_of(lines, place):
        return jnp.broadcast_to(lines[place : place + 1], (SUBLANES, shape[1]))

    def spread(line):
        return jnp.broadcast_to(line[None], (shape[0] // SUBLANES, *line.shape)).reshape(shape)

    state = []
    for gram in grams:
        lines = gram
        for bit in range(LOGB):
            is_set = jnp.bitwise_and(column, 2**bit) != 0
            lines = jnp.where(is_set, partner_rows(lines, 2**bit), lines)
        start = jnp.where(row == column, 1.0, 0.0).astype(jnp.float32)
        state.append((lines, line_of(lines, 0), start))
    for step in range(INNER):
        stride = 2 ** ((LOGB - 1 - step) % LOGB)
        after = []
        for lines, own, turned in state:
            other = partner_columns(own, stride)
            cross = line_of(lines, stride)
            cosine, sine = turn_of(own, other, cross)
            own = cosine * (cosine * own + 2.0 * sine * cross) + sine * sine * other
            cosine, sine = spread(cosine), spread(sine)
            turned = turned * cosine + partner_columns(turned, stride) * sine
            if step + 1 < INNER:
                across = partner_rows(partner_columns(lines, stride), stride)
                lines = lines * cosine + across * sine
                cos_mixed = jnp.take_along_axis(cosine, mixed, axis=1)
                sin_mixed = jnp.take_along_axis(sine, mixed, axis=1)
                lines = lines * cos_mixed + partner_rows(lines, stride) * sin_mixed
            after.append((lines, own, turned))
        state = after
    return [turned.T for _, _, turned in state]


def three_parts(value):
    high = value.astype(jnp.bfloat16)
    rest = value - high.astype(jnp.float32)
    middle = rest.astype(jnp.bfloat16)
    return high, middle, (rest - middle.astype(jnp.float32)).astype(jnp.bfloat16)


def split_store(split_ref, value, start, lane):
    order = split_ref.shape[0] // 3
    rows, lanes = value.shape
    for place, part in enumerate(three_parts(value)):
        split_ref[pl.ds(place * order + start, rows), pl.ds(lane, lanes)] = part


def gram_of(split_ref):
    order = split_ref.shape[0] // 3
    total = split_ref.shape[1]

    def body(place, acc):
        lanes = pl.ds(pl.multiple_of(place * DEPTH, DEPTH), DEPTH)
        return acc + lax.dot_general(
            split_ref[:, lanes],
            split_ref[: 2 * order, lanes],
            (((1,), (1,)), ((), ())),
            preferred_element_type=jnp.float32,
        )

    acc = lax.fori_loop(0, total // DEPTH, body, jnp.zeros((3 * order, 2 * order), jnp.float32))
    outer = acc[2 * order :, :order]
    inner = acc[:order, order:] + acc[order : 2 * order, :order] + acc[order : 2 * order, order:]
    return acc[:order, :order] + (inner + (outer + outer.T))


def product(turned, split_ref, lanes, terms=3):
    order = split_ref.shape[0] // 3
    rows = turned.shape[0]
    parts = three_parts(turned)[:terms]
    weights = jnp.concatenate([jnp.concatenate([part, part], axis=1) for part in parts], axis=0)
    both = lax.dot_general(
        weights,
        split_ref[: 2 * order, lanes],
        (((1,), (0,)), ((), ())),
        preferred_element_type=jnp.float32,
    )
    if terms == 2:
        return both[:rows] + both[rows:]
    small = lax.dot_general(
        parts[0],
        split_ref[2 * order :, lanes],
        (((1,), (0,)), ((), ())),
        preferred_element_type=jnp.float32,
    )
    return both[:rows] + (both[rows : 2 * rows] + (both[2 * rows :] + small))


def spans(length, body):
    whole = length // SPAN * SPAN
    if length <= UNROLLED:
        for lane in range(0, whole, SPAN):
            body(lane, SPAN)
    else:

        def step(place, carry):
            body(pl.multiple_of(place * SPAN, SPAN), SPAN)
            return carry

        lax.fori_loop(0, length // SPAN, step, 0)
    if whole < length:
        body(whole, length - whole)


def load_rows(split_ref, refs, start):
    done = 0
    for ref in refs:

        def body(lane, size):
            split_store(split_ref, ref[:, pl.ds(lane, size)], start, done + lane)

        spans(ref.shape[1], body)
        done += ref.shape[1]


def cuts_of(refs):
    cuts = [0]
    for ref in refs:
        cuts.append(cuts[-1] + ref.shape[1])
    return cuts


def send_out(turned, split_ref, first_refs, second_refs, swap):
    half = split_ref.shape[0] // 6
    swapped = jnp.concatenate([turned[half:], turned[:half]], axis=0)
    arranged = jnp.where(swap, swapped, turned)
    first_cuts, second_cuts = cuts_of(first_refs), cuts_of(second_refs)
    cuts = sorted(set(first_cuts + second_cuts))
    for begin, end in zip(cuts[:-1], cuts[1:]):
        first = max(place for place, cut in enumerate(first_cuts) if cut <= begin)
        second = max(place for place, cut in enumerate(second_cuts) if cut <= begin)
        first_lane, second_lane = begin - first_cuts[first], begin - second_cuts[second]

        def body(lane, size):
            lines = product(arranged, split_ref, pl.ds(begin + lane, size))
            first_refs[first][:, pl.ds(first_lane + lane, size)] = lines[:half]
            second_refs[second][:, pl.ds(second_lane + lane, size)] = lines[half:]

        spans(end - begin, body)


def run_of(column, row, row_count, column_count):
    last = jnp.where(row == row_count - 1, row, row_count - 2 - row)
    odd = jnp.where(column == column_count - 1, last, row_count - 1 - row)
    return jnp.where(jnp.bitwise_and(column, 1) == 0, row, odd)


def hosted_slot():
    column, columns = lax.axis_index("col"), lax.axis_size("col")
    run = run_of(column, lax.axis_index("row"), lax.axis_size("row"), columns)
    return run * columns + column


def slot_count():
    return lax.axis_size("row") * lax.axis_size("col")


def prepare_kernel(order, in_ref, *refs):
    count = lax.axis_size("row")
    out_refs, buffer, ready = refs[:-2], refs[-2], refs[-1]
    cycles, rows = in_ref.shape[0], in_ref.shape[1] // count
    copies = [
        pltpu.make_async_copy(in_ref.at[cycle], buffer.at[cycle], ready.at[cycle])
        for cycle in range(cycles)
    ]
    for copy in copies:
        copy.start()
    me = lax.axis_index("row")
    column, columns = lax.axis_index("col"), lax.axis_size("col")
    per_piece = cycles // PIECES
    for cycle, copy in enumerate(copies):
        copy.wait()
        piece, place = divmod(cycle, per_piece)
        for offset in range(count):
            tile = run_of(column, jnp.bitwise_xor(me, offset), count, columns)
            out_ref = out_refs[order.index((offset, piece))]
            out_ref[:, place * rows : (place + 1) * rows] = buffer[
                cycle, pl.ds(tile, rows, stride=count), :
            ].T


def odd_chip(slot):
    return jnp.bitwise_and(slot // 2, 1)


def first_kernel(order, near_count, *refs):
    chunk_refs, out_refs, split_ref = refs[: len(order)], refs[len(order) : -1], refs[-1]
    me, count = lax.axis_index("row"), lax.axis_size("row")
    total = split_ref.shape[1]
    rows = split_ref.shape[0] // 3
    per_piece = total // (PIECES * count * rows)
    for (offset, piece), chunk_ref in zip(order, chunk_refs):
        peer = jnp.bitwise_xor(me, offset)
        for place in range(per_piece):
            lane = ((piece * per_piece + place) * count + peer) * rows
            split_store(
                split_ref,
                chunk_ref[:, place * rows : (place + 1) * rows],
                0,
                pl.multiple_of(lane, rows),
            )
    (turned,) = inner_solve(gram_of(split_ref))
    slot = hosted_slot()
    bottom_first = jnp.logical_or(odd_chip(slot) == 1, slot == 0)
    send_out(turned, split_ref, out_refs[-near_count:], out_refs[:-near_count], bottom_first)


def middle_kernel(near_count, *refs):
    off_out, on_out, near_ref, far_ref = refs[-4:]
    in_refs, own_refs = refs[: (len(refs) - 4) // 2], refs[(len(refs) - 4) // 2 : -4]
    far_in, near_in = in_refs[:-near_count], in_refs[-near_count:]
    second, first = own_refs[:-near_count], own_refs[-near_count:]
    slot, slots = hosted_slot(), slot_count()
    half = off_out.shape[0]
    odd = odd_chip(slot)
    at_end = jnp.logical_or(slot == 0, slot == slots - 1).astype(jnp.int32)
    near_own = pl.multiple_of(odd * half, half)
    near_other = pl.multiple_of((1 - odd) * half, half)
    far_own = pl.multiple_of(jnp.bitwise_xor(1 - odd, at_end) * half, half)
    far_other = pl.multiple_of(jnp.bitwise_xor(odd, at_end) * half, half)
    load_rows(near_ref, first, near_own)
    load_rows(near_ref, near_in, near_other)
    load_rows(far_ref, second, far_own)
    load_rows(far_ref, far_in, far_other)
    near, far = inner_solve(gram_of(near_ref), gram_of(far_ref))
    near_half = jnp.where(odd == 0, near[half:], near[:half])
    flipped = jnp.logical_or(slot == 1, slot == slots - 1)
    far_bottom = jnp.logical_xor(odd == 1, flipped)
    far_half = jnp.where(far_bottom, far[half:], far[:half])

    def body(lane, size):
        near_lines = product(near_half, near_ref, pl.ds(lane, size))
        far_lines = product(far_half, far_ref, pl.ds(lane, size))
        split_store(near_ref, near_lines, near_other, lane)
        split_store(near_ref, far_lines, near_own, lane)

    spans(near_ref.shape[1], body)
    (turned,) = inner_solve(gram_of(near_ref))
    swap = jnp.logical_and(jnp.bitwise_and(slot, 1) == 0, slot != 0)
    send_out(turned, near_ref, [off_out], [on_out], swap)


def last_kernel(off_in, on_in, out_ref, split_ref, buffer, done):
    half = off_in.shape[0]
    odd = jnp.bitwise_and(lax.axis_index("col"), 1)
    load_rows(split_ref, [off_in], pl.multiple_of(odd * half, half))
    load_rows(split_ref, [on_in], pl.multiple_of((1 - odd) * half, half))
    (turned,) = inner_solve(gram_of(split_ref))
    total = split_ref.shape[1]

    def copy_of(lane):
        rows = pl.ds(lane, SPAN)
        return pltpu.make_async_copy(buffer.at[rows], out_ref.at[rows], done.at[lane // SPAN])

    def body(lane, size):
        lines = product(turned, split_ref, pl.ds(lane, size), terms=2)
        for place in range(0, size, LANES):
            buffer[pl.ds(lane + place, LANES), :] = lines[:, place : place + LANES].T
        copy_of(lane).start()

    spans(total, body)
    spans(total, lambda lane, size: copy_of(lane).wait())


def in_vmem(count):
    return [pl.BlockSpec(memory_space=pltpu.VMEM)] * count


def host_of(slot, row_count, column_count):
    run, column = divmod(slot, column_count)
    row = run
    if column == column_count - 1:
        row = run if run == row_count - 1 else row_count - 2 - run
    elif column % 2:
        row = row_count - 1 - run
    return row * column_count + column


def peer_pairs(offset, first_row, width, row_count, column_count):
    pairs = []
    for row in range(row_count):
        for column in range(column_count):
            peer = (row ^ offset) * column_count + column
            slot = host_of(peer, row_count, column_count)
            if (slot + 1) * width > first_row:
                pairs.append((row * column_count + column, peer))
    return pairs


def swap_pairs(first_row, width, row_count, column_count):
    slots = row_count * column_count
    near_pairs, far_pairs = [], []
    for slot in range(slots):
        if (slot + 1) * width <= first_row:
            continue
        source = host_of(slot, row_count, column_count)
        step = -2 if slot // 2 % 2 else 2
        near_pairs.append((source, host_of(slot + step, row_count, column_count)))
        target = slot - step if 0 <= slot - step < slots else slot ^ 1
        far_pairs.append((source, host_of(target, row_count, column_count)))
    return near_pairs, far_pairs


def per_device(factor_tiles):
    cycles, rows, tiles, width = factor_tiles.shape
    count, columns = lax.axis_size("row"), lax.axis_size("col")
    slots = count * columns
    half = width // 2
    length = cycles * rows * count
    axes = ("row", "col")
    split_bytes, spare = 6 * width * length, spare_bytes * length
    params = pltpu.CompilerParams(vmem_limit_bytes=split_bytes + spare)
    more_params = pltpu.CompilerParams(vmem_limit_bytes=2 * split_bytes + spare)
    whole_half = jax.ShapeDtypeStruct((half, length), jnp.float32)
    split = pltpu.VMEM((3 * width, length), jnp.bfloat16)

    order = [(peer, part) for peer in range(tiles - 1, -1, -1) for part in range(PIECES - 1, -1, -1)]
    pieces = len(order)
    chunks = pl.pallas_call(
        functools.partial(prepare_kernel, order),
        in_specs=[pl.BlockSpec(memory_space=pltpu.HBM)],
        out_specs=in_vmem(pieces),
        out_shape=[jax.ShapeDtypeStruct((width, cycles * rows // PIECES), jnp.float32)] * pieces,
        scratch_shapes=[
            pltpu.VMEM((cycles, rows * tiles, width), jnp.float32),
            pltpu.SemaphoreType.DMA((cycles,)),
        ],
        compiler_params=params,
        name="prepare",
    )(factor_tiles.reshape(cycles, rows * tiles, width))
    received = list(chunks)
    for place, (offset, piece) in enumerate(order):
        if offset:
            pairs = peer_pairs(offset, piece * (length // PIECES), width, count, columns)
            received[place] = lax.ppermute(chunks[place], axes, pairs)

    unit = length // UNITS
    near_starts = [0] + [cut * unit for cut in NEAR_CUTS]
    far_starts = [0] + [cut * unit for cut in FAR_CUTS]
    near_count = len(near_starts)
    halves = [
        jax.ShapeDtypeStruct((half, end - start), jnp.float32)
        for starts in (far_starts, near_starts)
        for start, end in zip(starts, starts[1:] + [length])
    ]
    moved = pl.pallas_call(
        functools.partial(first_kernel, order, near_count),
        in_specs=in_vmem(pieces),
        out_specs=in_vmem(len(halves)),
        out_shape=halves,
        scratch_shapes=[split],
        compiler_params=params,
        name="first_round",
    )(*received)
    far, near = list(moved[:-near_count]), list(moved[-near_count:])

    def swapped(value, first_row, side):
        return lax.ppermute(value, axes, swap_pairs(first_row, width, count, columns)[side])

    far = [swapped(value, start, 1) for value, start in zip(far, far_starts)]
    near = [swapped(value, start, 0) for value, start in zip(near, near_starts)]
    off, on = pl.pallas_call(
        functools.partial(middle_kernel, near_count),
        in_specs=in_vmem(2 * len(halves)),
        out_specs=in_vmem(2),
        out_shape=[whole_half] * 2,
        scratch_shapes=[split] * 2,
        compiler_params=more_params,
        name="middle_rounds",
    )(*far, *near, *moved)

    off_pairs, on_pairs = [], []
    for slot in range(slots):
        target = slot + 1 if slot % 2 else slot - 1
        source = host_of(slot, count, columns)
        off_pairs.append((source, target if 0 <= target < slots else slot))
        on_pairs.append((source, slot ^ 1))
    off = lax.ppermute(off, axes, off_pairs)
    on = lax.ppermute(on, axes, on_pairs)
    return pl.pallas_call(
        last_kernel,
        in_specs=in_vmem(2),
        out_specs=pl.BlockSpec(memory_space=pltpu.HBM),
        out_shape=jax.ShapeDtypeStruct((length, width), jnp.float32),
        scratch_shapes=[
            split,
            pltpu.VMEM((length, width), jnp.float32),
            pltpu.SemaphoreType.DMA((length // SPAN,)),
        ],
        compiler_params=params,
        name="last_round",
    )(off, on)


def solution(mesh):
    return jax.shard_map(
        per_device,
        mesh=mesh,
        in_specs=(P(None, "row", None, "col"),),
        out_specs=P(None, ("row", "col")),
        check_vma=False,
    )
```

```python
import functools

import jax
import jax.numpy as jnp
from jax import lax
from jax.experimental import pallas as pl
from jax.experimental.pallas import tpu as pltpu
from jax.sharding import PartitionSpec as P

LOGB = 7
OUTER = 4
INNER = 8
LANES = 128
SUBLANES = 8
SPAN = 512
DEPTH = 2048
UNROLLED = 4096
UNITS = 32
NEAR_CUTS = (10, 22)
FAR_CUTS = (16, 24)
PIECES = 2

damping_ratio = 0.01
spare_bytes = 2048


def partner_columns(value, stride):
    if 2 * stride == value.shape[-1]:
        return pltpu.roll(value, stride, 1)
    column = lax.broadcasted_iota(jnp.int32, value.shape, 1)
    return jnp.take_along_axis(value, jnp.bitwise_xor(column, stride), axis=1)


def partner_rows(value, stride):
    order = value.shape[0]
    if stride >= 8:
        pieces = [value[start : start + stride] for start in range(0, order, stride)]
        return jnp.concatenate([pieces[place ^ 1] for place in range(len(pieces))], axis=0)
    row = lax.broadcasted_iota(jnp.int32, value.shape, 0)
    is_tail = jnp.bitwise_and(row, stride) != 0
    return jnp.where(is_tail, pltpu.roll(value, stride, 0), pltpu.roll(value, order - stride, 0))


def turn_of(own, other, cross):
    gap = own - other
    total = own + other
    base = gap * gap + damping_ratio * total * total
    tangent = jnp.where(base > 0.0, 2.0 * cross * gap / jnp.where(base > 0.0, base, 1.0), 0.0)
    inverse = lax.rsqrt(1.0 + tangent * tangent)
    square = 0.5 + 0.5 * inverse
    root = lax.rsqrt(square)
    return square * root, 0.5 * tangent * inverse * root


def inner_solve(*grams):
    shape = grams[0].shape
    row = lax.broadcasted_iota(jnp.int32, shape, 0)
    column = lax.broadcasted_iota(jnp.int32, shape, 1)
    mixed = jnp.bitwise_xor(row, column)

    def line_of(lines, place):
        return jnp.broadcast_to(lines[place : place + 1], (SUBLANES, shape[1]))

    def spread(line):
        return jnp.broadcast_to(line[None], (shape[0] // SUBLANES, *line.shape)).reshape(shape)

    state = []
    for gram in grams:
        lines = gram
        for bit in range(LOGB):
            is_set = jnp.bitwise_and(column, 2**bit) != 0
            lines = jnp.where(is_set, partner_rows(lines, 2**bit), lines)
        start = jnp.where(row == column, 1.0, 0.0).astype(jnp.float32)
        state.append((lines, line_of(lines, 0), start))
    for step in range(INNER):
        stride = 2 ** ((LOGB - 1 - step) % LOGB)
        after = []
        for lines, own, turned in state:
            other = partner_columns(own, stride)
            cross = line_of(lines, stride)
            cosine, sine = turn_of(own, other, cross)
            own = cosine * (cosine * own + 2.0 * sine * cross) + sine * sine * other
            cosine, sine = spread(cosine), spread(sine)
            turned = turned * cosine + partner_columns(turned, stride) * sine
            if step + 1 < INNER:
                across = partner_rows(partner_columns(lines, stride), stride)
                lines = lines * cosine + across * sine
                cos_mixed = jnp.take_along_axis(cosine, mixed, axis=1)
                sin_mixed = jnp.take_along_axis(sine, mixed, axis=1)
                lines = lines * cos_mixed + partner_rows(lines, stride) * sin_mixed
            after.append((lines, own, turned))
        state = after
    return [turned.T for _, _, turned in state]


def three_parts(value):
    high = value.astype(jnp.bfloat16)
    rest = value - high.astype(jnp.float32)
    middle = rest.astype(jnp.bfloat16)
    return high, middle, (rest - middle.astype(jnp.float32)).astype(jnp.bfloat16)


def split_store(split_ref, value, start, lane):
    order = split_ref.shape[0] // 3
    rows, lanes = value.shape
    high, middle, low = three_parts(value)
    for place, part in enumerate((middle, high, low)):
        split_ref[pl.ds(place * order + start, rows), pl.ds(lane, lanes)] = part


def gram_of(split_ref):
    order = split_ref.shape[0] // 3
    total = split_ref.shape[1]

    def body(place, acc):
        lanes = pl.ds(pl.multiple_of(place * DEPTH, DEPTH), DEPTH)
        return acc + lax.dot_general(
            split_ref[:, lanes],
            split_ref[: 2 * order, lanes],
            (((1,), (1,)), ((), ())),
            preferred_element_type=jnp.float32,
        )

    acc = lax.fori_loop(0, total // DEPTH, body, jnp.zeros((3 * order, 2 * order), jnp.float32))
    outer = acc[2 * order :, order:]
    inner = acc[:order, order:] + acc[order : 2 * order, :order] + acc[:order, :order]
    return acc[order : 2 * order, order:] + (inner + (outer + outer.T))


def product(turned, split_ref, lanes, terms=6):
    order = split_ref.shape[0] // 3
    rows = turned.shape[0]
    high, middle, low = three_parts(turned)

    def dot(weights, start):
        return lax.dot_general(
            jnp.concatenate([jnp.concatenate(pair, axis=1) for pair in weights], axis=0),
            split_ref[start : start + 2 * order, lanes],
            (((1,), (0,)), ((), ())),
            preferred_element_type=jnp.float32,
        )

    both = dot(((high, high), (middle, middle)), 0)
    if terms == 4:
        return both[:rows] + both[rows:]
    return both[:rows] + (both[rows:] + dot(((low, high),), order))


def spans(length, body):
    whole = length // SPAN * SPAN
    if length <= UNROLLED:
        for lane in range(0, whole, SPAN):
            body(lane, SPAN)
    else:

        def step(place, carry):
            body(pl.multiple_of(place * SPAN, SPAN), SPAN)
            return carry

        lax.fori_loop(0, length // SPAN, step, 0)
    if whole < length:
        body(whole, length - whole)


def load_rows(split_ref, refs, start):
    done = 0
    for ref in refs:

        def body(lane, size):
            split_store(split_ref, ref[:, pl.ds(lane, size)], start, done + lane)

        spans(ref.shape[1], body)
        done += ref.shape[1]


def cuts_of(refs):
    cuts = [0]
    for ref in refs:
        cuts.append(cuts[-1] + ref.shape[1])
    return cuts


def send_out(turned, split_ref, first_refs, second_refs, swap, terms=6):
    half = split_ref.shape[0] // 6
    swapped = jnp.concatenate([turned[half:], turned[:half]], axis=0)
    arranged = jnp.where(swap, swapped, turned)
    first_cuts, second_cuts = cuts_of(first_refs), cuts_of(second_refs)
    cuts = sorted(set(first_cuts + second_cuts))
    for begin, end in zip(cuts[:-1], cuts[1:]):
        first = max(place for place, cut in enumerate(first_cuts) if cut <= begin)
        second = max(place for place, cut in enumerate(second_cuts) if cut <= begin)
        first_lane, second_lane = begin - first_cuts[first], begin - second_cuts[second]

        def body(lane, size):
            lines = product(arranged, split_ref, pl.ds(begin + lane, size), terms)
            first_refs[first][:, pl.ds(first_lane + lane, size)] = lines[:half]
            second_refs[second][:, pl.ds(second_lane + lane, size)] = lines[half:]

        spans(end - begin, body)


def run_of(column, row, row_count, column_count):
    last = jnp.where(row == row_count - 1, row, row_count - 2 - row)
    odd = jnp.where(column == column_count - 1, last, row_count - 1 - row)
    return jnp.where(jnp.bitwise_and(column, 1) == 0, row, odd)


def hosted_slot():
    column, columns = lax.axis_index("col"), lax.axis_size("col")
    run = run_of(column, lax.axis_index("row"), lax.axis_size("row"), columns)
    return run * columns + column


def slot_count():
    return lax.axis_size("row") * lax.axis_size("col")


def prepare_kernel(order, in_ref, *refs):
    count = lax.axis_size("row")
    out_refs, buffer, ready = refs[:-2], refs[-2], refs[-1]
    cycles, rows = in_ref.shape[0], in_ref.shape[1] // count
    copies = [
        pltpu.make_async_copy(in_ref.at[cycle], buffer.at[cycle], ready.at[cycle])
        for cycle in range(cycles)
    ]
    for copy in copies:
        copy.start()
    me = lax.axis_index("row")
    column, columns = lax.axis_index("col"), lax.axis_size("col")
    per_piece = cycles // PIECES
    for cycle, copy in enumerate(copies):
        copy.wait()
        piece, place = divmod(cycle, per_piece)
        for offset in range(count):
            tile = run_of(column, jnp.bitwise_xor(me, offset), count, columns)
            out_ref = out_refs[order.index((offset, piece))]
            out_ref[:, place * rows : (place + 1) * rows] = buffer[
                cycle, pl.ds(tile, rows, stride=count), :
            ].T


def odd_chip(slot):
    return jnp.bitwise_and(slot // 2, 1)


def first_kernel(order, near_count, *refs):
    chunk_refs, out_refs, split_ref = refs[: len(order)], refs[len(order) : -1], refs[-1]
    me, count = lax.axis_index("row"), lax.axis_size("row")
    total = split_ref.shape[1]
    rows = split_ref.shape[0] // 3
    per_piece = total // (PIECES * count * rows)
    for (offset, piece), chunk_ref in zip(order, chunk_refs):
        peer = jnp.bitwise_xor(me, offset)
        for place in range(per_piece):
            lane = ((piece * per_piece + place) * count + peer) * rows
            split_store(
                split_ref,
                chunk_ref[:, place * rows : (place + 1) * rows],
                0,
                pl.multiple_of(lane, rows),
            )
    (turned,) = inner_solve(gram_of(split_ref))
    slot = hosted_slot()
    bottom_first = jnp.logical_or(odd_chip(slot) == 1, slot == 0)
    send_out(turned, split_ref, out_refs[-near_count:], out_refs[:-near_count], bottom_first)


def middle_kernel(near_count, *refs):
    off_out, on_out, near_ref, far_ref = refs[-4:]
    in_refs, own_refs = refs[: (len(refs) - 4) // 2], refs[(len(refs) - 4) // 2 : -4]
    far_in, near_in = in_refs[:-near_count], in_refs[-near_count:]
    second, first = own_refs[:-near_count], own_refs[-near_count:]
    slot, slots = hosted_slot(), slot_count()
    half = off_out.shape[0]
    odd = odd_chip(slot)
    at_end = jnp.logical_or(slot == 0, slot == slots - 1).astype(jnp.int32)
    near_own = pl.multiple_of(odd * half, half)
    near_other = pl.multiple_of((1 - odd) * half, half)
    far_own = pl.multiple_of(jnp.bitwise_xor(1 - odd, at_end) * half, half)
    far_other = pl.multiple_of(jnp.bitwise_xor(odd, at_end) * half, half)
    load_rows(near_ref, first, near_own)
    load_rows(near_ref, near_in, near_other)
    load_rows(far_ref, second, far_own)
    load_rows(far_ref, far_in, far_other)
    near, far = inner_solve(gram_of(near_ref), gram_of(far_ref))
    near_half = jnp.where(odd == 0, near[half:], near[:half])
    flipped = jnp.logical_or(slot == 1, slot == slots - 1)
    far_bottom = jnp.logical_xor(odd == 1, flipped)
    far_half = jnp.where(far_bottom, far[half:], far[:half])

    def body(lane, size):
        near_lines = product(near_half, near_ref, pl.ds(lane, size))
        far_lines = product(far_half, far_ref, pl.ds(lane, size))
        split_store(near_ref, near_lines, near_other, lane)
        split_store(near_ref, far_lines, near_own, lane)

    spans(near_ref.shape[1], body)
    (turned,) = inner_solve(gram_of(near_ref))
    swap = jnp.logical_and(jnp.bitwise_and(slot, 1) == 0, slot != 0)
    send_out(turned, near_ref, [off_out], [on_out], swap, terms=4)


def last_kernel(off_in, on_in, out_ref, split_ref, buffer, done):
    half = off_in.shape[0]
    odd = jnp.bitwise_and(lax.axis_index("col"), 1)
    load_rows(split_ref, [off_in], pl.multiple_of(odd * half, half))
    load_rows(split_ref, [on_in], pl.multiple_of((1 - odd) * half, half))
    (turned,) = inner_solve(gram_of(split_ref))
    total = split_ref.shape[1]

    def copy_of(lane):
        rows = pl.ds(lane, SPAN)
        return pltpu.make_async_copy(buffer.at[rows], out_ref.at[rows], done.at[lane // SPAN])

    def body(lane, size):
        lines = product(turned, split_ref, pl.ds(lane, size), terms=4)
        for place in range(0, size, LANES):
            buffer[pl.ds(lane + place, LANES), :] = lines[:, place : place + LANES].T
        copy_of(lane).start()

    spans(total, body)
    spans(total, lambda lane, size: copy_of(lane).wait())


def in_vmem(count):
    return [pl.BlockSpec(memory_space=pltpu.VMEM)] * count


def host_of(slot, row_count, column_count):
    run, column = divmod(slot, column_count)
    row = run
    if column == column_count - 1:
        row = run if run == row_count - 1 else row_count - 2 - run
    elif column % 2:
        row = row_count - 1 - run
    return row * column_count + column


def peer_pairs(offset, first_row, width, row_count, column_count):
    pairs = []
    for row in range(row_count):
        for column in range(column_count):
            peer = (row ^ offset) * column_count + column
            slot = host_of(peer, row_count, column_count)
            if (slot + 1) * width > first_row:
                pairs.append((row * column_count + column, peer))
    return pairs


def swap_pairs(first_row, width, row_count, column_count):
    slots = row_count * column_count
    near_pairs, far_pairs = [], []
    for slot in range(slots):
        if (slot + 1) * width <= first_row:
            continue
        source = host_of(slot, row_count, column_count)
        step = -2 if slot // 2 % 2 else 2
        near_pairs.append((source, host_of(slot + step, row_count, column_count)))
        target = slot - step if 0 <= slot - step < slots else slot ^ 1
        far_pairs.append((source, host_of(target, row_count, column_count)))
    return near_pairs, far_pairs


def per_device(factor_tiles):
    cycles, rows, tiles, width = factor_tiles.shape
    count, columns = lax.axis_size("row"), lax.axis_size("col")
    slots = count * columns
    half = width // 2
    length = cycles * rows * count
    axes = ("row", "col")
    split_bytes, spare = 6 * width * length, spare_bytes * length
    params = pltpu.CompilerParams(vmem_limit_bytes=split_bytes + spare)
    more_params = pltpu.CompilerParams(vmem_limit_bytes=2 * split_bytes + spare)
    whole_half = jax.ShapeDtypeStruct((half, length), jnp.float32)
    split = pltpu.VMEM((3 * width, length), jnp.bfloat16)

    order = [(peer, part) for peer in range(tiles - 1, -1, -1) for part in range(PIECES - 1, -1, -1)]
    pieces = len(order)
    chunks = pl.pallas_call(
        functools.partial(prepare_kernel, order),
        in_specs=[pl.BlockSpec(memory_space=pltpu.HBM)],
        out_specs=in_vmem(pieces),
        out_shape=[jax.ShapeDtypeStruct((width, cycles * rows // PIECES), jnp.float32)] * pieces,
        scratch_shapes=[
            pltpu.VMEM((cycles, rows * tiles, width), jnp.float32),
            pltpu.SemaphoreType.DMA((cycles,)),
        ],
        compiler_params=pltpu.CompilerParams(vmem_limit_bytes=61 * 1024 * 1024),
        name="prepare",
    )(factor_tiles.reshape(cycles, rows * tiles, width))
    received = list(chunks)
    for place, (offset, piece) in enumerate(order):
        if offset:
            pairs = peer_pairs(offset, piece * (length // PIECES), width, count, columns)
            received[place] = lax.ppermute(chunks[place], axes, pairs)

    unit = length // UNITS
    near_starts = [0] + [cut * unit for cut in NEAR_CUTS]
    far_starts = [0] + [cut * unit for cut in FAR_CUTS]
    near_count = len(near_starts)
    halves = [
        jax.ShapeDtypeStruct((half, end - start), jnp.float32)
        for starts in (far_starts, near_starts)
        for start, end in zip(starts, starts[1:] + [length])
    ]
    moved = pl.pallas_call(
        functools.partial(first_kernel, order, near_count),
        in_specs=in_vmem(pieces),
        out_specs=in_vmem(len(halves)),
        out_shape=halves,
        scratch_shapes=[split],
        compiler_params=params,
        name="first_round",
    )(*received)
    far, near = list(moved[:-near_count]), list(moved[-near_count:])

    def swapped(value, first_row, side):
        return lax.ppermute(value, axes, swap_pairs(first_row, width, count, columns)[side])

    far = [swapped(value, start, 1) for value, start in zip(far, far_starts)]
    near = [swapped(value, start, 0) for value, start in zip(near, near_starts)]
    off, on = pl.pallas_call(
        functools.partial(middle_kernel, near_count),
        in_specs=in_vmem(2 * len(halves)),
        out_specs=in_vmem(2),
        out_shape=[whole_half] * 2,
        scratch_shapes=[split] * 2,
        compiler_params=more_params,
        name="middle_rounds",
    )(*far, *near, *moved)

    off_pairs, on_pairs = [], []
    for slot in range(slots):
        target = slot + 1 if slot % 2 else slot - 1
        source = host_of(slot, count, columns)
        off_pairs.append((source, target if 0 <= target < slots else slot))
        on_pairs.append((source, slot ^ 1))
    off = lax.ppermute(off, axes, off_pairs)
    on = lax.ppermute(on, axes, on_pairs)
    return pl.pallas_call(
        last_kernel,
        in_specs=in_vmem(2),
        out_specs=pl.BlockSpec(memory_space=pltpu.HBM),
        out_shape=jax.ShapeDtypeStruct((length, width), jnp.float32),
        scratch_shapes=[
            split,
            pltpu.VMEM((length, width), jnp.float32),
            pltpu.SemaphoreType.DMA((length // SPAN,)),
        ],
        compiler_params=params,
        name="last_round",
    )(off, on)


def solution(mesh):
    return jax.shard_map(
        per_device,
        mesh=mesh,
        in_specs=(P(None, "row", None, "col"),),
        out_specs=P(None, ("row", "col")),
        check_vma=False,
    )
```

```python
import functools

import jax
import jax.numpy as jnp
from jax import lax
from jax.experimental import pallas as pl
from jax.experimental.pallas import tpu as pltpu
from jax.sharding import PartitionSpec as P

LOGB = 7
OUTER = 4
INNER = 8
LANES = 128
SUBLANES = 8
SPAN = 512
DEPTH = 2048
UNROLLED = 4096
UNITS = 32
NEAR_CUTS = (10, 22)
FAR_CUTS = (16, 24)
LAST_CUTS = (18,)
PIECES = 2

damping_ratio = 0.01
spare_bytes = 2048


def partner_columns(value, stride):
    if 2 * stride == value.shape[-1]:
        return pltpu.roll(value, stride, 1)
    column = lax.broadcasted_iota(jnp.int32, value.shape, 1)
    return jnp.take_along_axis(value, jnp.bitwise_xor(column, stride), axis=1)


def partner_rows(value, stride):
    order = value.shape[0]
    if stride >= 8:
        pieces = [value[start : start + stride] for start in range(0, order, stride)]
        return jnp.concatenate([pieces[place ^ 1] for place in range(len(pieces))], axis=0)
    row = lax.broadcasted_iota(jnp.int32, value.shape, 0)
    is_tail = jnp.bitwise_and(row, stride) != 0
    return jnp.where(is_tail, pltpu.roll(value, stride, 0), pltpu.roll(value, order - stride, 0))


def turn_of(own, other, cross):
    gap = own - other
    total = own + other
    base = gap * gap + damping_ratio * total * total
    tangent = jnp.where(base > 0.0, 2.0 * cross * gap / jnp.where(base > 0.0, base, 1.0), 0.0)
    inverse = lax.rsqrt(1.0 + tangent * tangent)
    square = 0.5 + 0.5 * inverse
    root = lax.rsqrt(square)
    return square * root, 0.5 * tangent * inverse * root


def inner_solve(*grams):
    shape = grams[0].shape
    row = lax.broadcasted_iota(jnp.int32, shape, 0)
    column = lax.broadcasted_iota(jnp.int32, shape, 1)
    mixed = jnp.bitwise_xor(row, column)

    def line_of(lines, place):
        return jnp.broadcast_to(lines[place : place + 1], (SUBLANES, shape[1]))

    def spread(line):
        return jnp.broadcast_to(line[None], (shape[0] // SUBLANES, *line.shape)).reshape(shape)

    state = []
    for gram in grams:
        lines = gram
        for bit in range(LOGB):
            is_set = jnp.bitwise_and(column, 2**bit) != 0
            lines = jnp.where(is_set, partner_rows(lines, 2**bit), lines)
        start = jnp.where(row == column, 1.0, 0.0).astype(jnp.float32)
        state.append((lines, line_of(lines, 0), start))
    for step in range(INNER):
        stride = 2 ** ((LOGB - 1 - step) % LOGB)
        after = []
        for lines, own, turned in state:
            other = partner_columns(own, stride)
            cross = line_of(lines, stride)
            cosine, sine = turn_of(own, other, cross)
            own = cosine * (cosine * own + 2.0 * sine * cross) + sine * sine * other
            cosine, sine = spread(cosine), spread(sine)
            turned = turned * cosine + partner_columns(turned, stride) * sine
            if step + 1 < INNER:
                across = partner_rows(partner_columns(lines, stride), stride)
                lines = lines * cosine + across * sine
                cos_mixed = jnp.take_along_axis(cosine, mixed, axis=1)
                sin_mixed = jnp.take_along_axis(sine, mixed, axis=1)
                lines = lines * cos_mixed + partner_rows(lines, stride) * sin_mixed
            after.append((lines, own, turned))
        state = after
    return [turned.T for _, _, turned in state]


def three_parts(value):
    high = value.astype(jnp.bfloat16)
    rest = value - high.astype(jnp.float32)
    middle = rest.astype(jnp.bfloat16)
    return high, middle, (rest - middle.astype(jnp.float32)).astype(jnp.bfloat16)


def split_store(split_ref, value, start, lane):
    order = split_ref.shape[0] // 3
    rows, lanes = value.shape
    high, middle, low = three_parts(value)
    for place, part in enumerate((middle, high, low)):
        split_ref[pl.ds(place * order + start, rows), pl.ds(lane, lanes)] = part


def gram_of(split_ref):
    order = split_ref.shape[0] // 3
    total = split_ref.shape[1]

    def body(place, acc):
        lanes = pl.ds(pl.multiple_of(place * DEPTH, DEPTH), DEPTH)
        return acc + lax.dot_general(
            split_ref[:, lanes],
            split_ref[: 2 * order, lanes],
            (((1,), (1,)), ((), ())),
            preferred_element_type=jnp.float32,
        )

    acc = lax.fori_loop(0, total // DEPTH, body, jnp.zeros((3 * order, 2 * order), jnp.float32))
    outer = acc[2 * order :, order:]
    inner = acc[:order, order:] + acc[order : 2 * order, :order] + acc[:order, :order]
    return acc[order : 2 * order, order:] + (inner + (outer + outer.T))


def product(turned, split_ref, lanes, terms=6):
    order = split_ref.shape[0] // 3
    rows = turned.shape[0]
    high, middle, low = three_parts(turned)

    def dot(weights, start):
        return lax.dot_general(
            jnp.concatenate([jnp.concatenate(pair, axis=1) for pair in weights], axis=0),
            split_ref[start : start + 2 * order, lanes],
            (((1,), (0,)), ((), ())),
            preferred_element_type=jnp.float32,
        )

    both = dot(((high, high), (middle, middle)), 0)
    if terms == 4:
        return both[:rows] + both[rows:]
    return both[:rows] + (both[rows:] + dot(((low, high),), order))


def spans(length, body):
    whole = length // SPAN * SPAN
    if length <= UNROLLED:
        for lane in range(0, whole, SPAN):
            body(lane, SPAN)
    else:

        def step(place, carry):
            body(pl.multiple_of(place * SPAN, SPAN), SPAN)
            return carry

        lax.fori_loop(0, length // SPAN, step, 0)
    if whole < length:
        body(whole, length - whole)


def load_rows(split_ref, refs, start):
    done = 0
    for ref in refs:

        def body(lane, size):
            split_store(split_ref, ref[:, pl.ds(lane, size)], start, done + lane)

        spans(ref.shape[1], body)
        done += ref.shape[1]


def cuts_of(refs):
    cuts = [0]
    for ref in refs:
        cuts.append(cuts[-1] + ref.shape[1])
    return cuts


def send_out(turned, split_ref, first_refs, second_refs, swap, terms=6):
    half = split_ref.shape[0] // 6
    swapped = jnp.concatenate([turned[half:], turned[:half]], axis=0)
    arranged = jnp.where(swap, swapped, turned)
    first_cuts, second_cuts = cuts_of(first_refs), cuts_of(second_refs)
    cuts = sorted(set(first_cuts + second_cuts))
    for begin, end in zip(cuts[:-1], cuts[1:]):
        first = max(place for place, cut in enumerate(first_cuts) if cut <= begin)
        second = max(place for place, cut in enumerate(second_cuts) if cut <= begin)
        first_lane, second_lane = begin - first_cuts[first], begin - second_cuts[second]

        def body(lane, size):
            lines = product(arranged, split_ref, pl.ds(begin + lane, size), terms)
            first_refs[first][:, pl.ds(first_lane + lane, size)] = lines[:half]
            second_refs[second][:, pl.ds(second_lane + lane, size)] = lines[half:]

        spans(end - begin, body)


def run_of(column, row, row_count, column_count):
    last = jnp.where(row == row_count - 1, row, row_count - 2 - row)
    odd = jnp.where(column == column_count - 1, last, row_count - 1 - row)
    return jnp.where(jnp.bitwise_and(column, 1) == 0, row, odd)


def hosted_slot():
    column, columns = lax.axis_index("col"), lax.axis_size("col")
    run = run_of(column, lax.axis_index("row"), lax.axis_size("row"), columns)
    return run * columns + column


def slot_count():
    return lax.axis_size("row") * lax.axis_size("col")


def prepare_kernel(order, in_ref, *refs):
    count = lax.axis_size("row")
    out_refs, buffer, ready = refs[:-2], refs[-2], refs[-1]
    cycles, rows = in_ref.shape[0], in_ref.shape[1] // count
    copies = [
        pltpu.make_async_copy(in_ref.at[cycle], buffer.at[cycle], ready.at[cycle])
        for cycle in range(cycles)
    ]
    for copy in copies:
        copy.start()
    me = lax.axis_index("row")
    column, columns = lax.axis_index("col"), lax.axis_size("col")
    per_piece = cycles // PIECES
    for cycle, copy in enumerate(copies):
        copy.wait()
        piece, place = divmod(cycle, per_piece)
        for offset in range(count):
            tile = run_of(column, jnp.bitwise_xor(me, offset), count, columns)
            out_ref = out_refs[order.index((offset, piece))]
            out_ref[:, place * rows : (place + 1) * rows] = buffer[
                cycle, pl.ds(tile, rows, stride=count), :
            ].T


def odd_chip(slot):
    return jnp.bitwise_and(slot // 2, 1)


def first_kernel(order, near_count, *refs):
    chunk_refs, out_refs, split_ref = refs[: len(order)], refs[len(order) : -1], refs[-1]
    me, count = lax.axis_index("row"), lax.axis_size("row")
    total = split_ref.shape[1]
    rows = split_ref.shape[0] // 3
    per_piece = total // (PIECES * count * rows)
    for (offset, piece), chunk_ref in zip(order, chunk_refs):
        peer = jnp.bitwise_xor(me, offset)
        for place in range(per_piece):
            lane = ((piece * per_piece + place) * count + peer) * rows
            split_store(
                split_ref,
                chunk_ref[:, place * rows : (place + 1) * rows],
                0,
                pl.multiple_of(lane, rows),
            )
    (turned,) = inner_solve(gram_of(split_ref))
    slot = hosted_slot()
    bottom_first = jnp.logical_or(odd_chip(slot) == 1, slot == 0)
    send_out(turned, split_ref, out_refs[-near_count:], out_refs[:-near_count], bottom_first)


def middle_kernel(near_count, *refs):
    sizes = len(LAST_CUTS) + 1
    near_ref, far_ref = refs[-2:]
    off_outs, on_outs = refs[-2 - 2 * sizes : -2 - sizes], refs[-2 - sizes : -2]
    halves = refs[: -2 - 2 * sizes]
    in_refs, own_refs = halves[: len(halves) // 2], halves[len(halves) // 2 :]
    far_in, near_in = in_refs[:-near_count], in_refs[-near_count:]
    second, first = own_refs[:-near_count], own_refs[-near_count:]
    slot, slots = hosted_slot(), slot_count()
    half = off_outs[0].shape[0]
    odd = odd_chip(slot)
    at_end = jnp.logical_or(slot == 0, slot == slots - 1).astype(jnp.int32)
    near_own = pl.multiple_of(odd * half, half)
    near_other = pl.multiple_of((1 - odd) * half, half)
    far_own = pl.multiple_of(jnp.bitwise_xor(1 - odd, at_end) * half, half)
    far_other = pl.multiple_of(jnp.bitwise_xor(odd, at_end) * half, half)
    load_rows(near_ref, first, near_own)
    load_rows(near_ref, near_in, near_other)
    load_rows(far_ref, second, far_own)
    load_rows(far_ref, far_in, far_other)
    near, far = inner_solve(gram_of(near_ref), gram_of(far_ref))
    near_half = jnp.where(odd == 0, near[half:], near[:half])
    flipped = jnp.logical_or(slot == 1, slot == slots - 1)
    far_bottom = jnp.logical_xor(odd == 1, flipped)
    far_half = jnp.where(far_bottom, far[half:], far[:half])

    def body(lane, size):
        near_lines = product(near_half, near_ref, pl.ds(lane, size))
        far_lines = product(far_half, far_ref, pl.ds(lane, size))
        split_store(near_ref, near_lines, near_other, lane)
        split_store(near_ref, far_lines, near_own, lane)

    spans(near_ref.shape[1], body)
    (turned,) = inner_solve(gram_of(near_ref))
    swap = jnp.logical_and(jnp.bitwise_and(slot, 1) == 0, slot != 0)
    send_out(turned, near_ref, off_outs, on_outs, swap, terms=4)


def last_kernel(*refs):
    out_ref, split_ref, buffer, done = refs[-4:]
    sizes = (len(refs) - 4) // 2
    off_in, on_in = refs[:sizes], refs[sizes:-4]
    half = off_in[0].shape[0]
    odd = jnp.bitwise_and(lax.axis_index("col"), 1)
    load_rows(split_ref, off_in, pl.multiple_of(odd * half, half))
    load_rows(split_ref, on_in, pl.multiple_of((1 - odd) * half, half))
    (turned,) = inner_solve(gram_of(split_ref))
    total = split_ref.shape[1]

    def copy_of(lane):
        rows = pl.ds(lane, SPAN)
        return pltpu.make_async_copy(buffer.at[rows], out_ref.at[rows], done.at[lane // SPAN])

    def body(lane, size):
        lines = product(turned, split_ref, pl.ds(lane, size), terms=4)
        for place in range(0, size, LANES):
            buffer[pl.ds(lane + place, LANES), :] = lines[:, place : place + LANES].T
        copy_of(lane).start()

    spans(total, body)
    spans(total, lambda lane, size: copy_of(lane).wait())


def in_vmem(count):
    return [pl.BlockSpec(memory_space=pltpu.VMEM)] * count


def host_of(slot, row_count, column_count):
    run, column = divmod(slot, column_count)
    row = run
    if column == column_count - 1:
        row = run if run == row_count - 1 else row_count - 2 - run
    elif column % 2:
        row = row_count - 1 - run
    return row * column_count + column


def peer_pairs(offset, first_row, width, row_count, column_count):
    pairs = []
    for row in range(row_count):
        for column in range(column_count):
            peer = (row ^ offset) * column_count + column
            slot = host_of(peer, row_count, column_count)
            if (slot + 1) * width > first_row:
                pairs.append((row * column_count + column, peer))
    return pairs


def swap_pairs(first_row, width, row_count, column_count):
    slots = row_count * column_count
    near_pairs, far_pairs = [], []
    for slot in range(slots):
        if (slot + 1) * width <= first_row:
            continue
        source = host_of(slot, row_count, column_count)
        step = -2 if slot // 2 % 2 else 2
        near_pairs.append((source, host_of(slot + step, row_count, column_count)))
        target = slot - step if 0 <= slot - step < slots else slot ^ 1
        far_pairs.append((source, host_of(target, row_count, column_count)))
    return near_pairs, far_pairs


def last_pairs(first_row, width, row_count, column_count):
    slots = row_count * column_count
    off_pairs, on_pairs = [], []
    for slot in range(slots):
        if (slot + OUTER - 1) * width > first_row:
            target = slot + 1 if slot % 2 else slot - 1
            source = host_of(slot, row_count, column_count)
            off_pairs.append((source, target if 0 <= target < slots else slot))
            on_pairs.append((source, slot ^ 1))
    return off_pairs, on_pairs


def per_device(factor_tiles):
    cycles, rows, tiles, width = factor_tiles.shape
    count, columns = lax.axis_size("row"), lax.axis_size("col")
    half = width // 2
    length = cycles * rows * count
    axes = ("row", "col")
    split_bytes, spare = 6 * width * length, spare_bytes * length
    params = pltpu.CompilerParams(vmem_limit_bytes=split_bytes + spare)
    more_params = pltpu.CompilerParams(vmem_limit_bytes=2 * split_bytes + spare)
    split = pltpu.VMEM((3 * width, length), jnp.bfloat16)

    order = [(peer, part) for peer in range(tiles - 1, -1, -1) for part in range(PIECES - 1, -1, -1)]
    pieces = len(order)
    chunks = pl.pallas_call(
        functools.partial(prepare_kernel, order),
        in_specs=[pl.BlockSpec(memory_space=pltpu.HBM)],
        out_specs=in_vmem(pieces),
        out_shape=[jax.ShapeDtypeStruct((width, cycles * rows // PIECES), jnp.float32)] * pieces,
        scratch_shapes=[
            pltpu.VMEM((cycles, rows * tiles, width), jnp.float32),
            pltpu.SemaphoreType.DMA((cycles,)),
        ],
        compiler_params=params,
        name="prepare",
    )(factor_tiles.reshape(cycles, rows * tiles, width))
    received = list(chunks)
    for place, (offset, piece) in enumerate(order):
        if offset:
            pairs = peer_pairs(offset, piece * (length // PIECES), width, count, columns)
            received[place] = lax.ppermute(chunks[place], axes, pairs)

    unit = length // UNITS
    near_starts = [0] + [cut * unit for cut in NEAR_CUTS]
    far_starts = [0] + [cut * unit for cut in FAR_CUTS]
    near_count = len(near_starts)
    halves = [
        jax.ShapeDtypeStruct((half, end - start), jnp.float32)
        for starts in (far_starts, near_starts)
        for start, end in zip(starts, starts[1:] + [length])
    ]
    moved = pl.pallas_call(
        functools.partial(first_kernel, order, near_count),
        in_specs=in_vmem(pieces),
        out_specs=in_vmem(len(halves)),
        out_shape=halves,
        scratch_shapes=[split],
        compiler_params=params,
        name="first_round",
    )(*received)
    far, near = list(moved[:-near_count]), list(moved[-near_count:])

    def swapped(value, first_row, side):
        return lax.ppermute(value, axes, swap_pairs(first_row, width, count, columns)[side])

    far = [swapped(value, start, 1) for value, start in zip(far, far_starts)]
    near = [swapped(value, start, 0) for value, start in zip(near, near_starts)]
    last_starts = [0] + [cut * unit for cut in LAST_CUTS]
    sizes = len(last_starts)
    last_halves = [
        jax.ShapeDtypeStruct((half, end - start), jnp.float32)
        for start, end in zip(last_starts, last_starts[1:] + [length])
    ]
    last = pl.pallas_call(
        functools.partial(middle_kernel, near_count),
        in_specs=in_vmem(2 * len(halves)),
        out_specs=in_vmem(2 * sizes),
        out_shape=last_halves * 2,
        scratch_shapes=[split] * 2,
        compiler_params=more_params,
        name="middle_rounds",
    )(*far, *near, *moved)
    off, on = list(last[:sizes]), list(last[sizes:])
    for place, start in enumerate(last_starts):
        off_pairs, on_pairs = last_pairs(start, width, count, columns)
        off[place] = lax.ppermute(off[place], axes, off_pairs)
        on[place] = lax.ppermute(on[place], axes, on_pairs)
    return pl.pallas_call(
        last_kernel,
        in_specs=in_vmem(2 * sizes),
        out_specs=pl.BlockSpec(memory_space=pltpu.HBM),
        out_shape=jax.ShapeDtypeStruct((length, width), jnp.float32),
        scratch_shapes=[
            split,
            pltpu.VMEM((length, width), jnp.float32),
            pltpu.SemaphoreType.DMA((length // SPAN,)),
        ],
        compiler_params=params,
        name="last_round",
    )(*off, *on)


def solution(mesh):
    return jax.shard_map(
        per_device,
        mesh=mesh,
        in_specs=(P(None, "row", None, "col"),),
        out_specs=P(None, ("row", "col")),
        check_vma=False,
    )
```

```python
import functools

import jax
import jax.numpy as jnp
from jax import lax
from jax.experimental import pallas as pl
from jax.experimental.pallas import tpu as pltpu
from jax.sharding import PartitionSpec as P

LOGB = 7
OUTER = 4
INNER = 8
LANES = 128
SUBLANES = 8
SPAN = 512
DEPTH = 2048
UNROLLED = 4096
UNITS = 32
NEAR_CUTS = (10, 22)
FAR_CUTS = (16, 24)
LAST_CUTS = (18, 26)
PIECES = 2

damping_ratio = 0.01
spare_bytes = 2048


def partner_columns(value, stride):
    if 2 * stride == value.shape[-1]:
        return pltpu.roll(value, stride, 1)
    column = lax.broadcasted_iota(jnp.int32, value.shape, 1)
    return jnp.take_along_axis(value, jnp.bitwise_xor(column, stride), axis=1)


def partner_rows(value, stride):
    order = value.shape[0]
    if stride >= 8:
        pieces = [value[start : start + stride] for start in range(0, order, stride)]
        return jnp.concatenate([pieces[place ^ 1] for place in range(len(pieces))], axis=0)
    row = lax.broadcasted_iota(jnp.int32, value.shape, 0)
    is_tail = jnp.bitwise_and(row, stride) != 0
    return jnp.where(is_tail, pltpu.roll(value, stride, 0), pltpu.roll(value, order - stride, 0))


def turn_of(own, other, cross):
    gap = own - other
    total = own + other
    base = gap * gap + damping_ratio * total * total
    tangent = jnp.where(base > 0.0, 2.0 * cross * gap / jnp.where(base > 0.0, base, 1.0), 0.0)
    inverse = lax.rsqrt(1.0 + tangent * tangent)
    square = 0.5 + 0.5 * inverse
    root = lax.rsqrt(square)
    return square * root, 0.5 * tangent * inverse * root


def inner_solve(*grams):
    shape = grams[0].shape
    row = lax.broadcasted_iota(jnp.int32, shape, 0)
    column = lax.broadcasted_iota(jnp.int32, shape, 1)
    mixed = jnp.bitwise_xor(row, column)

    def line_of(lines, place):
        return jnp.broadcast_to(lines[place : place + 1], (SUBLANES, shape[1]))

    def spread(line):
        return jnp.broadcast_to(line[None], (shape[0] // SUBLANES, *line.shape)).reshape(shape)

    state = []
    for gram in grams:
        lines = gram
        for bit in range(LOGB):
            is_set = jnp.bitwise_and(column, 2**bit) != 0
            lines = jnp.where(is_set, partner_rows(lines, 2**bit), lines)
        start = jnp.where(row == column, 1.0, 0.0).astype(jnp.float32)
        state.append((lines, line_of(lines, 0), start))
    for step in range(INNER):
        stride = 2 ** ((LOGB - 1 - step) % LOGB)
        after = []
        for lines, own, turned in state:
            other = partner_columns(own, stride)
            cross = line_of(lines, stride)
            cosine, sine = turn_of(own, other, cross)
            own = cosine * (cosine * own + 2.0 * sine * cross) + sine * sine * other
            cosine, sine = spread(cosine), spread(sine)
            turned = turned * cosine + partner_columns(turned, stride) * sine
            if step + 1 < INNER:
                across = partner_rows(partner_columns(lines, stride), stride)
                lines = lines * cosine + across * sine
                cos_mixed = jnp.take_along_axis(cosine, mixed, axis=1)
                sin_mixed = jnp.take_along_axis(sine, mixed, axis=1)
                lines = lines * cos_mixed + partner_rows(lines, stride) * sin_mixed
            after.append((lines, own, turned))
        state = after
    return [turned.T for _, _, turned in state]


def three_parts(value):
    high = value.astype(jnp.bfloat16)
    rest = value - high.astype(jnp.float32)
    middle = rest.astype(jnp.bfloat16)
    return high, middle, (rest - middle.astype(jnp.float32)).astype(jnp.bfloat16)


def split_store(split_ref, value, start, lane):
    order = split_ref.shape[0] // 3
    rows, lanes = value.shape
    high, middle, low = three_parts(value)
    for place, part in enumerate((middle, high, low)):
        split_ref[pl.ds(place * order + start, rows), pl.ds(lane, lanes)] = part


def gram_of(split_ref):
    order = split_ref.shape[0] // 3
    total = split_ref.shape[1]

    def body(place, acc):
        lanes = pl.ds(pl.multiple_of(place * DEPTH, DEPTH), DEPTH)
        return acc + lax.dot_general(
            split_ref[:, lanes],
            split_ref[: 2 * order, lanes],
            (((1,), (1,)), ((), ())),
            preferred_element_type=jnp.float32,
        )

    acc = lax.fori_loop(0, total // DEPTH, body, jnp.zeros((3 * order, 2 * order), jnp.float32))
    outer = acc[2 * order :, order:]
    inner = acc[:order, order:] + acc[order : 2 * order, :order] + acc[:order, :order]
    return acc[order : 2 * order, order:] + (inner + (outer + outer.T))


def product(turned, split_ref, lanes, terms=6):
    order = split_ref.shape[0] // 3
    rows = turned.shape[0]
    high, middle, low = three_parts(turned)

    def dot(weights, start):
        return lax.dot_general(
            jnp.concatenate([jnp.concatenate(pair, axis=1) for pair in weights], axis=0),
            split_ref[start : start + 2 * order, lanes],
            (((1,), (0,)), ((), ())),
            preferred_element_type=jnp.float32,
        )

    both = dot(((high, high), (middle, middle)), 0)
    if terms == 4:
        return both[:rows] + both[rows:]
    return both[:rows] + (both[rows:] + dot(((low, high),), order))


def spans(length, body):
    whole = length // SPAN * SPAN
    if length <= UNROLLED:
        for lane in range(0, whole, SPAN):
            body(lane, SPAN)
    else:

        def step(place, carry):
            body(pl.multiple_of(place * SPAN, SPAN), SPAN)
            return carry

        lax.fori_loop(0, length // SPAN, step, 0)
    if whole < length:
        body(whole, length - whole)


def load_rows(split_ref, refs, start):
    done = 0
    for ref in refs:

        def body(lane, size):
            split_store(split_ref, ref[:, pl.ds(lane, size)], start, done + lane)

        spans(ref.shape[1], body)
        done += ref.shape[1]


def cuts_of(refs):
    cuts = [0]
    for ref in refs:
        cuts.append(cuts[-1] + ref.shape[1])
    return cuts


def send_out(turned, split_ref, first_refs, second_refs, swap, terms=6):
    half = split_ref.shape[0] // 6
    swapped = jnp.concatenate([turned[half:], turned[:half]], axis=0)
    arranged = jnp.where(swap, swapped, turned)
    first_cuts, second_cuts = cuts_of(first_refs), cuts_of(second_refs)
    cuts = sorted(set(first_cuts + second_cuts))
    for begin, end in zip(cuts[:-1], cuts[1:]):
        first = max(place for place, cut in enumerate(first_cuts) if cut <= begin)
        second = max(place for place, cut in enumerate(second_cuts) if cut <= begin)
        first_lane, second_lane = begin - first_cuts[first], begin - second_cuts[second]

        def body(lane, size):
            lines = product(arranged, split_ref, pl.ds(begin + lane, size), terms)
            first_refs[first][:, pl.ds(first_lane + lane, size)] = lines[:half]
            second_refs[second][:, pl.ds(second_lane + lane, size)] = lines[half:]

        spans(end - begin, body)


def run_of(column, row, row_count, column_count):
    last = jnp.where(row == row_count - 1, row, row_count - 2 - row)
    odd = jnp.where(column == column_count - 1, last, row_count - 1 - row)
    return jnp.where(jnp.bitwise_and(column, 1) == 0, row, odd)


def hosted_slot():
    column, columns = lax.axis_index("col"), lax.axis_size("col")
    run = run_of(column, lax.axis_index("row"), lax.axis_size("row"), columns)
    return run * columns + column


def slot_count():
    return lax.axis_size("row") * lax.axis_size("col")


def prepare_kernel(order, in_ref, *refs):
    count = lax.axis_size("row")
    out_refs, buffer, ready = refs[:-2], refs[-2], refs[-1]
    cycles, rows = in_ref.shape[0], in_ref.shape[1] // count
    copies = [
        pltpu.make_async_copy(in_ref.at[cycle], buffer.at[cycle], ready.at[cycle])
        for cycle in range(cycles)
    ]
    for copy in copies:
        copy.start()
    me = lax.axis_index("row")
    column, columns = lax.axis_index("col"), lax.axis_size("col")
    per_piece = cycles // PIECES
    for cycle, copy in enumerate(copies):
        copy.wait()
        piece, place = divmod(cycle, per_piece)
        for offset in range(count):
            tile = run_of(column, jnp.bitwise_xor(me, offset), count, columns)
            out_ref = out_refs[order.index((offset, piece))]
            out_ref[:, place * rows : (place + 1) * rows] = buffer[
                cycle, pl.ds(tile, rows, stride=count), :
            ].T


def odd_chip(slot):
    return jnp.bitwise_and(slot // 2, 1)


def first_kernel(order, near_count, *refs):
    chunk_refs, out_refs, split_ref = refs[: len(order)], refs[len(order) : -1], refs[-1]
    me, count = lax.axis_index("row"), lax.axis_size("row")
    total = split_ref.shape[1]
    rows = split_ref.shape[0] // 3
    per_piece = total // (PIECES * count * rows)
    for (offset, piece), chunk_ref in zip(order, chunk_refs):
        peer = jnp.bitwise_xor(me, offset)
        for place in range(per_piece):
            lane = ((piece * per_piece + place) * count + peer) * rows
            split_store(
                split_ref,
                chunk_ref[:, place * rows : (place + 1) * rows],
                0,
                pl.multiple_of(lane, rows),
            )
    (turned,) = inner_solve(gram_of(split_ref))
    slot = hosted_slot()
    bottom_first = jnp.logical_or(odd_chip(slot) == 1, slot == 0)
    send_out(turned, split_ref, out_refs[-near_count:], out_refs[:-near_count], bottom_first)


def middle_kernel(near_count, *refs):
    sizes = len(LAST_CUTS) + 1
    near_ref, far_ref = refs[-2:]
    off_outs, on_outs = refs[-2 - 2 * sizes : -2 - sizes], refs[-2 - sizes : -2]
    halves = refs[: -2 - 2 * sizes]
    in_refs, own_refs = halves[: len(halves) // 2], halves[len(halves) // 2 :]
    far_in, near_in = in_refs[:-near_count], in_refs[-near_count:]
    second, first = own_refs[:-near_count], own_refs[-near_count:]
    slot, slots = hosted_slot(), slot_count()
    half = off_outs[0].shape[0]
    odd = odd_chip(slot)
    at_end = jnp.logical_or(slot == 0, slot == slots - 1).astype(jnp.int32)
    near_own = pl.multiple_of(odd * half, half)
    near_other = pl.multiple_of((1 - odd) * half, half)
    far_own = pl.multiple_of(jnp.bitwise_xor(1 - odd, at_end) * half, half)
    far_other = pl.multiple_of(jnp.bitwise_xor(odd, at_end) * half, half)
    load_rows(near_ref, first, near_own)
    load_rows(near_ref, near_in, near_other)
    load_rows(far_ref, second, far_own)
    load_rows(far_ref, far_in, far_other)
    near, far = inner_solve(gram_of(near_ref), gram_of(far_ref))
    near_half = jnp.where(odd == 0, near[half:], near[:half])
    flipped = jnp.logical_or(slot == 1, slot == slots - 1)
    far_bottom = jnp.logical_xor(odd == 1, flipped)
    far_half = jnp.where(far_bottom, far[half:], far[:half])

    def body(lane, size):
        near_lines = product(near_half, near_ref, pl.ds(lane, size))
        far_lines = product(far_half, far_ref, pl.ds(lane, size))
        split_store(near_ref, near_lines, near_other, lane)
        split_store(near_ref, far_lines, near_own, lane)

    spans(near_ref.shape[1], body)
    (turned,) = inner_solve(gram_of(near_ref))
    swap = jnp.logical_and(jnp.bitwise_and(slot, 1) == 0, slot != 0)
    send_out(turned, near_ref, off_outs, on_outs, swap, terms=4)


def last_kernel(*refs):
    out_ref, split_ref, buffer, done = refs[-4:]
    sizes = (len(refs) - 4) // 2
    off_in, on_in = refs[:sizes], refs[sizes:-4]
    half = off_in[0].shape[0]
    odd = jnp.bitwise_and(lax.axis_index("col"), 1)
    load_rows(split_ref, off_in, pl.multiple_of(odd * half, half))
    load_rows(split_ref, on_in, pl.multiple_of((1 - odd) * half, half))
    (turned,) = inner_solve(gram_of(split_ref))
    total = split_ref.shape[1]

    def copy_of(lane):
        rows = pl.ds(lane, SPAN)
        return pltpu.make_async_copy(buffer.at[rows], out_ref.at[rows], done.at[lane // SPAN])

    def body(lane, size):
        lines = product(turned, split_ref, pl.ds(lane, size), terms=4)
        for place in range(0, size, LANES):
            buffer[pl.ds(lane + place, LANES), :] = lines[:, place : place + LANES].T
        copy_of(lane).start()

    spans(total, body)
    spans(total, lambda lane, size: copy_of(lane).wait())


def in_vmem(count):
    return [pl.BlockSpec(memory_space=pltpu.VMEM)] * count


def host_of(slot, row_count, column_count):
    run, column = divmod(slot, column_count)
    row = run
    if column == column_count - 1:
        row = run if run == row_count - 1 else row_count - 2 - run
    elif column % 2:
        row = row_count - 1 - run
    return row * column_count + column


def peer_pairs(offset, first_row, width, row_count, column_count):
    pairs = []
    for row in range(row_count):
        for column in range(column_count):
            peer = (row ^ offset) * column_count + column
            slot = host_of(peer, row_count, column_count)
            if (slot + 1) * width > first_row:
                pairs.append((row * column_count + column, peer))
    return pairs


def swap_pairs(first_row, width, row_count, column_count):
    slots = row_count * column_count
    near_pairs, far_pairs = [], []
    for slot in range(slots):
        if (slot + 1) * width <= first_row:
            continue
        source = host_of(slot, row_count, column_count)
        step = -2 if slot // 2 % 2 else 2
        near_pairs.append((source, host_of(slot + step, row_count, column_count)))
        target = slot - step if 0 <= slot - step < slots else slot ^ 1
        far_pairs.append((source, host_of(target, row_count, column_count)))
    return near_pairs, far_pairs


def last_pairs(first_row, width, row_count, column_count):
    slots = row_count * column_count
    off_pairs, on_pairs = [], []
    for slot in range(slots):
        if (slot + OUTER - 1) * width > first_row:
            target = slot + 1 if slot % 2 else slot - 1
            source = host_of(slot, row_count, column_count)
            off_pairs.append((source, target if 0 <= target < slots else slot))
            on_pairs.append((source, slot ^ 1))
    return off_pairs, on_pairs


def per_device(factor_tiles):
    cycles, rows, tiles, width = factor_tiles.shape
    count, columns = lax.axis_size("row"), lax.axis_size("col")
    half = width // 2
    length = cycles * rows * count
    axes = ("row", "col")
    split_bytes, spare = 6 * width * length, spare_bytes * length
    params = pltpu.CompilerParams(vmem_limit_bytes=split_bytes + spare)
    more_params = pltpu.CompilerParams(vmem_limit_bytes=2 * split_bytes + spare)
    split = pltpu.VMEM((3 * width, length), jnp.bfloat16)

    order = [(peer, part) for peer in range(tiles - 1, -1, -1) for part in range(PIECES - 1, -1, -1)]
    pieces = len(order)
    chunks = pl.pallas_call(
        functools.partial(prepare_kernel, order),
        in_specs=[pl.BlockSpec(memory_space=pltpu.HBM)],
        out_specs=in_vmem(pieces),
        out_shape=[jax.ShapeDtypeStruct((width, cycles * rows // PIECES), jnp.float32)] * pieces,
        scratch_shapes=[
            pltpu.VMEM((cycles, rows * tiles, width), jnp.float32),
            pltpu.SemaphoreType.DMA((cycles,)),
        ],
        compiler_params=params,
        name="prepare",
    )(factor_tiles.reshape(cycles, rows * tiles, width))
    received = list(chunks)
    for place, (offset, piece) in enumerate(order):
        if offset:
            pairs = peer_pairs(offset, piece * (length // PIECES), width, count, columns)
            received[place] = lax.ppermute(chunks[place], axes, pairs)

    unit = length // UNITS
    near_starts = [0] + [cut * unit for cut in NEAR_CUTS]
    far_starts = [0] + [cut * unit for cut in FAR_CUTS]
    near_count = len(near_starts)
    halves = [
        jax.ShapeDtypeStruct((half, end - start), jnp.float32)
        for starts in (far_starts, near_starts)
        for start, end in zip(starts, starts[1:] + [length])
    ]
    moved = pl.pallas_call(
        functools.partial(first_kernel, order, near_count),
        in_specs=in_vmem(pieces),
        out_specs=in_vmem(len(halves)),
        out_shape=halves,
        scratch_shapes=[split],
        compiler_params=params,
        name="first_round",
    )(*received)
    far, near = list(moved[:-near_count]), list(moved[-near_count:])

    def swapped(value, first_row, side):
        return lax.ppermute(value, axes, swap_pairs(first_row, width, count, columns)[side])

    far = [swapped(value, start, 1) for value, start in zip(far, far_starts)]
    near = [swapped(value, start, 0) for value, start in zip(near, near_starts)]
    last_starts = [0] + [cut * unit for cut in LAST_CUTS]
    sizes = len(last_starts)
    last_halves = [
        jax.ShapeDtypeStruct((half, end - start), jnp.float32)
        for start, end in zip(last_starts, last_starts[1:] + [length])
    ]
    last = pl.pallas_call(
        functools.partial(middle_kernel, near_count),
        in_specs=in_vmem(2 * len(halves)),
        out_specs=in_vmem(2 * sizes),
        out_shape=last_halves * 2,
        scratch_shapes=[split] * 2,
        compiler_params=more_params,
        name="middle_rounds",
    )(*far, *near, *moved)
    off, on = list(last[:sizes]), list(last[sizes:])
    for place, start in enumerate(last_starts):
        off_pairs, on_pairs = last_pairs(start, width, count, columns)
        off[place] = lax.ppermute(off[place], axes, off_pairs)
        on[place] = lax.ppermute(on[place], axes, on_pairs)
    return pl.pallas_call(
        last_kernel,
        in_specs=in_vmem(2 * sizes),
        out_specs=pl.BlockSpec(memory_space=pltpu.HBM),
        out_shape=jax.ShapeDtypeStruct((length, width), jnp.float32),
        scratch_shapes=[
            split,
            pltpu.VMEM((length, width), jnp.float32),
            pltpu.SemaphoreType.DMA((length // SPAN,)),
        ],
        compiler_params=params,
        name="last_round",
    )(*off, *on)


def solution(mesh):
    return jax.shard_map(
        per_device,
        mesh=mesh,
        in_specs=(P(None, "row", None, "col"),),
        out_specs=P(None, ("row", "col")),
        check_vma=False,
    )
```

```python
import functools

import jax
import jax.numpy as jnp
from jax import lax
from jax.experimental import pallas as pl
from jax.experimental.pallas import tpu as pltpu
from jax.sharding import PartitionSpec as P

LOGB = 7
OUTER = 4
INNER = 8
LANES = 128
SUBLANES = 8
SPAN = 512
DEPTH = 2048
UNROLLED = 4096
UNITS = 32
NEAR_CUTS = (10, 22)
FAR_CUTS = (16, 24)
LAST_CUTS = (18, 26)
PIECES = 2

damping_ratio = 0.01
spare_bytes = 2048


def partner_columns(value, stride):
    if 2 * stride == value.shape[-1]:
        return pltpu.roll(value, stride, 1)
    column = lax.broadcasted_iota(jnp.int32, value.shape, 1)
    return jnp.take_along_axis(value, jnp.bitwise_xor(column, stride), axis=1)


def partner_rows(value, stride):
    order = value.shape[0]
    if stride >= 8:
        pieces = [value[start : start + stride] for start in range(0, order, stride)]
        return jnp.concatenate([pieces[place ^ 1] for place in range(len(pieces))], axis=0)
    row = lax.broadcasted_iota(jnp.int32, value.shape, 0)
    is_tail = jnp.bitwise_and(row, stride) != 0
    return jnp.where(is_tail, pltpu.roll(value, stride, 0), pltpu.roll(value, order - stride, 0))


def turn_of(own, other, cross):
    gap = own - other
    total = own + other
    base = gap * gap + damping_ratio * total * total
    tangent = jnp.where(base > 0.0, 2.0 * cross * gap / jnp.where(base > 0.0, base, 1.0), 0.0)
    inverse = lax.rsqrt(1.0 + tangent * tangent)
    square = 0.5 + 0.5 * inverse
    root = lax.rsqrt(square)
    return square * root, 0.5 * tangent * inverse * root


def inner_solve(*grams):
    shape = grams[0].shape
    row = lax.broadcasted_iota(jnp.int32, shape, 0)
    column = lax.broadcasted_iota(jnp.int32, shape, 1)
    mixed = jnp.bitwise_xor(row, column)

    def line_of(lines, place):
        return jnp.broadcast_to(lines[place : place + 1], (SUBLANES, shape[1]))

    def spread(line):
        return jnp.broadcast_to(line[None], (shape[0] // SUBLANES, *line.shape)).reshape(shape)

    state = []
    for gram in grams:
        lines = gram
        for bit in range(LOGB):
            is_set = jnp.bitwise_and(column, 2**bit) != 0
            lines = jnp.where(is_set, partner_rows(lines, 2**bit), lines)
        start = jnp.where(row == column, 1.0, 0.0).astype(jnp.float32)
        state.append((lines, line_of(lines, 0), start))
    for step in range(INNER):
        stride = 2 ** ((LOGB - 1 - step) % LOGB)
        after = []
        for lines, own, turned in state:
            other = partner_columns(own, stride)
            cross = line_of(lines, stride)
            cosine, sine = turn_of(own, other, cross)
            own = cosine * (cosine * own + 2.0 * sine * cross) + sine * sine * other
            cosine, sine = spread(cosine), spread(sine)
            turned = turned * cosine + partner_columns(turned, stride) * sine
            if step + 1 < INNER:
                across = partner_rows(partner_columns(lines, stride), stride)
                lines = lines * cosine + across * sine
                cos_mixed = jnp.take_along_axis(cosine, mixed, axis=1)
                sin_mixed = jnp.take_along_axis(sine, mixed, axis=1)
                lines = lines * cos_mixed + partner_rows(lines, stride) * sin_mixed
            after.append((lines, own, turned))
        state = after
    return [turned.T for _, _, turned in state]


def three_parts(value):
    high = value.astype(jnp.bfloat16)
    rest = value - high.astype(jnp.float32)
    middle = rest.astype(jnp.bfloat16)
    return high, middle, (rest - middle.astype(jnp.float32)).astype(jnp.bfloat16)


def split_store(split_ref, value, start, lane):
    order = split_ref.shape[0] // 3
    rows, lanes = value.shape
    high, middle, low = three_parts(value)
    for place, part in enumerate((middle, high, low)):
        split_ref[pl.ds(place * order + start, rows), pl.ds(lane, lanes)] = part


def gram_of(split_ref):
    order = split_ref.shape[0] // 3
    total = split_ref.shape[1]

    def body(place, acc):
        lanes = pl.ds(pl.multiple_of(place * DEPTH, DEPTH), DEPTH)
        return acc + lax.dot_general(
            split_ref[:, lanes],
            split_ref[: 2 * order, lanes],
            (((1,), (1,)), ((), ())),
            preferred_element_type=jnp.float32,
        )

    acc = lax.fori_loop(0, total // DEPTH, body, jnp.zeros((3 * order, 2 * order), jnp.float32))
    outer = acc[2 * order :, order:]
    inner = acc[:order, order:] + acc[order : 2 * order, :order] + acc[:order, :order]
    return acc[order : 2 * order, order:] + (inner + (outer + outer.T))


def product(turned, split_ref, lanes, terms=6):
    order = split_ref.shape[0] // 3
    rows = turned.shape[0]
    high, middle, low = three_parts(turned)

    def dot(weights, start):
        return lax.dot_general(
            jnp.concatenate([jnp.concatenate(pair, axis=1) for pair in weights], axis=0),
            split_ref[start : start + 2 * order, lanes],
            (((1,), (0,)), ((), ())),
            preferred_element_type=jnp.float32,
        )

    both = dot(((high, high), (middle, middle)), 0)
    if terms == 4:
        return both[:rows] + both[rows:]
    return both[:rows] + (both[rows:] + dot(((low, high),), order))


def spans(length, body):
    whole = length // SPAN * SPAN
    if length <= UNROLLED:
        for lane in range(0, whole, SPAN):
            body(lane, SPAN)
    else:

        def step(place, carry):
            body(pl.multiple_of(place * SPAN, SPAN), SPAN)
            return carry

        lax.fori_loop(0, length // SPAN, step, 0)
    if whole < length:
        body(whole, length - whole)


def load_rows(split_ref, refs, start):
    done = 0
    for ref in refs:

        def body(lane, size):
            split_store(split_ref, ref[:, pl.ds(lane, size)], start, done + lane)

        spans(ref.shape[1], body)
        done += ref.shape[1]


def cuts_of(refs):
    cuts = [0]
    for ref in refs:
        cuts.append(cuts[-1] + ref.shape[1])
    return cuts


def send_out(turned, split_ref, first_refs, second_refs, swap, terms=6):
    half = split_ref.shape[0] // 6
    swapped = jnp.concatenate([turned[half:], turned[:half]], axis=0)
    arranged = jnp.where(swap, swapped, turned)
    first_cuts, second_cuts = cuts_of(first_refs), cuts_of(second_refs)
    cuts = sorted(set(first_cuts + second_cuts))
    for begin, end in zip(cuts[:-1], cuts[1:]):
        first = max(place for place, cut in enumerate(first_cuts) if cut <= begin)
        second = max(place for place, cut in enumerate(second_cuts) if cut <= begin)
        first_lane, second_lane = begin - first_cuts[first], begin - second_cuts[second]

        def body(lane, size):
            lines = product(arranged, split_ref, pl.ds(begin + lane, size), terms)
            first_refs[first][:, pl.ds(first_lane + lane, size)] = lines[:half]
            second_refs[second][:, pl.ds(second_lane + lane, size)] = lines[half:]

        spans(end - begin, body)


def run_of(column, row, row_count, column_count):
    last = jnp.where(row == row_count - 1, row, row_count - 2 - row)
    odd = jnp.where(column == column_count - 1, last, row_count - 1 - row)
    return jnp.where(jnp.bitwise_and(column, 1) == 0, row, odd)


def hosted_slot():
    column, columns = lax.axis_index("col"), lax.axis_size("col")
    run = run_of(column, lax.axis_index("row"), lax.axis_size("row"), columns)
    return run * columns + column


def slot_count():
    return lax.axis_size("row") * lax.axis_size("col")


def prepare_kernel(order, in_ref, *refs):
    count = lax.axis_size("row")
    out_refs, buffer, ready = refs[:-2], refs[-2], refs[-1]
    cycles, rows = in_ref.shape[0], in_ref.shape[1] // count
    copies = [
        pltpu.make_async_copy(in_ref.at[cycle], buffer.at[cycle], ready.at[cycle])
        for cycle in range(cycles)
    ]
    for copy in copies:
        copy.start()
    me = lax.axis_index("row")
    column, columns = lax.axis_index("col"), lax.axis_size("col")
    per_piece = cycles // PIECES
    for cycle, copy in enumerate(copies):
        copy.wait()
        piece, place = divmod(cycle, per_piece)
        for offset in range(count):
            tile = run_of(column, jnp.bitwise_xor(me, offset), count, columns)
            out_ref = out_refs[order.index((offset, piece))]
            out_ref[:, place * rows : (place + 1) * rows] = buffer[
                cycle, pl.ds(tile, rows, stride=count), :
            ].T


def odd_chip(slot):
    return jnp.bitwise_and(slot // 2, 1)


def first_kernel(order, near_count, *refs):
    chunk_refs, out_refs, split_ref = refs[: len(order)], refs[len(order) : -1], refs[-1]
    me, count = lax.axis_index("row"), lax.axis_size("row")
    total = split_ref.shape[1]
    rows = split_ref.shape[0] // 3
    per_piece = total // (PIECES * count * rows)
    for (offset, piece), chunk_ref in zip(order, chunk_refs):
        peer = jnp.bitwise_xor(me, offset)
        for place in range(per_piece):
            lane = ((piece * per_piece + place) * count + peer) * rows
            split_store(
                split_ref,
                chunk_ref[:, place * rows : (place + 1) * rows],
                0,
                pl.multiple_of(lane, rows),
            )
    (turned,) = inner_solve(gram_of(split_ref))
    slot = hosted_slot()
    bottom_first = jnp.logical_or(odd_chip(slot) == 1, slot == 0)
    send_out(turned, split_ref, out_refs[-near_count:], out_refs[:-near_count], bottom_first)


def middle_kernel(near_count, *refs):
    sizes = len(LAST_CUTS) + 1
    near_ref, far_ref = refs[-2:]
    off_outs, on_outs = refs[-2 - 2 * sizes : -2 - sizes], refs[-2 - sizes : -2]
    halves = refs[: -2 - 2 * sizes]
    in_refs, own_refs = halves[: len(halves) // 2], halves[len(halves) // 2 :]
    far_in, near_in = in_refs[:-near_count], in_refs[-near_count:]
    second, first = own_refs[:-near_count], own_refs[-near_count:]
    slot, slots = hosted_slot(), slot_count()
    half = off_outs[0].shape[0]
    odd = odd_chip(slot)
    at_end = jnp.logical_or(slot == 0, slot == slots - 1).astype(jnp.int32)
    near_own = pl.multiple_of(odd * half, half)
    near_other = pl.multiple_of((1 - odd) * half, half)
    far_own = pl.multiple_of(jnp.bitwise_xor(1 - odd, at_end) * half, half)
    far_other = pl.multiple_of(jnp.bitwise_xor(odd, at_end) * half, half)
    load_rows(near_ref, first, near_own)
    load_rows(near_ref, near_in, near_other)
    load_rows(far_ref, second, far_own)
    load_rows(far_ref, far_in, far_other)
    near, far = inner_solve(gram_of(near_ref), gram_of(far_ref))
    near_half = jnp.where(odd == 0, near[half:], near[:half])
    flipped = jnp.logical_or(slot == 1, slot == slots - 1)
    far_bottom = jnp.logical_xor(odd == 1, flipped)
    far_half = jnp.where(far_bottom, far[half:], far[:half])

    def body(lane, size):
        near_lines = product(near_half, near_ref, pl.ds(lane, size))
        far_lines = product(far_half, far_ref, pl.ds(lane, size))
        split_store(near_ref, near_lines, near_other, lane)
        split_store(near_ref, far_lines, near_own, lane)

    spans(near_ref.shape[1], body)
    (turned,) = inner_solve(gram_of(near_ref))
    swap = jnp.logical_and(jnp.bitwise_and(slot, 1) == 0, slot != 0)
    send_out(turned, near_ref, off_outs, on_outs, swap, terms=4)


def last_kernel(*refs):
    out_ref, split_ref, buffer, done = refs[-4:]
    sizes = (len(refs) - 4) // 2
    off_in, on_in = refs[:sizes], refs[sizes:-4]
    half = off_in[0].shape[0]
    odd = jnp.bitwise_and(lax.axis_index("col"), 1)
    load_rows(split_ref, off_in, pl.multiple_of(odd * half, half))
    load_rows(split_ref, on_in, pl.multiple_of((1 - odd) * half, half))
    (turned,) = inner_solve(gram_of(split_ref))
    total = split_ref.shape[1]

    def copy_of(lane):
        rows = pl.ds(lane, SPAN)
        return pltpu.make_async_copy(buffer.at[rows], out_ref.at[rows], done.at[lane // SPAN])

    def body(lane, size):
        lines = product(turned, split_ref, pl.ds(lane, size), terms=4)
        for place in range(0, size, LANES):
            buffer[pl.ds(lane + place, LANES), :] = lines[:, place : place + LANES].T
        copy_of(lane).start()

    spans(total, body)
    spans(total, lambda lane, size: copy_of(lane).wait())


def in_vmem(count):
    return [pl.BlockSpec(memory_space=pltpu.VMEM)] * count


def host_of(slot, row_count, column_count):
    run, column = divmod(slot, column_count)
    row = run
    if column == column_count - 1:
        row = run if run == row_count - 1 else row_count - 2 - run
    elif column % 2:
        row = row_count - 1 - run
    return row * column_count + column


def peer_pairs(offset, first_row, width, row_count, column_count):
    pairs = []
    for row in range(row_count):
        for column in range(column_count):
            peer = (row ^ offset) * column_count + column
            slot = host_of(peer, row_count, column_count)
            if (slot + 1) * width > first_row:
                pairs.append((row * column_count + column, peer))
    return pairs


def swap_pairs(first_row, width, row_count, column_count):
    slots = row_count * column_count
    near_pairs, far_pairs = [], []
    for slot in range(slots):
        if (slot + 1) * width <= first_row:
            continue
        source = host_of(slot, row_count, column_count)
        step = -2 if slot // 2 % 2 else 2
        near_pairs.append((source, host_of(slot + step, row_count, column_count)))
        target = slot - step if 0 <= slot - step < slots else slot ^ 1
        far_pairs.append((source, host_of(target, row_count, column_count)))
    return near_pairs, far_pairs


def last_pairs(first_row, width, row_count, column_count):
    slots = row_count * column_count
    off_pairs, on_pairs = [], []
    for slot in range(slots):
        if (slot + OUTER - 1) * width > first_row:
            target = slot + 1 if slot % 2 else slot - 1
            source = host_of(slot, row_count, column_count)
            off_pairs.append((source, target if 0 <= target < slots else slot))
            on_pairs.append((source, slot ^ 1))
    return off_pairs, on_pairs


def per_device(factor_tiles):
    cycles, rows, tiles, width = factor_tiles.shape
    count, columns = lax.axis_size("row"), lax.axis_size("col")
    half = width // 2
    length = cycles * rows * count
    axes = ("row", "col")
    split_bytes, spare = 6 * width * length, spare_bytes * length
    params = pltpu.CompilerParams(vmem_limit_bytes=split_bytes + spare)
    more_params = pltpu.CompilerParams(vmem_limit_bytes=2 * split_bytes + spare)
    split = pltpu.VMEM((3 * width, length), jnp.bfloat16)

    peers = sorted(range(tiles), key=lambda peer: (peer != tiles // 2, -peer))
    order = [(peer, part) for peer in peers for part in reversed(range(PIECES))]
    pieces = len(order)
    chunks = pl.pallas_call(
        functools.partial(prepare_kernel, order),
        in_specs=[pl.BlockSpec(memory_space=pltpu.HBM)],
        out_specs=in_vmem(pieces),
        out_shape=[jax.ShapeDtypeStruct((width, cycles * rows // PIECES), jnp.float32)] * pieces,
        scratch_shapes=[
            pltpu.VMEM((cycles, rows * tiles, width), jnp.float32),
            pltpu.SemaphoreType.DMA((cycles,)),
        ],
        compiler_params=params,
        name="prepare",
    )(factor_tiles.reshape(cycles, rows * tiles, width))
    received = list(chunks)
    for place, (offset, piece) in enumerate(order):
        if offset:
            pairs = peer_pairs(offset, piece * (length // PIECES), width, count, columns)
            received[place] = lax.ppermute(chunks[place], axes, pairs)

    unit = length // UNITS
    near_starts = [0] + [cut * unit for cut in NEAR_CUTS]
    far_starts = [0] + [cut * unit for cut in FAR_CUTS]
    near_count = len(near_starts)
    halves = [
        jax.ShapeDtypeStruct((half, end - start), jnp.float32)
        for starts in (far_starts, near_starts)
        for start, end in zip(starts, starts[1:] + [length])
    ]
    moved = pl.pallas_call(
        functools.partial(first_kernel, order, near_count),
        in_specs=in_vmem(pieces),
        out_specs=in_vmem(len(halves)),
        out_shape=halves,
        scratch_shapes=[split],
        compiler_params=params,
        name="first_round",
    )(*received)
    far, near = list(moved[:-near_count]), list(moved[-near_count:])

    def swapped(value, first_row, side):
        return lax.ppermute(value, axes, swap_pairs(first_row, width, count, columns)[side])

    far = [swapped(value, start, 1) for value, start in zip(far, far_starts)]
    near = [swapped(value, start, 0) for value, start in zip(near, near_starts)]
    last_starts = [0] + [cut * unit for cut in LAST_CUTS]
    sizes = len(last_starts)
    last_halves = [
        jax.ShapeDtypeStruct((half, end - start), jnp.float32)
        for start, end in zip(last_starts, last_starts[1:] + [length])
    ]
    last = pl.pallas_call(
        functools.partial(middle_kernel, near_count),
        in_specs=in_vmem(2 * len(halves)),
        out_specs=in_vmem(2 * sizes),
        out_shape=last_halves * 2,
        scratch_shapes=[split] * 2,
        compiler_params=more_params,
        name="middle_rounds",
    )(*far, *near, *moved)
    off, on = list(last[:sizes]), list(last[sizes:])
    for place, start in enumerate(last_starts):
        off_pairs, on_pairs = last_pairs(start, width, count, columns)
        off[place] = lax.ppermute(off[place], axes, off_pairs)
        on[place] = lax.ppermute(on[place], axes, on_pairs)
    return pl.pallas_call(
        last_kernel,
        in_specs=in_vmem(2 * sizes),
        out_specs=pl.BlockSpec(memory_space=pltpu.HBM),
        out_shape=jax.ShapeDtypeStruct((length, width), jnp.float32),
        scratch_shapes=[
            split,
            pltpu.VMEM((length, width), jnp.float32),
            pltpu.SemaphoreType.DMA((length // SPAN,)),
        ],
        compiler_params=params,
        name="last_round",
    )(*off, *on)


def solution(mesh):
    return jax.shard_map(
        per_device,
        mesh=mesh,
        in_specs=(P(None, "row", None, "col"),),
        out_specs=P(None, ("row", "col")),
        check_vma=False,
    )
```

```python
import functools

import jax
import jax.numpy as jnp
from jax import lax
from jax.experimental import pallas as pl
from jax.experimental.pallas import tpu as pltpu
from jax.sharding import PartitionSpec as P

LOGB = 7
OUTER = 4
INNER = 8
LANES = 128
SUBLANES = 8
SPAN = 512
DEPTH = 2048
UNROLLED = 4096
UNITS = 32
NEAR_CUTS = (10, 22)
FAR_CUTS = (16, 24)
LAST_CUTS = (18, 26)
PIECES = 2

damping_ratio = 0.01
spare_bytes = 2048


def partner_columns(value, stride):
    if 2 * stride == value.shape[-1]:
        return pltpu.roll(value, stride, 1)
    column = lax.broadcasted_iota(jnp.int32, value.shape, 1)
    return jnp.take_along_axis(value, jnp.bitwise_xor(column, stride), axis=1)


def partner_rows(value, stride):
    order = value.shape[0]
    if stride >= 8:
        pieces = [value[start : start + stride] for start in range(0, order, stride)]
        return jnp.concatenate([pieces[place ^ 1] for place in range(len(pieces))], axis=0)
    row = lax.broadcasted_iota(jnp.int32, value.shape, 0)
    is_tail = jnp.bitwise_and(row, stride) != 0
    return jnp.where(is_tail, pltpu.roll(value, stride, 0), pltpu.roll(value, order - stride, 0))


def turn_of(own, other, cross):
    gap = own - other
    total = own + other
    base = gap * gap + damping_ratio * total * total
    tangent = jnp.where(base > 0.0, 2.0 * cross * gap / jnp.where(base > 0.0, base, 1.0), 0.0)
    inverse = lax.rsqrt(1.0 + tangent * tangent)
    square = 0.5 + 0.5 * inverse
    root = lax.rsqrt(square)
    return square * root, 0.5 * tangent * inverse * root


def inner_solve(*grams):
    shape = grams[0].shape
    row = lax.broadcasted_iota(jnp.int32, shape, 0)
    column = lax.broadcasted_iota(jnp.int32, shape, 1)
    mixed = jnp.bitwise_xor(row, column)

    def line_of(lines, place):
        return jnp.broadcast_to(lines[place : place + 1], (SUBLANES, shape[1]))

    def spread(line):
        return jnp.broadcast_to(line[None], (shape[0] // SUBLANES, *line.shape)).reshape(shape)

    state = []
    for gram in grams:
        lines = gram
        for bit in range(LOGB):
            is_set = jnp.bitwise_and(column, 2**bit) != 0
            lines = jnp.where(is_set, partner_rows(lines, 2**bit), lines)
        start = jnp.where(row == column, 1.0, 0.0).astype(jnp.float32)
        state.append((lines, line_of(lines, 0), start))
    for step in range(INNER):
        stride = 2 ** ((LOGB - 1 - step) % LOGB)
        after = []
        for lines, own, turned in state:
            other = partner_columns(own, stride)
            cross = line_of(lines, stride)
            cosine, sine = turn_of(own, other, cross)
            own = cosine * (cosine * own + 2.0 * sine * cross) + sine * sine * other
            cosine, sine = spread(cosine), spread(sine)
            turned = turned * cosine + partner_columns(turned, stride) * sine
            if step + 1 < INNER:
                across = partner_rows(partner_columns(lines, stride), stride)
                lines = lines * cosine + across * sine
                cos_mixed = jnp.take_along_axis(cosine, mixed, axis=1)
                sin_mixed = jnp.take_along_axis(sine, mixed, axis=1)
                lines = lines * cos_mixed + partner_rows(lines, stride) * sin_mixed
            after.append((lines, own, turned))
        state = after
    return [turned.T for _, _, turned in state]


def three_parts(value):
    high = value.astype(jnp.bfloat16)
    rest = value - high.astype(jnp.float32)
    middle = rest.astype(jnp.bfloat16)
    return high, middle, (rest - middle.astype(jnp.float32)).astype(jnp.bfloat16)


def split_store(split_ref, value, start, lane):
    order = split_ref.shape[0] // 3
    rows, lanes = value.shape
    high, middle, low = three_parts(value)
    for place, part in enumerate((middle, high, low)):
        split_ref[pl.ds(place * order + start, rows), pl.ds(lane, lanes)] = part


def gram_of(split_ref):
    order = split_ref.shape[0] // 3
    total = split_ref.shape[1]

    def body(place, acc):
        lanes = pl.ds(pl.multiple_of(place * DEPTH, DEPTH), DEPTH)
        return acc + lax.dot_general(
            split_ref[:, lanes],
            split_ref[: 2 * order, lanes],
            (((1,), (1,)), ((), ())),
            preferred_element_type=jnp.float32,
        )

    acc = lax.fori_loop(0, total // DEPTH, body, jnp.zeros((3 * order, 2 * order), jnp.float32))
    outer = acc[2 * order :, order:]
    inner = acc[:order, order:] + acc[order : 2 * order, :order] + acc[:order, :order]
    return acc[order : 2 * order, order:] + (inner + (outer + outer.T))


def product(turned, split_ref, lanes, terms=6):
    order = split_ref.shape[0] // 3
    rows = turned.shape[0]
    high, middle, low = three_parts(turned)

    def dot(weights, start):
        return lax.dot_general(
            jnp.concatenate([jnp.concatenate(pair, axis=1) for pair in weights], axis=0),
            split_ref[start : start + 2 * order, lanes],
            (((1,), (0,)), ((), ())),
            preferred_element_type=jnp.float32,
        )

    both = dot(((high, high), (middle, middle)), 0)
    if terms == 4:
        return both[:rows] + both[rows:]
    return both[:rows] + (both[rows:] + dot(((low, high),), order))


def spans(length, body):
    whole = length // SPAN * SPAN
    if length <= UNROLLED:
        for lane in range(0, whole, SPAN):
            body(lane, SPAN)
    else:

        def step(place, carry):
            body(pl.multiple_of(place * SPAN, SPAN), SPAN)
            return carry

        lax.fori_loop(0, length // SPAN, step, 0)
    if whole < length:
        body(whole, length - whole)


def load_rows(split_ref, refs, start):
    done = 0
    for ref in refs:

        def body(lane, size):
            split_store(split_ref, ref[:, pl.ds(lane, size)], start, done + lane)

        spans(ref.shape[1], body)
        done += ref.shape[1]


def cuts_of(refs):
    cuts = [0]
    for ref in refs:
        cuts.append(cuts[-1] + ref.shape[1])
    return cuts


def send_out(turned, split_ref, first_refs, second_refs, swap, terms=6):
    half = split_ref.shape[0] // 6
    swapped = jnp.concatenate([turned[half:], turned[:half]], axis=0)
    arranged = jnp.where(swap, swapped, turned)
    first_cuts, second_cuts = cuts_of(first_refs), cuts_of(second_refs)
    cuts = sorted(set(first_cuts + second_cuts))
    for begin, end in zip(cuts[:-1], cuts[1:]):
        first = max(place for place, cut in enumerate(first_cuts) if cut <= begin)
        second = max(place for place, cut in enumerate(second_cuts) if cut <= begin)
        first_lane, second_lane = begin - first_cuts[first], begin - second_cuts[second]

        def body(lane, size):
            lines = product(arranged, split_ref, pl.ds(begin + lane, size), terms)
            first_refs[first][:, pl.ds(first_lane + lane, size)] = lines[:half]
            second_refs[second][:, pl.ds(second_lane + lane, size)] = lines[half:]

        spans(end - begin, body)


def run_of(column, row, row_count, column_count):
    last = jnp.where(row == row_count - 1, row, row_count - 2 - row)
    odd = jnp.where(column == column_count - 1, last, row_count - 1 - row)
    return jnp.where(jnp.bitwise_and(column, 1) == 0, row, odd)


def hosted_slot():
    column, columns = lax.axis_index("col"), lax.axis_size("col")
    run = run_of(column, lax.axis_index("row"), lax.axis_size("row"), columns)
    return run * columns + column


def slot_count():
    return lax.axis_size("row") * lax.axis_size("col")


def prepare_kernel(order, in_ref, *refs):
    count = lax.axis_size("row")
    out_refs, buffer, ready = refs[:-2], refs[-2], refs[-1]
    cycles, rows = in_ref.shape[0], in_ref.shape[1] // count
    copies = [
        pltpu.make_async_copy(in_ref.at[cycle], buffer.at[cycle], ready.at[cycle])
        for cycle in range(cycles)
    ]
    for copy in copies:
        copy.start()
    me = lax.axis_index("row")
    column, columns = lax.axis_index("col"), lax.axis_size("col")
    per_piece = cycles // PIECES
    for cycle, copy in enumerate(copies):
        copy.wait()
        piece, place = divmod(cycle, per_piece)
        for offset in range(count):
            tile = run_of(column, jnp.bitwise_xor(me, offset), count, columns)
            out_ref = out_refs[order.index((offset, piece))]
            out_ref[:, place * rows : (place + 1) * rows] = buffer[
                cycle, pl.ds(tile, rows, stride=count), :
            ].T


def odd_chip(slot):
    return jnp.bitwise_and(slot // 2, 1)


def first_kernel(order, near_count, *refs):
    chunk_refs, out_refs, split_ref = refs[: len(order)], refs[len(order) : -1], refs[-1]
    me, count = lax.axis_index("row"), lax.axis_size("row")
    total = split_ref.shape[1]
    rows = split_ref.shape[0] // 3
    per_piece = total // (PIECES * count * rows)
    for (offset, piece), chunk_ref in zip(order, chunk_refs):
        peer = jnp.bitwise_xor(me, offset)
        for place in range(per_piece):
            lane = ((piece * per_piece + place) * count + peer) * rows
            split_store(
                split_ref,
                chunk_ref[:, place * rows : (place + 1) * rows],
                0,
                pl.multiple_of(lane, rows),
            )
    (turned,) = inner_solve(gram_of(split_ref))
    slot = hosted_slot()
    bottom_first = jnp.logical_or(odd_chip(slot) == 1, slot == 0)
    send_out(turned, split_ref, out_refs[-near_count:], out_refs[:-near_count], bottom_first)


def middle_kernel(near_count, *refs):
    sizes = len(LAST_CUTS) + 1
    near_ref, far_ref = refs[-2:]
    off_outs, on_outs = refs[-2 - 2 * sizes : -2 - sizes], refs[-2 - sizes : -2]
    halves = refs[: -2 - 2 * sizes]
    in_refs, own_refs = halves[: len(halves) // 2], halves[len(halves) // 2 :]
    far_in, near_in = in_refs[:-near_count], in_refs[-near_count:]
    second, first = own_refs[:-near_count], own_refs[-near_count:]
    slot, slots = hosted_slot(), slot_count()
    half = off_outs[0].shape[0]
    odd = odd_chip(slot)
    at_end = jnp.logical_or(slot == 0, slot == slots - 1).astype(jnp.int32)
    near_own = pl.multiple_of(odd * half, half)
    near_other = pl.multiple_of((1 - odd) * half, half)
    far_own = pl.multiple_of(jnp.bitwise_xor(1 - odd, at_end) * half, half)
    far_other = pl.multiple_of(jnp.bitwise_xor(odd, at_end) * half, half)
    load_rows(near_ref, first, near_own)
    load_rows(near_ref, near_in, near_other)
    load_rows(far_ref, second, far_own)
    load_rows(far_ref, far_in, far_other)
    near, far = inner_solve(gram_of(near_ref), gram_of(far_ref))
    near_half = jnp.where(odd == 0, near[half:], near[:half])
    flipped = jnp.logical_or(slot == 1, slot == slots - 1)
    far_bottom = jnp.logical_xor(odd == 1, flipped)
    far_half = jnp.where(far_bottom, far[half:], far[:half])

    def body(lane, size):
        near_lines = product(near_half, near_ref, pl.ds(lane, size))
        far_lines = product(far_half, far_ref, pl.ds(lane, size))
        split_store(near_ref, near_lines, near_other, lane)
        split_store(near_ref, far_lines, near_own, lane)

    spans(near_ref.shape[1], body)
    (turned,) = inner_solve(gram_of(near_ref))
    swap = jnp.logical_and(jnp.bitwise_and(slot, 1) == 0, slot != 0)
    send_out(turned, near_ref, off_outs, on_outs, swap, terms=4)


def last_kernel(*refs):
    out_ref, split_ref, buffer, done = refs[-4:]
    sizes = (len(refs) - 4) // 2
    off_in, on_in = refs[:sizes], refs[sizes:-4]
    half = off_in[0].shape[0]
    odd = jnp.bitwise_and(lax.axis_index("col"), 1)
    load_rows(split_ref, off_in, pl.multiple_of(odd * half, half))
    load_rows(split_ref, on_in, pl.multiple_of((1 - odd) * half, half))
    (turned,) = inner_solve(gram_of(split_ref))
    total = split_ref.shape[1]

    def copy_of(lane):
        rows = pl.ds(lane, SPAN)
        return pltpu.make_async_copy(buffer.at[rows], out_ref.at[rows], done.at[lane // SPAN])

    def body(lane, size):
        lines = product(turned, split_ref, pl.ds(lane, size), terms=4)
        for place in range(0, size, LANES):
            buffer[pl.ds(lane + place, LANES), :] = lines[:, place : place + LANES].T
        copy_of(lane).start()

    spans(total, body)
    spans(total, lambda lane, size: copy_of(lane).wait())


def in_vmem(count):
    return [pl.BlockSpec(memory_space=pltpu.VMEM)] * count


def host_of(slot, row_count, column_count):
    run, column = divmod(slot, column_count)
    row = run
    if column == column_count - 1:
        row = run if run == row_count - 1 else row_count - 2 - run
    elif column % 2:
        row = row_count - 1 - run
    return row * column_count + column


def peer_pairs(offset, first_row, width, row_count, column_count):
    pairs = []
    for row in range(row_count):
        for column in range(column_count):
            peer = (row ^ offset) * column_count + column
            slot = host_of(peer, row_count, column_count)
            if (slot + 1) * width > first_row:
                pairs.append((row * column_count + column, peer))
    return pairs


def swap_pairs(first_row, width, row_count, column_count):
    slots = row_count * column_count
    near_pairs, far_pairs = [], []
    for slot in range(slots):
        if (slot + 1) * width <= first_row:
            continue
        source = host_of(slot, row_count, column_count)
        step = -2 if slot // 2 % 2 else 2
        near_pairs.append((source, host_of(slot + step, row_count, column_count)))
        target = slot - step if 0 <= slot - step < slots else slot ^ 1
        far_pairs.append((source, host_of(target, row_count, column_count)))
    return near_pairs, far_pairs


def last_pairs(first_row, width, row_count, column_count):
    slots = row_count * column_count
    off_pairs, on_pairs = [], []
    for slot in range(slots):
        if (slot + OUTER - 1) * width > first_row:
            target = slot + 1 if slot % 2 else slot - 1
            source = host_of(slot, row_count, column_count)
            off_pairs.append((source, target if 0 <= target < slots else slot))
            on_pairs.append((source, slot ^ 1))
    return off_pairs, on_pairs


def per_device(factor_tiles):
    cycles, rows, tiles, width = factor_tiles.shape
    count, columns = lax.axis_size("row"), lax.axis_size("col")
    half = width // 2
    length = cycles * rows * count
    axes = ("row", "col")
    split_bytes, spare = 6 * width * length, spare_bytes * length
    params = pltpu.CompilerParams(vmem_limit_bytes=split_bytes + spare)
    more_params = pltpu.CompilerParams(vmem_limit_bytes=2 * split_bytes + spare)
    split = pltpu.VMEM((3 * width, length), jnp.bfloat16)

    order = [(peer, part) for peer in range(tiles - 1, -1, -1) for part in range(PIECES - 1, -1, -1)]
    pieces = len(order)
    chunks = pl.pallas_call(
        functools.partial(prepare_kernel, order),
        in_specs=[pl.BlockSpec(memory_space=pltpu.HBM)],
        out_specs=in_vmem(pieces),
        out_shape=[jax.ShapeDtypeStruct((width, cycles * rows // PIECES), jnp.float32)] * pieces,
        scratch_shapes=[
            pltpu.VMEM((cycles, rows * tiles, width), jnp.float32),
            pltpu.SemaphoreType.DMA((cycles,)),
        ],
        compiler_params=params,
        name="prepare",
    )(pltpu.with_memory_space_constraint(factor_tiles.reshape(cycles, rows * tiles, width), pltpu.HBM))
    received = list(chunks)
    for place, (offset, piece) in enumerate(order):
        if offset:
            pairs = peer_pairs(offset, piece * (length // PIECES), width, count, columns)
            received[place] = lax.ppermute(chunks[place], axes, pairs)

    unit = length // UNITS
    near_starts = [0] + [cut * unit for cut in NEAR_CUTS]
    far_starts = [0] + [cut * unit for cut in FAR_CUTS]
    near_count = len(near_starts)
    halves = [
        jax.ShapeDtypeStruct((half, end - start), jnp.float32)
        for starts in (far_starts, near_starts)
        for start, end in zip(starts, starts[1:] + [length])
    ]
    moved = pl.pallas_call(
        functools.partial(first_kernel, order, near_count),
        in_specs=in_vmem(pieces),
        out_specs=in_vmem(len(halves)),
        out_shape=halves,
        scratch_shapes=[split],
        compiler_params=params,
        name="first_round",
    )(*received)
    far, near = list(moved[:-near_count]), list(moved[-near_count:])

    def swapped(value, first_row, side):
        return lax.ppermute(value, axes, swap_pairs(first_row, width, count, columns)[side])

    far = [swapped(value, start, 1) for value, start in zip(far, far_starts)]
    near = [swapped(value, start, 0) for value, start in zip(near, near_starts)]
    last_starts = [0] + [cut * unit for cut in LAST_CUTS]
    sizes = len(last_starts)
    last_halves = [
        jax.ShapeDtypeStruct((half, end - start), jnp.float32)
        for start, end in zip(last_starts, last_starts[1:] + [length])
    ]
    last = pl.pallas_call(
        functools.partial(middle_kernel, near_count),
        in_specs=in_vmem(2 * len(halves)),
        out_specs=in_vmem(2 * sizes),
        out_shape=last_halves * 2,
        scratch_shapes=[split] * 2,
        compiler_params=more_params,
        name="middle_rounds",
    )(*far, *near, *moved)
    off, on = list(last[:sizes]), list(last[sizes:])
    for place, start in enumerate(last_starts):
        off_pairs, on_pairs = last_pairs(start, width, count, columns)
        off[place] = lax.ppermute(off[place], axes, off_pairs)
        on[place] = lax.ppermute(on[place], axes, on_pairs)
    return pl.pallas_call(
        last_kernel,
        in_specs=in_vmem(2 * sizes),
        out_specs=pl.BlockSpec(memory_space=pltpu.HBM),
        out_shape=jax.ShapeDtypeStruct((length, width), jnp.float32),
        scratch_shapes=[
            split,
            pltpu.VMEM((length, width), jnp.float32),
            pltpu.SemaphoreType.DMA((length // SPAN,)),
        ],
        compiler_params=params,
        name="last_round",
    )(*off, *on)


def solution(mesh):
    return jax.shard_map(
        per_device,
        mesh=mesh,
        in_specs=(P(None, "row", None, "col"),),
        out_specs=P(None, ("row", "col")),
        check_vma=False,
    )
```

```python
import functools

import jax
import jax.numpy as jnp
from jax import lax
from jax.experimental import pallas as pl
from jax.experimental.pallas import tpu as pltpu
from jax.sharding import PartitionSpec as P

LOGB = 7
OUTER = 4
INNER = 8
LANES = 128
SUBLANES = 8
SPAN = 512
DEPTH = 2048
UNROLLED = 4096
UNITS = 32
NEAR_CUTS = (10, 20)
FAR_CUTS = (14, 18, 24)
LAST_CUTS = (18, 26)
PIECES = 2

damping_ratio = 0.01
spare_bytes = 2048


def partner_columns(value, stride):
    if 2 * stride == value.shape[-1]:
        return pltpu.roll(value, stride, 1)
    column = lax.broadcasted_iota(jnp.int32, value.shape, 1)
    return jnp.take_along_axis(value, jnp.bitwise_xor(column, stride), axis=1)


def partner_rows(value, stride):
    order = value.shape[0]
    if stride >= 8:
        pieces = [value[start : start + stride] for start in range(0, order, stride)]
        return jnp.concatenate([pieces[place ^ 1] for place in range(len(pieces))], axis=0)
    row = lax.broadcasted_iota(jnp.int32, value.shape, 0)
    is_tail = jnp.bitwise_and(row, stride) != 0
    return jnp.where(is_tail, pltpu.roll(value, stride, 0), pltpu.roll(value, order - stride, 0))


def turn_of(own, other, cross):
    gap = own - other
    total = own + other
    base = gap * gap + damping_ratio * total * total
    tangent = jnp.where(base > 0.0, 2.0 * cross * gap / jnp.where(base > 0.0, base, 1.0), 0.0)
    inverse = lax.rsqrt(1.0 + tangent * tangent)
    square = 0.5 + 0.5 * inverse
    root = lax.rsqrt(square)
    return square * root, 0.5 * tangent * inverse * root


def inner_solve(*grams):
    shape = grams[0].shape
    row = lax.broadcasted_iota(jnp.int32, shape, 0)
    column = lax.broadcasted_iota(jnp.int32, shape, 1)
    mixed = jnp.bitwise_xor(row, column)

    def line_of(lines, place):
        return jnp.broadcast_to(lines[place : place + 1], (SUBLANES, shape[1]))

    def spread(line):
        return jnp.broadcast_to(line[None], (shape[0] // SUBLANES, *line.shape)).reshape(shape)

    state = []
    for gram in grams:
        lines = gram
        for bit in range(LOGB):
            is_set = jnp.bitwise_and(column, 2**bit) != 0
            lines = jnp.where(is_set, partner_rows(lines, 2**bit), lines)
        start = jnp.where(row == column, 1.0, 0.0).astype(jnp.float32)
        state.append((lines, line_of(lines, 0), start))
    for step in range(INNER):
        stride = 2 ** ((LOGB - 1 - step) % LOGB)
        after = []
        for lines, own, turned in state:
            other = partner_columns(own, stride)
            cross = line_of(lines, stride)
            cosine, sine = turn_of(own, other, cross)
            own = cosine * (cosine * own + 2.0 * sine * cross) + sine * sine * other
            cosine, sine = spread(cosine), spread(sine)
            turned = turned * cosine + partner_columns(turned, stride) * sine
            if step + 1 < INNER:
                across = partner_rows(partner_columns(lines, stride), stride)
                lines = lines * cosine + across * sine
                cos_mixed = jnp.take_along_axis(cosine, mixed, axis=1)
                sin_mixed = jnp.take_along_axis(sine, mixed, axis=1)
                lines = lines * cos_mixed + partner_rows(lines, stride) * sin_mixed
            after.append((lines, own, turned))
        state = after
    return [turned.T for _, _, turned in state]


def three_parts(value):
    high = value.astype(jnp.bfloat16)
    rest = value - high.astype(jnp.float32)
    middle = rest.astype(jnp.bfloat16)
    return high, middle, (rest - middle.astype(jnp.float32)).astype(jnp.bfloat16)


def split_store(split_ref, value, start, lane):
    order = split_ref.shape[0] // 3
    rows, lanes = value.shape
    high, middle, low = three_parts(value)
    for place, part in enumerate((middle, high, low)):
        split_ref[pl.ds(place * order + start, rows), pl.ds(lane, lanes)] = part


def gram_of(split_ref):
    order = split_ref.shape[0] // 3
    total = split_ref.shape[1]

    def body(place, acc):
        lanes = pl.ds(pl.multiple_of(place * DEPTH, DEPTH), DEPTH)
        return acc + lax.dot_general(
            split_ref[:, lanes],
            split_ref[: 2 * order, lanes],
            (((1,), (1,)), ((), ())),
            preferred_element_type=jnp.float32,
        )

    acc = lax.fori_loop(0, total // DEPTH, body, jnp.zeros((3 * order, 2 * order), jnp.float32))
    outer = acc[2 * order :, order:]
    inner = acc[:order, order:] + acc[order : 2 * order, :order] + acc[:order, :order]
    return acc[order : 2 * order, order:] + (inner + (outer + outer.T))


def product(turned, split_ref, lanes, terms=6):
    order = split_ref.shape[0] // 3
    rows = turned.shape[0]
    high, middle, low = three_parts(turned)

    def dot(weights, start):
        return lax.dot_general(
            jnp.concatenate([jnp.concatenate(pair, axis=1) for pair in weights], axis=0),
            split_ref[start : start + 2 * order, lanes],
            (((1,), (0,)), ((), ())),
            preferred_element_type=jnp.float32,
        )

    both = dot(((high, high), (middle, middle)), 0)
    if terms == 4:
        return both[:rows] + both[rows:]
    return both[:rows] + (both[rows:] + dot(((low, high),), order))


def spans(length, body):
    whole = length // SPAN * SPAN
    if length <= UNROLLED:
        for lane in range(0, whole, SPAN):
            body(lane, SPAN)
    else:

        def step(place, carry):
            body(pl.multiple_of(place * SPAN, SPAN), SPAN)
            return carry

        lax.fori_loop(0, length // SPAN, step, 0)
    if whole < length:
        body(whole, length - whole)


def load_rows(split_ref, refs, start):
    done = 0
    for ref in refs:

        def body(lane, size):
            split_store(split_ref, ref[:, pl.ds(lane, size)], start, done + lane)

        spans(ref.shape[1], body)
        done += ref.shape[1]


def cuts_of(refs):
    cuts = [0]
    for ref in refs:
        cuts.append(cuts[-1] + ref.shape[1])
    return cuts


def send_out(turned, split_ref, first_refs, second_refs, swap, terms=6):
    half = split_ref.shape[0] // 6
    swapped = jnp.concatenate([turned[half:], turned[:half]], axis=0)
    arranged = jnp.where(swap, swapped, turned)
    first_cuts, second_cuts = cuts_of(first_refs), cuts_of(second_refs)
    cuts = sorted(set(first_cuts + second_cuts))
    for begin, end in zip(cuts[:-1], cuts[1:]):
        first = max(place for place, cut in enumerate(first_cuts) if cut <= begin)
        second = max(place for place, cut in enumerate(second_cuts) if cut <= begin)
        first_lane, second_lane = begin - first_cuts[first], begin - second_cuts[second]

        def body(lane, size):
            lines = product(arranged, split_ref, pl.ds(begin + lane, size), terms)
            first_refs[first][:, pl.ds(first_lane + lane, size)] = lines[:half]
            second_refs[second][:, pl.ds(second_lane + lane, size)] = lines[half:]

        spans(end - begin, body)


def run_of(column, row, row_count, column_count):
    last = jnp.where(row == row_count - 1, row, row_count - 2 - row)
    odd = jnp.where(column == column_count - 1, last, row_count - 1 - row)
    return jnp.where(jnp.bitwise_and(column, 1) == 0, row, odd)


def hosted_slot():
    column, columns = lax.axis_index("col"), lax.axis_size("col")
    run = run_of(column, lax.axis_index("row"), lax.axis_size("row"), columns)
    return run * columns + column


def slot_count():
    return lax.axis_size("row") * lax.axis_size("col")


def prepare_kernel(order, in_ref, *refs):
    count = lax.axis_size("row")
    out_refs, buffer, ready = refs[:-2], refs[-2], refs[-1]
    cycles, rows = in_ref.shape[0], in_ref.shape[1] // count
    copies = [
        pltpu.make_async_copy(in_ref.at[cycle], buffer.at[cycle], ready.at[cycle])
        for cycle in range(cycles)
    ]
    for copy in copies:
        copy.start()
    me = lax.axis_index("row")
    column, columns = lax.axis_index("col"), lax.axis_size("col")
    per_piece = cycles // PIECES
    for cycle, copy in enumerate(copies):
        copy.wait()
        piece, place = divmod(cycle, per_piece)
        for offset in range(count):
            tile = run_of(column, jnp.bitwise_xor(me, offset), count, columns)
            out_ref = out_refs[order.index((offset, piece))]
            out_ref[:, place * rows : (place + 1) * rows] = buffer[
                cycle, pl.ds(tile, rows, stride=count), :
            ].T


def odd_chip(slot):
    return jnp.bitwise_and(slot // 2, 1)


def first_kernel(order, near_count, *refs):
    chunk_refs, out_refs, split_ref = refs[: len(order)], refs[len(order) : -1], refs[-1]
    me, count = lax.axis_index("row"), lax.axis_size("row")
    total = split_ref.shape[1]
    rows = split_ref.shape[0] // 3
    per_piece = total // (PIECES * count * rows)
    for (offset, piece), chunk_ref in zip(order, chunk_refs):
        peer = jnp.bitwise_xor(me, offset)
        for place in range(per_piece):
            lane = ((piece * per_piece + place) * count + peer) * rows
            split_store(
                split_ref,
                chunk_ref[:, place * rows : (place + 1) * rows],
                0,
                pl.multiple_of(lane, rows),
            )
    (turned,) = inner_solve(gram_of(split_ref))
    slot = hosted_slot()
    bottom_first = jnp.logical_or(odd_chip(slot) == 1, slot == 0)
    send_out(turned, split_ref, out_refs[-near_count:], out_refs[:-near_count], bottom_first)


def middle_kernel(near_count, *refs):
    sizes = len(LAST_CUTS) + 1
    near_ref, far_ref = refs[-2:]
    off_outs, on_outs = refs[-2 - 2 * sizes : -2 - sizes], refs[-2 - sizes : -2]
    halves = refs[: -2 - 2 * sizes]
    in_refs, own_refs = halves[: len(halves) // 2], halves[len(halves) // 2 :]
    far_in, near_in = in_refs[:-near_count], in_refs[-near_count:]
    second, first = own_refs[:-near_count], own_refs[-near_count:]
    slot, slots = hosted_slot(), slot_count()
    half = off_outs[0].shape[0]
    odd = odd_chip(slot)
    at_end = jnp.logical_or(slot == 0, slot == slots - 1).astype(jnp.int32)
    near_own = pl.multiple_of(odd * half, half)
    near_other = pl.multiple_of((1 - odd) * half, half)
    far_own = pl.multiple_of(jnp.bitwise_xor(1 - odd, at_end) * half, half)
    far_other = pl.multiple_of(jnp.bitwise_xor(odd, at_end) * half, half)
    load_rows(near_ref, first, near_own)
    load_rows(near_ref, near_in, near_other)
    load_rows(far_ref, second, far_own)
    load_rows(far_ref, far_in, far_other)
    near, far = inner_solve(gram_of(near_ref), gram_of(far_ref))
    near_half = jnp.where(odd == 0, near[half:], near[:half])
    flipped = jnp.logical_or(slot == 1, slot == slots - 1)
    far_bottom = jnp.logical_xor(odd == 1, flipped)
    far_half = jnp.where(far_bottom, far[half:], far[:half])

    def body(lane, size):
        near_lines = product(near_half, near_ref, pl.ds(lane, size))
        far_lines = product(far_half, far_ref, pl.ds(lane, size))
        split_store(near_ref, near_lines, near_other, lane)
        split_store(near_ref, far_lines, near_own, lane)

    spans(near_ref.shape[1], body)
    (turned,) = inner_solve(gram_of(near_ref))
    swap = jnp.logical_and(jnp.bitwise_and(slot, 1) == 0, slot != 0)
    send_out(turned, near_ref, off_outs, on_outs, swap, terms=4)


def last_kernel(*refs):
    out_ref, split_ref, buffer, done = refs[-4:]
    sizes = (len(refs) - 4) // 2
    off_in, on_in = refs[:sizes], refs[sizes:-4]
    half = off_in[0].shape[0]
    odd = jnp.bitwise_and(lax.axis_index("col"), 1)
    load_rows(split_ref, off_in, pl.multiple_of(odd * half, half))
    load_rows(split_ref, on_in, pl.multiple_of((1 - odd) * half, half))
    (turned,) = inner_solve(gram_of(split_ref))
    total = split_ref.shape[1]

    def copy_of(lane):
        rows = pl.ds(lane, SPAN)
        return pltpu.make_async_copy(buffer.at[rows], out_ref.at[rows], done.at[lane // SPAN])

    def body(lane, size):
        lines = product(turned, split_ref, pl.ds(lane, size), terms=4)
        for place in range(0, size, LANES):
            buffer[pl.ds(lane + place, LANES), :] = lines[:, place : place + LANES].T
        copy_of(lane).start()

    spans(total, body)
    spans(total, lambda lane, size: copy_of(lane).wait())


def in_vmem(count):
    return [pl.BlockSpec(memory_space=pltpu.VMEM)] * count


def host_of(slot, row_count, column_count):
    run, column = divmod(slot, column_count)
    row = run
    if column == column_count - 1:
        row = run if run == row_count - 1 else row_count - 2 - run
    elif column % 2:
        row = row_count - 1 - run
    return row * column_count + column


def peer_pairs(offset, first_row, width, row_count, column_count):
    pairs = []
    for row in range(row_count):
        for column in range(column_count):
            peer = (row ^ offset) * column_count + column
            slot = host_of(peer, row_count, column_count)
            if (slot + 1) * width > first_row:
                pairs.append((row * column_count + column, peer))
    return pairs


def swap_pairs(first_row, width, row_count, column_count):
    slots = row_count * column_count
    near_pairs, far_pairs = [], []
    for slot in range(slots):
        if (slot + 1) * width <= first_row:
            continue
        source = host_of(slot, row_count, column_count)
        step = -2 if slot // 2 % 2 else 2
        near_pairs.append((source, host_of(slot + step, row_count, column_count)))
        target = slot - step if 0 <= slot - step < slots else slot ^ 1
        far_pairs.append((source, host_of(target, row_count, column_count)))
    return near_pairs, far_pairs


def last_pairs(first_row, width, row_count, column_count):
    slots = row_count * column_count
    off_pairs, on_pairs = [], []
    for slot in range(slots):
        if (slot + OUTER - 1) * width > first_row:
            target = slot + 1 if slot % 2 else slot - 1
            source = host_of(slot, row_count, column_count)
            off_pairs.append((source, target if 0 <= target < slots else slot))
            on_pairs.append((source, slot ^ 1))
    return off_pairs, on_pairs


def per_device(factor_tiles):
    cycles, rows, tiles, width = factor_tiles.shape
    count, columns = lax.axis_size("row"), lax.axis_size("col")
    half = width // 2
    length = cycles * rows * count
    axes = ("row", "col")
    split_bytes, spare = 6 * width * length, spare_bytes * length
    params = pltpu.CompilerParams(vmem_limit_bytes=split_bytes + spare)
    more_params = pltpu.CompilerParams(vmem_limit_bytes=2 * split_bytes + spare)
    split = pltpu.VMEM((3 * width, length), jnp.bfloat16)

    order = [(peer, part) for peer in range(tiles - 1, -1, -1) for part in range(PIECES - 1, -1, -1)]
    pieces = len(order)
    chunks = pl.pallas_call(
        functools.partial(prepare_kernel, order),
        in_specs=[pl.BlockSpec(memory_space=pltpu.HBM)],
        out_specs=in_vmem(pieces),
        out_shape=[jax.ShapeDtypeStruct((width, cycles * rows // PIECES), jnp.float32)] * pieces,
        scratch_shapes=[
            pltpu.VMEM((cycles, rows * tiles, width), jnp.float32),
            pltpu.SemaphoreType.DMA((cycles,)),
        ],
        compiler_params=params,
        name="prepare",
    )(pltpu.with_memory_space_constraint(factor_tiles.reshape(cycles, rows * tiles, width), pltpu.HBM))
    received = list(chunks)
    for place, (offset, piece) in enumerate(order):
        if offset:
            pairs = peer_pairs(offset, piece * (length // PIECES), width, count, columns)
            received[place] = lax.ppermute(chunks[place], axes, pairs)

    unit = length // UNITS
    near_starts = [0] + [cut * unit for cut in NEAR_CUTS]
    far_starts = [0] + [cut * unit for cut in FAR_CUTS]
    near_count = len(near_starts)
    halves = [
        jax.ShapeDtypeStruct((half, end - start), jnp.float32)
        for starts in (far_starts, near_starts)
        for start, end in zip(starts, starts[1:] + [length])
    ]
    moved = pl.pallas_call(
        functools.partial(first_kernel, order, near_count),
        in_specs=in_vmem(pieces),
        out_specs=in_vmem(len(halves)),
        out_shape=halves,
        scratch_shapes=[split],
        compiler_params=params,
        name="first_round",
    )(*received)
    far, near = list(moved[:-near_count]), list(moved[-near_count:])

    def swapped(value, first_row, side):
        return lax.ppermute(value, axes, swap_pairs(first_row, width, count, columns)[side])

    far = [swapped(value, start, 1) for value, start in zip(far, far_starts)]
    near = [swapped(value, start, 0) for value, start in zip(near, near_starts)]
    last_starts = [0] + [cut * unit for cut in LAST_CUTS]
    sizes = len(last_starts)
    last_halves = [
        jax.ShapeDtypeStruct((half, end - start), jnp.float32)
        for start, end in zip(last_starts, last_starts[1:] + [length])
    ]
    last = pl.pallas_call(
        functools.partial(middle_kernel, near_count),
        in_specs=in_vmem(2 * len(halves)),
        out_specs=in_vmem(2 * sizes),
        out_shape=last_halves * 2,
        scratch_shapes=[split] * 2,
        compiler_params=more_params,
        name="middle_rounds",
    )(*far, *near, *moved)
    off, on = list(last[:sizes]), list(last[sizes:])
    for place, start in enumerate(last_starts):
        off_pairs, on_pairs = last_pairs(start, width, count, columns)
        off[place] = lax.ppermute(off[place], axes, off_pairs)
        on[place] = lax.ppermute(on[place], axes, on_pairs)
    return pl.pallas_call(
        last_kernel,
        in_specs=in_vmem(2 * sizes),
        out_specs=pl.BlockSpec(memory_space=pltpu.HBM),
        out_shape=jax.ShapeDtypeStruct((length, width), jnp.float32),
        scratch_shapes=[
            split,
            pltpu.VMEM((length, width), jnp.float32),
            pltpu.SemaphoreType.DMA((length // SPAN,)),
        ],
        compiler_params=params,
        name="last_round",
    )(*off, *on)


def solution(mesh):
    return jax.shard_map(
        per_device,
        mesh=mesh,
        in_specs=(P(None, "row", None, "col"),),
        out_specs=P(None, ("row", "col")),
        check_vma=False,
    )
```

```python
import functools

import jax
import jax.numpy as jnp
from jax import lax
from jax.experimental import pallas as pl
from jax.experimental.pallas import tpu as pltpu
from jax.sharding import PartitionSpec as P

LOGB = 7
OUTER = 4
INNER = 8
LANES = 128
SUBLANES = 8
SPAN = 512
UNROLLED = 4096
UNITS = 32
NEAR_CUTS = (10, 22)
FAR_CUTS = (16, 24)
LAST_CUTS = (18, 26)
PIECES = 2

damping_ratio = 0.01
spare_bytes = 2048


def partner_columns(value, stride):
    if 2 * stride == value.shape[-1]:
        return pltpu.roll(value, stride, 1)
    column = lax.broadcasted_iota(jnp.int32, value.shape, 1)
    return jnp.take_along_axis(value, jnp.bitwise_xor(column, stride), axis=1)


def partner_rows(value, stride):
    order = value.shape[0]
    if stride >= 8:
        pieces = [value[start : start + stride] for start in range(0, order, stride)]
        return jnp.concatenate([pieces[place ^ 1] for place in range(len(pieces))], axis=0)
    row = lax.broadcasted_iota(jnp.int32, value.shape, 0)
    is_tail = jnp.bitwise_and(row, stride) != 0
    return jnp.where(is_tail, pltpu.roll(value, stride, 0), pltpu.roll(value, order - stride, 0))


def turn_of(own, other, cross):
    gap = own - other
    total = own + other
    base = gap * gap + damping_ratio * total * total
    tangent = jnp.where(base > 0.0, 2.0 * cross * gap / jnp.where(base > 0.0, base, 1.0), 0.0)
    inverse = lax.rsqrt(1.0 + tangent * tangent)
    square = 0.5 + 0.5 * inverse
    root = lax.rsqrt(square)
    return square * root, 0.5 * tangent * inverse * root


def inner_solve(*grams):
    shape = grams[0].shape
    row = lax.broadcasted_iota(jnp.int32, shape, 0)
    column = lax.broadcasted_iota(jnp.int32, shape, 1)
    mixed = jnp.bitwise_xor(row, column)

    def line_of(lines, place):
        return jnp.broadcast_to(lines[place : place + 1], (SUBLANES, shape[1]))

    def spread(line):
        return jnp.broadcast_to(line[None], (shape[0] // SUBLANES, *line.shape)).reshape(shape)

    state = []
    for gram in grams:
        lines = gram
        for bit in range(LOGB):
            is_set = jnp.bitwise_and(column, 2**bit) != 0
            lines = jnp.where(is_set, partner_rows(lines, 2**bit), lines)
        start = jnp.where(row == column, 1.0, 0.0).astype(jnp.float32)
        state.append((lines, line_of(lines, 0), start))
    for step in range(INNER):
        stride = 2 ** ((LOGB - 1 - step) % LOGB)
        after = []
        for lines, own, turned in state:
            other = partner_columns(own, stride)
            cross = line_of(lines, stride)
            cosine, sine = turn_of(own, other, cross)
            own = cosine * (cosine * own + 2.0 * sine * cross) + sine * sine * other
            cosine, sine = spread(cosine), spread(sine)
            turned = turned * cosine + partner_columns(turned, stride) * sine
            if step + 1 < INNER:
                across = partner_rows(partner_columns(lines, stride), stride)
                lines = lines * cosine + across * sine
                cos_mixed = jnp.take_along_axis(cosine, mixed, axis=1)
                sin_mixed = jnp.take_along_axis(sine, mixed, axis=1)
                lines = lines * cos_mixed + partner_rows(lines, stride) * sin_mixed
            after.append((lines, own, turned))
        state = after
    return [turned.T for _, _, turned in state]


def three_parts(value):
    high = value.astype(jnp.bfloat16)
    rest = value - high.astype(jnp.float32)
    middle = rest.astype(jnp.bfloat16)
    return high, middle, (rest - middle.astype(jnp.float32)).astype(jnp.bfloat16)


def split_store(split_ref, value, start, lane):
    order = split_ref.shape[0] // 3
    rows, lanes = value.shape
    high, middle, low = three_parts(value)
    for place, part in enumerate((middle, high, low)):
        split_ref[pl.ds(place * order + start, rows), pl.ds(lane, lanes)] = part


def gram_of(split_ref):
    order = split_ref.shape[0] // 3
    total = split_ref.shape[1]

    def dot(lanes):
        return lax.dot_general(
            split_ref[:, lanes],
            split_ref[: 2 * order, lanes],
            (((1,), (1,)), ((), ())),
            preferred_element_type=jnp.float32,
        )

    if total <= UNROLLED:
        acc = dot(pl.ds(0, total))
    else:
        acc = lax.fori_loop(
            0,
            total // UNROLLED,
            lambda place, acc: acc + dot(pl.ds(pl.multiple_of(place * UNROLLED, UNROLLED), UNROLLED)),
            jnp.zeros((3 * order, 2 * order), jnp.float32),
        )
    outer = acc[2 * order :, order:]
    inner = acc[:order, order:] + acc[order : 2 * order, :order] + acc[:order, :order]
    return acc[order : 2 * order, order:] + (inner + (outer + outer.T))


def product(turned, split_ref, lanes, terms=6):
    order = split_ref.shape[0] // 3
    rows = turned.shape[0]
    high, middle, low = three_parts(turned)

    def dot(weights, start):
        return lax.dot_general(
            jnp.concatenate([jnp.concatenate(pair, axis=1) for pair in weights], axis=0),
            split_ref[start : start + 2 * order, lanes],
            (((1,), (0,)), ((), ())),
            preferred_element_type=jnp.float32,
        )

    both = dot(((high, high), (middle, middle)), 0)
    if terms == 4:
        return both[:rows] + both[rows:]
    return both[:rows] + (both[rows:] + dot(((low, high),), order))


def spans(length, body):
    whole = length // SPAN * SPAN
    if length <= UNROLLED:
        for lane in range(0, whole, SPAN):
            body(lane, SPAN)
    else:

        def step(place, carry):
            body(pl.multiple_of(place * SPAN, SPAN), SPAN)
            return carry

        lax.fori_loop(0, length // SPAN, step, 0)
    if whole < length:
        body(whole, length - whole)


def load_rows(split_ref, refs, start):
    done = 0
    for ref in refs:

        def body(lane, size):
            split_store(split_ref, ref[:, pl.ds(lane, size)], start, done + lane)

        spans(ref.shape[1], body)
        done += ref.shape[1]


def cuts_of(refs):
    cuts = [0]
    for ref in refs:
        cuts.append(cuts[-1] + ref.shape[1])
    return cuts


def send_out(turned, split_ref, first_refs, second_refs, swap, terms=6):
    half = split_ref.shape[0] // 6
    swapped = jnp.concatenate([turned[half:], turned[:half]], axis=0)
    arranged = jnp.where(swap, swapped, turned)
    first_cuts, second_cuts = cuts_of(first_refs), cuts_of(second_refs)
    cuts = sorted(set(first_cuts + second_cuts))
    for begin, end in zip(cuts[:-1], cuts[1:]):
        first = max(place for place, cut in enumerate(first_cuts) if cut <= begin)
        second = max(place for place, cut in enumerate(second_cuts) if cut <= begin)
        first_lane, second_lane = begin - first_cuts[first], begin - second_cuts[second]

        def body(lane, size):
            lines = product(arranged, split_ref, pl.ds(begin + lane, size), terms)
            first_refs[first][:, pl.ds(first_lane + lane, size)] = lines[:half]
            second_refs[second][:, pl.ds(second_lane + lane, size)] = lines[half:]

        spans(end - begin, body)


def run_of(column, row, row_count, column_count):
    last = jnp.where(row == row_count - 1, row, row_count - 2 - row)
    odd = jnp.where(column == column_count - 1, last, row_count - 1 - row)
    return jnp.where(jnp.bitwise_and(column, 1) == 0, row, odd)


def hosted_slot():
    column, columns = lax.axis_index("col"), lax.axis_size("col")
    run = run_of(column, lax.axis_index("row"), lax.axis_size("row"), columns)
    return run * columns + column


def slot_count():
    return lax.axis_size("row") * lax.axis_size("col")


def prepare_kernel(order, in_ref, *refs):
    count = lax.axis_size("row")
    out_refs, buffer, ready = refs[:-2], refs[-2], refs[-1]
    cycles, rows = in_ref.shape[0], in_ref.shape[1] // count
    copies = [
        pltpu.make_async_copy(in_ref.at[cycle], buffer.at[cycle], ready.at[cycle])
        for cycle in range(cycles)
    ]
    for copy in copies:
        copy.start()
    me = lax.axis_index("row")
    column, columns = lax.axis_index("col"), lax.axis_size("col")
    per_piece = cycles // PIECES
    for cycle, copy in enumerate(copies):
        copy.wait()
        piece, place = divmod(cycle, per_piece)
        for offset in range(count):
            tile = run_of(column, jnp.bitwise_xor(me, offset), count, columns)
            out_ref = out_refs[order.index((offset, piece))]
            out_ref[:, place * rows : (place + 1) * rows] = buffer[
                cycle, pl.ds(tile, rows, stride=count), :
            ].T


def odd_chip(slot):
    return jnp.bitwise_and(slot // 2, 1)


def first_kernel(order, near_count, *refs):
    chunk_refs, out_refs, split_ref = refs[: len(order)], refs[len(order) : -1], refs[-1]
    me, count = lax.axis_index("row"), lax.axis_size("row")
    total = split_ref.shape[1]
    rows = split_ref.shape[0] // 3
    per_piece = total // (PIECES * count * rows)
    for (offset, piece), chunk_ref in zip(order, chunk_refs):
        peer = jnp.bitwise_xor(me, offset)
        for place in range(per_piece):
            lane = ((piece * per_piece + place) * count + peer) * rows
            split_store(
                split_ref,
                chunk_ref[:, place * rows : (place + 1) * rows],
                0,
                pl.multiple_of(lane, rows),
            )
    (turned,) = inner_solve(gram_of(split_ref))
    slot = hosted_slot()
    bottom_first = jnp.logical_or(odd_chip(slot) == 1, slot == 0)
    send_out(turned, split_ref, out_refs[-near_count:], out_refs[:-near_count], bottom_first)


def middle_kernel(near_count, *refs):
    sizes = len(LAST_CUTS) + 1
    near_ref, far_ref = refs[-2:]
    off_outs, on_outs = refs[-2 - 2 * sizes : -2 - sizes], refs[-2 - sizes : -2]
    halves = refs[: -2 - 2 * sizes]
    in_refs, own_refs = halves[: len(halves) // 2], halves[len(halves) // 2 :]
    far_in, near_in = in_refs[:-near_count], in_refs[-near_count:]
    second, first = own_refs[:-near_count], own_refs[-near_count:]
    slot, slots = hosted_slot(), slot_count()
    half = off_outs[0].shape[0]
    odd = odd_chip(slot)
    at_end = jnp.logical_or(slot == 0, slot == slots - 1).astype(jnp.int32)
    near_own = pl.multiple_of(odd * half, half)
    near_other = pl.multiple_of((1 - odd) * half, half)
    far_own = pl.multiple_of(jnp.bitwise_xor(1 - odd, at_end) * half, half)
    far_other = pl.multiple_of(jnp.bitwise_xor(odd, at_end) * half, half)
    load_rows(near_ref, first, near_own)
    load_rows(near_ref, near_in, near_other)
    load_rows(far_ref, second, far_own)
    load_rows(far_ref, far_in, far_other)
    near, far = inner_solve(gram_of(near_ref), gram_of(far_ref))
    near_half = jnp.where(odd == 0, near[half:], near[:half])
    flipped = jnp.logical_or(slot == 1, slot == slots - 1)
    far_bottom = jnp.logical_xor(odd == 1, flipped)
    far_half = jnp.where(far_bottom, far[half:], far[:half])

    def body(lane, size):
        near_lines = product(near_half, near_ref, pl.ds(lane, size))
        far_lines = product(far_half, far_ref, pl.ds(lane, size))
        split_store(near_ref, near_lines, near_other, lane)
        split_store(near_ref, far_lines, near_own, lane)

    spans(near_ref.shape[1], body)
    (turned,) = inner_solve(gram_of(near_ref))
    swap = jnp.logical_and(jnp.bitwise_and(slot, 1) == 0, slot != 0)
    send_out(turned, near_ref, off_outs, on_outs, swap, terms=4)


def last_kernel(*refs):
    out_ref, split_ref, buffer, done = refs[-4:]
    sizes = (len(refs) - 4) // 2
    off_in, on_in = refs[:sizes], refs[sizes:-4]
    half = off_in[0].shape[0]
    odd = jnp.bitwise_and(lax.axis_index("col"), 1)
    load_rows(split_ref, off_in, pl.multiple_of(odd * half, half))
    load_rows(split_ref, on_in, pl.multiple_of((1 - odd) * half, half))
    (turned,) = inner_solve(gram_of(split_ref))
    total = split_ref.shape[1]

    def copy_of(lane):
        rows = pl.ds(lane, SPAN)
        return pltpu.make_async_copy(buffer.at[rows], out_ref.at[rows], done.at[lane // SPAN])

    def body(lane, size):
        lines = product(turned, split_ref, pl.ds(lane, size), terms=4)
        for place in range(0, size, LANES):
            buffer[pl.ds(lane + place, LANES), :] = lines[:, place : place + LANES].T
        copy_of(lane).start()

    spans(total, body)
    spans(total, lambda lane, size: copy_of(lane).wait())


def in_vmem(count):
    return [pl.BlockSpec(memory_space=pltpu.VMEM)] * count


def host_of(slot, row_count, column_count):
    run, column = divmod(slot, column_count)
    row = run
    if column == column_count - 1:
        row = run if run == row_count - 1 else row_count - 2 - run
    elif column % 2:
        row = row_count - 1 - run
    return row * column_count + column


def peer_pairs(offset, first_row, width, row_count, column_count):
    pairs = []
    for row in range(row_count):
        for column in range(column_count):
            peer = (row ^ offset) * column_count + column
            slot = host_of(peer, row_count, column_count)
            if (slot + 1) * width > first_row:
                pairs.append((row * column_count + column, peer))
    return pairs


def swap_pairs(first_row, width, row_count, column_count):
    slots = row_count * column_count
    near_pairs, far_pairs = [], []
    for slot in range(slots):
        if (slot + 1) * width <= first_row:
            continue
        source = host_of(slot, row_count, column_count)
        step = -2 if slot // 2 % 2 else 2
        near_pairs.append((source, host_of(slot + step, row_count, column_count)))
        target = slot - step if 0 <= slot - step < slots else slot ^ 1
        far_pairs.append((source, host_of(target, row_count, column_count)))
    return near_pairs, far_pairs


def last_pairs(first_row, width, row_count, column_count):
    slots = row_count * column_count
    off_pairs, on_pairs = [], []
    for slot in range(slots):
        if (slot + OUTER - 1) * width > first_row:
            target = slot + 1 if slot % 2 else slot - 1
            source = host_of(slot, row_count, column_count)
            off_pairs.append((source, target if 0 <= target < slots else slot))
            on_pairs.append((source, slot ^ 1))
    return off_pairs, on_pairs


def per_device(factor_tiles):
    cycles, rows, tiles, width = factor_tiles.shape
    count, columns = lax.axis_size("row"), lax.axis_size("col")
    half = width // 2
    length = cycles * rows * count
    axes = ("row", "col")
    split_bytes, spare = 6 * width * length, spare_bytes * length
    params = pltpu.CompilerParams(vmem_limit_bytes=split_bytes + spare)
    more_params = pltpu.CompilerParams(vmem_limit_bytes=2 * split_bytes + spare)
    split = pltpu.VMEM((3 * width, length), jnp.bfloat16)

    order = [(peer, part) for peer in range(tiles - 1, -1, -1) for part in range(PIECES - 1, -1, -1)]
    pieces = len(order)
    chunks = pl.pallas_call(
        functools.partial(prepare_kernel, order),
        in_specs=[pl.BlockSpec(memory_space=pltpu.HBM)],
        out_specs=in_vmem(pieces),
        out_shape=[jax.ShapeDtypeStruct((width, cycles * rows // PIECES), jnp.float32)] * pieces,
        scratch_shapes=[
            pltpu.VMEM((cycles, rows * tiles, width), jnp.float32),
            pltpu.SemaphoreType.DMA((cycles,)),
        ],
        compiler_params=params,
        name="prepare",
    )(pltpu.with_memory_space_constraint(factor_tiles.reshape(cycles, rows * tiles, width), pltpu.HBM))
    received = list(chunks)
    for place, (offset, piece) in enumerate(order):
        if offset:
            pairs = peer_pairs(offset, piece * (length // PIECES), width, count, columns)
            received[place] = lax.ppermute(chunks[place], axes, pairs)

    unit = length // UNITS
    near_starts = [0] + [cut * unit for cut in NEAR_CUTS]
    far_starts = [0] + [cut * unit for cut in FAR_CUTS]
    near_count = len(near_starts)
    halves = [
        jax.ShapeDtypeStruct((half, end - start), jnp.float32)
        for starts in (far_starts, near_starts)
        for start, end in zip(starts, starts[1:] + [length])
    ]
    moved = pl.pallas_call(
        functools.partial(first_kernel, order, near_count),
        in_specs=in_vmem(pieces),
        out_specs=in_vmem(len(halves)),
        out_shape=halves,
        scratch_shapes=[split],
        compiler_params=params,
        name="first_round",
    )(*received)
    far, near = list(moved[:-near_count]), list(moved[-near_count:])

    def swapped(value, first_row, side):
        return lax.ppermute(value, axes, swap_pairs(first_row, width, count, columns)[side])

    far = [swapped(value, start, 1) for value, start in zip(far, far_starts)]
    near = [swapped(value, start, 0) for value, start in zip(near, near_starts)]
    last_starts = [0] + [cut * unit for cut in LAST_CUTS]
    sizes = len(last_starts)
    last_halves = [
        jax.ShapeDtypeStruct((half, end - start), jnp.float32)
        for start, end in zip(last_starts, last_starts[1:] + [length])
    ]
    last = pl.pallas_call(
        functools.partial(middle_kernel, near_count),
        in_specs=in_vmem(2 * len(halves)),
        out_specs=in_vmem(2 * sizes),
        out_shape=last_halves * 2,
        scratch_shapes=[split] * 2,
        compiler_params=more_params,
        name="middle_rounds",
    )(*far, *near, *moved)
    off, on = list(last[:sizes]), list(last[sizes:])
    for place, start in enumerate(last_starts):
        off_pairs, on_pairs = last_pairs(start, width, count, columns)
        off[place] = lax.ppermute(off[place], axes, off_pairs)
        on[place] = lax.ppermute(on[place], axes, on_pairs)
    return pl.pallas_call(
        last_kernel,
        in_specs=in_vmem(2 * sizes),
        out_specs=pl.BlockSpec(memory_space=pltpu.HBM),
        out_shape=jax.ShapeDtypeStruct((length, width), jnp.float32),
        scratch_shapes=[
            split,
            pltpu.VMEM((length, width), jnp.float32),
            pltpu.SemaphoreType.DMA((length // SPAN,)),
        ],
        compiler_params=params,
        name="last_round",
    )(*off, *on)


def solution(mesh):
    return jax.shard_map(
        per_device,
        mesh=mesh,
        in_specs=(P(None, "row", None, "col"),),
        out_specs=P(None, ("row", "col")),
        check_vma=False,
    )
```

```python
import functools

import jax
import jax.numpy as jnp
from jax import lax
from jax.experimental import pallas as pl
from jax.experimental.pallas import tpu as pltpu
from jax.sharding import PartitionSpec as P

LOGB = 7
OUTER = 4
INNER = 8
LANES = 128
SUBLANES = 8
SPAN = 512
DEPTH = 1024
UNROLLED = 4096
UNITS = 32
NEAR_CUTS = (10, 22)
FAR_CUTS = (16, 24)
LAST_CUTS = (18, 26)
PIECES = 2

damping_ratio = 0.01
spare_bytes = 2048


def partner_columns(value, stride):
    if 2 * stride == value.shape[-1]:
        return pltpu.roll(value, stride, 1)
    column = lax.broadcasted_iota(jnp.int32, value.shape, 1)
    return jnp.take_along_axis(value, jnp.bitwise_xor(column, stride), axis=1)


def partner_rows(value, stride):
    order = value.shape[0]
    if stride >= 8:
        pieces = [value[start : start + stride] for start in range(0, order, stride)]
        return jnp.concatenate([pieces[place ^ 1] for place in range(len(pieces))], axis=0)
    row = lax.broadcasted_iota(jnp.int32, value.shape, 0)
    is_tail = jnp.bitwise_and(row, stride) != 0
    return jnp.where(is_tail, pltpu.roll(value, stride, 0), pltpu.roll(value, order - stride, 0))


def turn_of(own, other, cross):
    gap = own - other
    total = own + other
    base = gap * gap + damping_ratio * total * total
    tangent = jnp.where(base > 0.0, 2.0 * cross * gap / jnp.where(base > 0.0, base, 1.0), 0.0)
    inverse = lax.rsqrt(1.0 + tangent * tangent)
    square = 0.5 + 0.5 * inverse
    root = lax.rsqrt(square)
    return square * root, 0.5 * tangent * inverse * root


def inner_solve(*grams):
    shape = grams[0].shape
    row = lax.broadcasted_iota(jnp.int32, shape, 0)
    column = lax.broadcasted_iota(jnp.int32, shape, 1)
    mixed = jnp.bitwise_xor(row, column)

    def line_of(lines, place):
        return jnp.broadcast_to(lines[place : place + 1], (SUBLANES, shape[1]))

    def spread(line):
        return jnp.broadcast_to(line[None], (shape[0] // SUBLANES, *line.shape)).reshape(shape)

    state = []
    for gram in grams:
        lines = gram
        for bit in range(LOGB):
            is_set = jnp.bitwise_and(column, 2**bit) != 0
            lines = jnp.where(is_set, partner_rows(lines, 2**bit), lines)
        start = jnp.where(row == column, 1.0, 0.0).astype(jnp.float32)
        state.append((lines, line_of(lines, 0), start))
    for step in range(INNER):
        stride = 2 ** ((LOGB - 1 - step) % LOGB)
        after = []
        for lines, own, turned in state:
            other = partner_columns(own, stride)
            cross = line_of(lines, stride)
            cosine, sine = turn_of(own, other, cross)
            own = cosine * (cosine * own + 2.0 * sine * cross) + sine * sine * other
            cosine, sine = spread(cosine), spread(sine)
            turned = turned * cosine + partner_columns(turned, stride) * sine
            if step + 1 < INNER:
                across = partner_rows(partner_columns(lines, stride), stride)
                lines = lines * cosine + across * sine
                cos_mixed = jnp.take_along_axis(cosine, mixed, axis=1)
                sin_mixed = jnp.take_along_axis(sine, mixed, axis=1)
                lines = lines * cos_mixed + partner_rows(lines, stride) * sin_mixed
            after.append((lines, own, turned))
        state = after
    return [turned.T for _, _, turned in state]


def three_parts(value):
    high = value.astype(jnp.bfloat16)
    rest = value - high.astype(jnp.float32)
    middle = rest.astype(jnp.bfloat16)
    return high, middle, (rest - middle.astype(jnp.float32)).astype(jnp.bfloat16)


def split_store(split_ref, value, start, lane):
    order = split_ref.shape[0] // 3
    rows, lanes = value.shape
    high, middle, low = three_parts(value)
    for place, part in enumerate((middle, high, low)):
        split_ref[pl.ds(place * order + start, rows), pl.ds(lane, lanes)] = part


def gram_of(split_ref):
    order = split_ref.shape[0] // 3
    total = split_ref.shape[1]

    def body(place, acc):
        lanes = pl.ds(pl.multiple_of(place * DEPTH, DEPTH), DEPTH)
        return acc + lax.dot_general(
            split_ref[:, lanes],
            split_ref[: 2 * order, lanes],
            (((1,), (1,)), ((), ())),
            preferred_element_type=jnp.float32,
        )

    acc = lax.fori_loop(0, total // DEPTH, body, jnp.zeros((3 * order, 2 * order), jnp.float32))
    outer = acc[2 * order :, order:]
    inner = acc[:order, order:] + acc[order : 2 * order, :order] + acc[:order, :order]
    return acc[order : 2 * order, order:] + (inner + (outer + outer.T))


def product(turned, split_ref, lanes, terms=6):
    order = split_ref.shape[0] // 3
    rows = turned.shape[0]
    high, middle, low = three_parts(turned)

    def dot(weights, start):
        return lax.dot_general(
            jnp.concatenate([jnp.concatenate(pair, axis=1) for pair in weights], axis=0),
            split_ref[start : start + 2 * order, lanes],
            (((1,), (0,)), ((), ())),
            preferred_element_type=jnp.float32,
        )

    both = dot(((high, high), (middle, middle)), 0)
    if terms == 4:
        return both[:rows] + both[rows:]
    return both[:rows] + (both[rows:] + dot(((low, high),), order))


def spans(length, body):
    whole = length // SPAN * SPAN
    if length <= UNROLLED:
        for lane in range(0, whole, SPAN):
            body(lane, SPAN)
    else:

        def step(place, carry):
            body(pl.multiple_of(place * SPAN, SPAN), SPAN)
            return carry

        lax.fori_loop(0, length // SPAN, step, 0)
    if whole < length:
        body(whole, length - whole)


def load_rows(split_ref, refs, start):
    done = 0
    for ref in refs:

        def body(lane, size):
            split_store(split_ref, ref[:, pl.ds(lane, size)], start, done + lane)

        spans(ref.shape[1], body)
        done += ref.shape[1]


def cuts_of(refs):
    cuts = [0]
    for ref in refs:
        cuts.append(cuts[-1] + ref.shape[1])
    return cuts


def send_out(turned, split_ref, first_refs, second_refs, swap, terms=6):
    half = split_ref.shape[0] // 6
    swapped = jnp.concatenate([turned[half:], turned[:half]], axis=0)
    arranged = jnp.where(swap, swapped, turned)
    first_cuts, second_cuts = cuts_of(first_refs), cuts_of(second_refs)
    cuts = sorted(set(first_cuts + second_cuts))
    for begin, end in zip(cuts[:-1], cuts[1:]):
        first = max(place for place, cut in enumerate(first_cuts) if cut <= begin)
        second = max(place for place, cut in enumerate(second_cuts) if cut <= begin)
        first_lane, second_lane = begin - first_cuts[first], begin - second_cuts[second]

        def body(lane, size):
            lines = product(arranged, split_ref, pl.ds(begin + lane, size), terms)
            first_refs[first][:, pl.ds(first_lane + lane, size)] = lines[:half]
            second_refs[second][:, pl.ds(second_lane + lane, size)] = lines[half:]

        spans(end - begin, body)


def run_of(column, row, row_count, column_count):
    last = jnp.where(row == row_count - 1, row, row_count - 2 - row)
    odd = jnp.where(column == column_count - 1, last, row_count - 1 - row)
    return jnp.where(jnp.bitwise_and(column, 1) == 0, row, odd)


def hosted_slot():
    column, columns = lax.axis_index("col"), lax.axis_size("col")
    run = run_of(column, lax.axis_index("row"), lax.axis_size("row"), columns)
    return run * columns + column


def slot_count():
    return lax.axis_size("row") * lax.axis_size("col")


def prepare_kernel(order, in_ref, *refs):
    count = lax.axis_size("row")
    out_refs, buffer, ready = refs[:-2], refs[-2], refs[-1]
    cycles, rows = in_ref.shape[0], in_ref.shape[1] // count
    copies = [
        pltpu.make_async_copy(in_ref.at[cycle], buffer.at[cycle], ready.at[cycle])
        for cycle in range(cycles)
    ]
    for copy in copies:
        copy.start()
    me = lax.axis_index("row")
    column, columns = lax.axis_index("col"), lax.axis_size("col")
    per_piece = cycles // PIECES
    for cycle, copy in enumerate(copies):
        copy.wait()
        piece, place = divmod(cycle, per_piece)
        for offset in range(count):
            tile = run_of(column, jnp.bitwise_xor(me, offset), count, columns)
            out_ref = out_refs[order.index((offset, piece))]
            out_ref[:, place * rows : (place + 1) * rows] = buffer[
                cycle, pl.ds(tile, rows, stride=count), :
            ].T


def odd_chip(slot):
    return jnp.bitwise_and(slot // 2, 1)


def first_kernel(order, near_count, *refs):
    chunk_refs, out_refs, split_ref = refs[: len(order)], refs[len(order) : -1], refs[-1]
    me, count = lax.axis_index("row"), lax.axis_size("row")
    total = split_ref.shape[1]
    rows = split_ref.shape[0] // 3
    per_piece = total // (PIECES * count * rows)
    for (offset, piece), chunk_ref in zip(order, chunk_refs):
        peer = jnp.bitwise_xor(me, offset)
        for place in range(per_piece):
            lane = ((piece * per_piece + place) * count + peer) * rows
            split_store(
                split_ref,
                chunk_ref[:, place * rows : (place + 1) * rows],
                0,
                pl.multiple_of(lane, rows),
            )
    (turned,) = inner_solve(gram_of(split_ref))
    slot = hosted_slot()
    bottom_first = jnp.logical_or(odd_chip(slot) == 1, slot == 0)
    send_out(turned, split_ref, out_refs[-near_count:], out_refs[:-near_count], bottom_first)


def middle_kernel(near_count, *refs):
    sizes = len(LAST_CUTS) + 1
    near_ref, far_ref = refs[-2:]
    off_outs, on_outs = refs[-2 - 2 * sizes : -2 - sizes], refs[-2 - sizes : -2]
    halves = refs[: -2 - 2 * sizes]
    in_refs, own_refs = halves[: len(halves) // 2], halves[len(halves) // 2 :]
    far_in, near_in = in_refs[:-near_count], in_refs[-near_count:]
    second, first = own_refs[:-near_count], own_refs[-near_count:]
    slot, slots = hosted_slot(), slot_count()
    half = off_outs[0].shape[0]
    odd = odd_chip(slot)
    at_end = jnp.logical_or(slot == 0, slot == slots - 1).astype(jnp.int32)
    near_own = pl.multiple_of(odd * half, half)
    near_other = pl.multiple_of((1 - odd) * half, half)
    far_own = pl.multiple_of(jnp.bitwise_xor(1 - odd, at_end) * half, half)
    far_other = pl.multiple_of(jnp.bitwise_xor(odd, at_end) * half, half)
    load_rows(near_ref, first, near_own)
    load_rows(near_ref, near_in, near_other)
    load_rows(far_ref, second, far_own)
    load_rows(far_ref, far_in, far_other)
    near, far = inner_solve(gram_of(near_ref), gram_of(far_ref))
    near_half = jnp.where(odd == 0, near[half:], near[:half])
    flipped = jnp.logical_or(slot == 1, slot == slots - 1)
    far_bottom = jnp.logical_xor(odd == 1, flipped)
    far_half = jnp.where(far_bottom, far[half:], far[:half])

    def body(lane, size):
        near_lines = product(near_half, near_ref, pl.ds(lane, size))
        far_lines = product(far_half, far_ref, pl.ds(lane, size))
        split_store(near_ref, near_lines, near_other, lane)
        split_store(near_ref, far_lines, near_own, lane)

    spans(near_ref.shape[1], body)
    (turned,) = inner_solve(gram_of(near_ref))
    swap = jnp.logical_and(jnp.bitwise_and(slot, 1) == 0, slot != 0)
    send_out(turned, near_ref, off_outs, on_outs, swap, terms=4)


def last_kernel(*refs):
    out_ref, split_ref, buffer, done = refs[-4:]
    sizes = (len(refs) - 4) // 2
    off_in, on_in = refs[:sizes], refs[sizes:-4]
    half = off_in[0].shape[0]
    odd = jnp.bitwise_and(lax.axis_index("col"), 1)
    load_rows(split_ref, off_in, pl.multiple_of(odd * half, half))
    load_rows(split_ref, on_in, pl.multiple_of((1 - odd) * half, half))
    (turned,) = inner_solve(gram_of(split_ref))
    total = split_ref.shape[1]

    def copy_of(lane):
        rows = pl.ds(lane, SPAN)
        return pltpu.make_async_copy(buffer.at[rows], out_ref.at[rows], done.at[lane // SPAN])

    def body(lane, size):
        lines = product(turned, split_ref, pl.ds(lane, size), terms=4)
        for place in range(0, size, LANES):
            buffer[pl.ds(lane + place, LANES), :] = lines[:, place : place + LANES].T
        copy_of(lane).start()

    spans(total, body)
    spans(total, lambda lane, size: copy_of(lane).wait())


def in_vmem(count):
    return [pl.BlockSpec(memory_space=pltpu.VMEM)] * count


def host_of(slot, row_count, column_count):
    run, column = divmod(slot, column_count)
    row = run
    if column == column_count - 1:
        row = run if run == row_count - 1 else row_count - 2 - run
    elif column % 2:
        row = row_count - 1 - run
    return row * column_count + column


def peer_pairs(offset, first_row, width, row_count, column_count):
    pairs = []
    for row in range(row_count):
        for column in range(column_count):
            peer = (row ^ offset) * column_count + column
            slot = host_of(peer, row_count, column_count)
            if (slot + 1) * width > first_row:
                pairs.append((row * column_count + column, peer))
    return pairs


def swap_pairs(first_row, width, row_count, column_count):
    slots = row_count * column_count
    near_pairs, far_pairs = [], []
    for slot in range(slots):
        if (slot + 1) * width <= first_row:
            continue
        source = host_of(slot, row_count, column_count)
        step = -2 if slot // 2 % 2 else 2
        near_pairs.append((source, host_of(slot + step, row_count, column_count)))
        target = slot - step if 0 <= slot - step < slots else slot ^ 1
        far_pairs.append((source, host_of(target, row_count, column_count)))
    return near_pairs, far_pairs


def last_pairs(first_row, width, row_count, column_count):
    slots = row_count * column_count
    off_pairs, on_pairs = [], []
    for slot in range(slots):
        if (slot + OUTER - 1) * width > first_row:
            target = slot + 1 if slot % 2 else slot - 1
            source = host_of(slot, row_count, column_count)
            off_pairs.append((source, target if 0 <= target < slots else slot))
            on_pairs.append((source, slot ^ 1))
    return off_pairs, on_pairs


def per_device(factor_tiles):
    cycles, rows, tiles, width = factor_tiles.shape
    count, columns = lax.axis_size("row"), lax.axis_size("col")
    half = width // 2
    length = cycles * rows * count
    axes = ("row", "col")
    split_bytes, spare = 6 * width * length, spare_bytes * length
    params = pltpu.CompilerParams(vmem_limit_bytes=split_bytes + spare)
    more_params = pltpu.CompilerParams(vmem_limit_bytes=2 * split_bytes + spare)
    split = pltpu.VMEM((3 * width, length), jnp.bfloat16)

    order = [(peer, part) for peer in range(tiles - 1, -1, -1) for part in range(PIECES - 1, -1, -1)]
    pieces = len(order)
    chunks = pl.pallas_call(
        functools.partial(prepare_kernel, order),
        in_specs=[pl.BlockSpec(memory_space=pltpu.HBM)],
        out_specs=in_vmem(pieces),
        out_shape=[jax.ShapeDtypeStruct((width, cycles * rows // PIECES), jnp.float32)] * pieces,
        scratch_shapes=[
            pltpu.VMEM((cycles, rows * tiles, width), jnp.float32),
            pltpu.SemaphoreType.DMA((cycles,)),
        ],
        compiler_params=params,
        name="prepare",
    )(pltpu.with_memory_space_constraint(factor_tiles.reshape(cycles, rows * tiles, width), pltpu.HBM))
    received = list(chunks)
    for place, (offset, piece) in enumerate(order):
        if offset:
            pairs = peer_pairs(offset, piece * (length // PIECES), width, count, columns)
            received[place] = lax.ppermute(chunks[place], axes, pairs)

    unit = length // UNITS
    near_starts = [0] + [cut * unit for cut in NEAR_CUTS]
    far_starts = [0] + [cut * unit for cut in FAR_CUTS]
    near_count = len(near_starts)
    halves = [
        jax.ShapeDtypeStruct((half, end - start), jnp.float32)
        for starts in (far_starts, near_starts)
        for start, end in zip(starts, starts[1:] + [length])
    ]
    moved = pl.pallas_call(
        functools.partial(first_kernel, order, near_count),
        in_specs=in_vmem(pieces),
        out_specs=in_vmem(len(halves)),
        out_shape=halves,
        scratch_shapes=[split],
        compiler_params=params,
        name="first_round",
    )(*received)
    far, near = list(moved[:-near_count]), list(moved[-near_count:])

    def swapped(value, first_row, side):
        return lax.ppermute(value, axes, swap_pairs(first_row, width, count, columns)[side])

    far = [swapped(value, start, 1) for value, start in zip(far, far_starts)]
    near = [swapped(value, start, 0) for value, start in zip(near, near_starts)]
    last_starts = [0] + [cut * unit for cut in LAST_CUTS]
    sizes = len(last_starts)
    last_halves = [
        jax.ShapeDtypeStruct((half, end - start), jnp.float32)
        for start, end in zip(last_starts, last_starts[1:] + [length])
    ]
    last = pl.pallas_call(
        functools.partial(middle_kernel, near_count),
        in_specs=in_vmem(2 * len(halves)),
        out_specs=in_vmem(2 * sizes),
        out_shape=last_halves * 2,
        scratch_shapes=[split] * 2,
        compiler_params=more_params,
        name="middle_rounds",
    )(*far, *near, *moved)
    off, on = list(last[:sizes]), list(last[sizes:])
    for place, start in enumerate(last_starts):
        off_pairs, on_pairs = last_pairs(start, width, count, columns)
        off[place] = lax.ppermute(off[place], axes, off_pairs)
        on[place] = lax.ppermute(on[place], axes, on_pairs)
    return pl.pallas_call(
        last_kernel,
        in_specs=in_vmem(2 * sizes),
        out_specs=pl.BlockSpec(memory_space=pltpu.HBM),
        out_shape=jax.ShapeDtypeStruct((length, width), jnp.float32),
        scratch_shapes=[
            split,
            pltpu.VMEM((length, width), jnp.float32),
            pltpu.SemaphoreType.DMA((length // SPAN,)),
        ],
        compiler_params=params,
        name="last_round",
    )(*off, *on)


def solution(mesh):
    return jax.shard_map(
        per_device,
        mesh=mesh,
        in_specs=(P(None, "row", None, "col"),),
        out_specs=P(None, ("row", "col")),
        check_vma=False,
    )
```

```python
import functools

import jax
import jax.numpy as jnp
from jax import lax
from jax.experimental import pallas as pl
from jax.experimental.pallas import tpu as pltpu
from jax.sharding import PartitionSpec as P

LOGB = 7
OUTER = 4
INNER = 8
LANES = 128
SUBLANES = 8
SPAN = 512
DEPTH = 2048
UNROLLED = 4096
UNITS = 32
NEAR_CUTS = (10, 22)
FAR_CUTS = (16, 24)
LAST_CUTS = (18, 26)
PIECES = 2

damping_ratio = 0.01
spare_bytes = 2048


def partner_columns(value, stride):
    if 2 * stride == value.shape[-1]:
        return pltpu.roll(value, stride, 1)
    column = lax.broadcasted_iota(jnp.int32, value.shape, 1)
    return jnp.take_along_axis(value, jnp.bitwise_xor(column, stride), axis=1)


def partner_rows(value, stride):
    order = value.shape[0]
    if stride >= 8:
        pieces = [value[start : start + stride] for start in range(0, order, stride)]
        return jnp.concatenate([pieces[place ^ 1] for place in range(len(pieces))], axis=0)
    row = lax.broadcasted_iota(jnp.int32, value.shape, 0)
    is_tail = jnp.bitwise_and(row, stride) != 0
    return jnp.where(is_tail, pltpu.roll(value, stride, 0), pltpu.roll(value, order - stride, 0))


def turn_of(own, other, cross):
    gap = own - other
    total = own + other
    base = gap * gap + damping_ratio * total * total
    tangent = jnp.where(base > 0.0, 2.0 * cross * gap / jnp.where(base > 0.0, base, 1.0), 0.0)
    inverse = lax.rsqrt(1.0 + tangent * tangent)
    square = 0.5 + 0.5 * inverse
    root = lax.rsqrt(square)
    return square * root, 0.5 * tangent * inverse * root


def inner_solve(*grams):
    shape = grams[0].shape
    row = lax.broadcasted_iota(jnp.int32, shape, 0)
    column = lax.broadcasted_iota(jnp.int32, shape, 1)
    mixed = jnp.bitwise_xor(row, column)

    def line_of(lines, place):
        return jnp.broadcast_to(lines[place : place + 1], (SUBLANES, shape[1]))

    def spread(line):
        return jnp.broadcast_to(line[None], (shape[0] // SUBLANES, *line.shape)).reshape(shape)

    state = []
    for gram in grams:
        lines = gram
        for bit in range(LOGB):
            is_set = jnp.bitwise_and(column, 2**bit) != 0
            lines = jnp.where(is_set, partner_rows(lines, 2**bit), lines)
        start = jnp.where(row == column, 1.0, 0.0).astype(jnp.float32)
        state.append((lines, line_of(lines, 0), start))
    for step in range(INNER):
        stride = 2 ** ((LOGB - 1 - step) % LOGB)
        after = []
        for lines, own, turned in state:
            other = partner_columns(own, stride)
            cross = line_of(lines, stride)
            cosine, sine = turn_of(own, other, cross)
            own = cosine * (cosine * own + 2.0 * sine * cross) + sine * sine * other
            cosine, sine = spread(cosine), spread(sine)
            turned = turned * cosine + partner_columns(turned, stride) * sine
            if step + 1 < INNER:
                across = partner_rows(partner_columns(lines, stride), stride)
                lines = lines * cosine + across * sine
                cos_mixed = jnp.take_along_axis(cosine, mixed, axis=1)
                sin_mixed = jnp.take_along_axis(sine, mixed, axis=1)
                lines = lines * cos_mixed + partner_rows(lines, stride) * sin_mixed
            after.append((lines, own, turned))
        state = after
    return [turned.T for _, _, turned in state]


def three_parts(value):
    high = value.astype(jnp.bfloat16)
    rest = value - high.astype(jnp.float32)
    middle = rest.astype(jnp.bfloat16)
    return high, middle, (rest - middle.astype(jnp.float32)).astype(jnp.bfloat16)


def split_store(split_ref, value, start, lane):
    order = split_ref.shape[0] // 3
    rows, lanes = value.shape
    high, middle, low = three_parts(value)
    for place, part in enumerate((middle, high, low)):
        split_ref[pl.ds(place * order + start, rows), pl.ds(lane, lanes)] = part


def gram_of(split_ref):
    order = split_ref.shape[0] // 3
    total = split_ref.shape[1]

    def dot(start):
        lanes = pl.ds(start, DEPTH)
        return lax.dot_general(
            split_ref[:, lanes],
            split_ref[: 2 * order, lanes],
            (((1,), (1,)), ((), ())),
            preferred_element_type=jnp.float32,
        )

    if total <= UNROLLED:
        acc = dot(0)
        for start in range(DEPTH, total, DEPTH):
            acc = acc + dot(start)
    else:
        acc = lax.fori_loop(
            1,
            total // DEPTH,
            lambda place, acc: acc + dot(pl.multiple_of(place * DEPTH, DEPTH)),
            dot(0),
        )
    outer = acc[2 * order :, order:]
    inner = acc[:order, order:] + acc[order : 2 * order, :order] + acc[:order, :order]
    return acc[order : 2 * order, order:] + (inner + (outer + outer.T))


def product(turned, split_ref, lanes, terms=6):
    order = split_ref.shape[0] // 3
    rows = turned.shape[0]
    high, middle, low = three_parts(turned)

    def dot(weights, start):
        return lax.dot_general(
            jnp.concatenate([jnp.concatenate(pair, axis=1) for pair in weights], axis=0),
            split_ref[start : start + 2 * order, lanes],
            (((1,), (0,)), ((), ())),
            preferred_element_type=jnp.float32,
        )

    both = dot(((high, high), (middle, middle)), 0)
    if terms == 4:
        return both[:rows] + both[rows:]
    return both[:rows] + (both[rows:] + dot(((low, high),), order))


def spans(length, body):
    whole = length // SPAN * SPAN
    if length <= UNROLLED:
        for lane in range(0, whole, SPAN):
            body(lane, SPAN)
    else:

        def step(place, carry):
            body(pl.multiple_of(place * SPAN, SPAN), SPAN)
            return carry

        lax.fori_loop(0, length // SPAN, step, 0)
    if whole < length:
        body(whole, length - whole)


def load_rows(split_ref, refs, start):
    done = 0
    for ref in refs:

        def body(lane, size):
            split_store(split_ref, ref[:, pl.ds(lane, size)], start, done + lane)

        spans(ref.shape[1], body)
        done += ref.shape[1]


def cuts_of(refs):
    cuts = [0]
    for ref in refs:
        cuts.append(cuts[-1] + ref.shape[1])
    return cuts


def send_out(turned, split_ref, first_refs, second_refs, swap, terms=6):
    half = split_ref.shape[0] // 6
    swapped = jnp.concatenate([turned[half:], turned[:half]], axis=0)
    arranged = jnp.where(swap, swapped, turned)
    first_cuts, second_cuts = cuts_of(first_refs), cuts_of(second_refs)
    cuts = sorted(set(first_cuts + second_cuts))
    for begin, end in zip(cuts[:-1], cuts[1:]):
        first = max(place for place, cut in enumerate(first_cuts) if cut <= begin)
        second = max(place for place, cut in enumerate(second_cuts) if cut <= begin)
        first_lane, second_lane = begin - first_cuts[first], begin - second_cuts[second]

        def body(lane, size):
            lines = product(arranged, split_ref, pl.ds(begin + lane, size), terms)
            first_refs[first][:, pl.ds(first_lane + lane, size)] = lines[:half]
            second_refs[second][:, pl.ds(second_lane + lane, size)] = lines[half:]

        spans(end - begin, body)


def run_of(column, row, row_count, column_count):
    last = jnp.where(row == row_count - 1, row, row_count - 2 - row)
    odd = jnp.where(column == column_count - 1, last, row_count - 1 - row)
    return jnp.where(jnp.bitwise_and(column, 1) == 0, row, odd)


def hosted_slot():
    column, columns = lax.axis_index("col"), lax.axis_size("col")
    run = run_of(column, lax.axis_index("row"), lax.axis_size("row"), columns)
    return run * columns + column


def slot_count():
    return lax.axis_size("row") * lax.axis_size("col")


def prepare_kernel(order, in_ref, *refs):
    count = lax.axis_size("row")
    out_refs, buffer, ready = refs[:-2], refs[-2], refs[-1]
    cycles, rows = in_ref.shape[0], in_ref.shape[1] // count
    copies = [
        pltpu.make_async_copy(in_ref.at[cycle], buffer.at[cycle], ready.at[cycle])
        for cycle in range(cycles)
    ]
    for copy in copies:
        copy.start()
    me = lax.axis_index("row")
    column, columns = lax.axis_index("col"), lax.axis_size("col")
    per_piece = cycles // PIECES
    for cycle, copy in enumerate(copies):
        copy.wait()
        piece, place = divmod(cycle, per_piece)
        for offset in range(count):
            tile = run_of(column, jnp.bitwise_xor(me, offset), count, columns)
            out_ref = out_refs[order.index((offset, piece))]
            out_ref[:, place * rows : (place + 1) * rows] = buffer[
                cycle, pl.ds(tile, rows, stride=count), :
            ].T


def odd_chip(slot):
    return jnp.bitwise_and(slot // 2, 1)


def first_kernel(order, near_count, *refs):
    chunk_refs, out_refs, split_ref = refs[: len(order)], refs[len(order) : -1], refs[-1]
    me, count = lax.axis_index("row"), lax.axis_size("row")
    total = split_ref.shape[1]
    rows = split_ref.shape[0] // 3
    per_piece = total // (PIECES * count * rows)
    for (offset, piece), chunk_ref in zip(order, chunk_refs):
        peer = jnp.bitwise_xor(me, offset)
        for place in range(per_piece):
            lane = ((piece * per_piece + place) * count + peer) * rows
            split_store(
                split_ref,
                chunk_ref[:, place * rows : (place + 1) * rows],
                0,
                pl.multiple_of(lane, rows),
            )
    (turned,) = inner_solve(gram_of(split_ref))
    slot = hosted_slot()
    bottom_first = jnp.logical_or(odd_chip(slot) == 1, slot == 0)
    send_out(turned, split_ref, out_refs[-near_count:], out_refs[:-near_count], bottom_first)


def middle_kernel(near_count, *refs):
    sizes = len(LAST_CUTS) + 1
    near_ref, far_ref = refs[-2:]
    off_outs, on_outs = refs[-2 - 2 * sizes : -2 - sizes], refs[-2 - sizes : -2]
    halves = refs[: -2 - 2 * sizes]
    in_refs, own_refs = halves[: len(halves) // 2], halves[len(halves) // 2 :]
    far_in, near_in = in_refs[:-near_count], in_refs[-near_count:]
    second, first = own_refs[:-near_count], own_refs[-near_count:]
    slot, slots = hosted_slot(), slot_count()
    half = off_outs[0].shape[0]
    odd = odd_chip(slot)
    at_end = jnp.logical_or(slot == 0, slot == slots - 1).astype(jnp.int32)
    near_own = pl.multiple_of(odd * half, half)
    near_other = pl.multiple_of((1 - odd) * half, half)
    far_own = pl.multiple_of(jnp.bitwise_xor(1 - odd, at_end) * half, half)
    far_other = pl.multiple_of(jnp.bitwise_xor(odd, at_end) * half, half)
    load_rows(near_ref, first, near_own)
    load_rows(near_ref, near_in, near_other)
    load_rows(far_ref, second, far_own)
    load_rows(far_ref, far_in, far_other)
    near, far = inner_solve(gram_of(near_ref), gram_of(far_ref))
    near_half = jnp.where(odd == 0, near[half:], near[:half])
    flipped = jnp.logical_or(slot == 1, slot == slots - 1)
    far_bottom = jnp.logical_xor(odd == 1, flipped)
    far_half = jnp.where(far_bottom, far[half:], far[:half])

    def body(lane, size):
        near_lines = product(near_half, near_ref, pl.ds(lane, size))
        far_lines = product(far_half, far_ref, pl.ds(lane, size))
        split_store(near_ref, near_lines, near_other, lane)
        split_store(near_ref, far_lines, near_own, lane)

    spans(near_ref.shape[1], body)
    (turned,) = inner_solve(gram_of(near_ref))
    swap = jnp.logical_and(jnp.bitwise_and(slot, 1) == 0, slot != 0)
    send_out(turned, near_ref, off_outs, on_outs, swap, terms=4)


def last_kernel(*refs):
    out_ref, split_ref, buffer, done = refs[-4:]
    sizes = (len(refs) - 4) // 2
    off_in, on_in = refs[:sizes], refs[sizes:-4]
    half = off_in[0].shape[0]
    odd = jnp.bitwise_and(lax.axis_index("col"), 1)
    load_rows(split_ref, off_in, pl.multiple_of(odd * half, half))
    load_rows(split_ref, on_in, pl.multiple_of((1 - odd) * half, half))
    (turned,) = inner_solve(gram_of(split_ref))
    total = split_ref.shape[1]

    def copy_of(lane):
        rows = pl.ds(lane, SPAN)
        return pltpu.make_async_copy(buffer.at[rows], out_ref.at[rows], done.at[lane // SPAN])

    def body(lane, size):
        lines = product(turned, split_ref, pl.ds(lane, size), terms=4)
        for place in range(0, size, LANES):
            buffer[pl.ds(lane + place, LANES), :] = lines[:, place : place + LANES].T
        copy_of(lane).start()

    spans(total, body)
    spans(total, lambda lane, size: copy_of(lane).wait())


def in_vmem(count):
    return [pl.BlockSpec(memory_space=pltpu.VMEM)] * count


def host_of(slot, row_count, column_count):
    run, column = divmod(slot, column_count)
    row = run
    if column == column_count - 1:
        row = run if run == row_count - 1 else row_count - 2 - run
    elif column % 2:
        row = row_count - 1 - run
    return row * column_count + column


def peer_pairs(offset, first_row, width, row_count, column_count):
    pairs = []
    for row in range(row_count):
        for column in range(column_count):
            peer = (row ^ offset) * column_count + column
            slot = host_of(peer, row_count, column_count)
            if (slot + 1) * width > first_row:
                pairs.append((row * column_count + column, peer))
    return pairs


def swap_pairs(first_row, width, row_count, column_count):
    slots = row_count * column_count
    near_pairs, far_pairs = [], []
    for slot in range(slots):
        if (slot + 1) * width <= first_row:
            continue
        source = host_of(slot, row_count, column_count)
        step = -2 if slot // 2 % 2 else 2
        near_pairs.append((source, host_of(slot + step, row_count, column_count)))
        target = slot - step if 0 <= slot - step < slots else slot ^ 1
        far_pairs.append((source, host_of(target, row_count, column_count)))
    return near_pairs, far_pairs


def last_pairs(first_row, width, row_count, column_count):
    slots = row_count * column_count
    off_pairs, on_pairs = [], []
    for slot in range(slots):
        if (slot + OUTER - 1) * width > first_row:
            target = slot + 1 if slot % 2 else slot - 1
            source = host_of(slot, row_count, column_count)
            off_pairs.append((source, target if 0 <= target < slots else slot))
            on_pairs.append((source, slot ^ 1))
    return off_pairs, on_pairs


def per_device(factor_tiles):
    cycles, rows, tiles, width = factor_tiles.shape
    count, columns = lax.axis_size("row"), lax.axis_size("col")
    half = width // 2
    length = cycles * rows * count
    axes = ("row", "col")
    split_bytes, spare = 6 * width * length, spare_bytes * length
    params = pltpu.CompilerParams(vmem_limit_bytes=split_bytes + spare)
    more_params = pltpu.CompilerParams(vmem_limit_bytes=2 * split_bytes + spare)
    split = pltpu.VMEM((3 * width, length), jnp.bfloat16)

    order = [(peer, part) for peer in range(tiles - 1, -1, -1) for part in range(PIECES - 1, -1, -1)]
    pieces = len(order)
    chunks = pl.pallas_call(
        functools.partial(prepare_kernel, order),
        in_specs=[pl.BlockSpec(memory_space=pltpu.HBM)],
        out_specs=in_vmem(pieces),
        out_shape=[jax.ShapeDtypeStruct((width, cycles * rows // PIECES), jnp.float32)] * pieces,
        scratch_shapes=[
            pltpu.VMEM((cycles, rows * tiles, width), jnp.float32),
            pltpu.SemaphoreType.DMA((cycles,)),
        ],
        compiler_params=params,
        name="prepare",
    )(pltpu.with_memory_space_constraint(factor_tiles.reshape(cycles, rows * tiles, width), pltpu.HBM))
    received = list(chunks)
    for place, (offset, piece) in enumerate(order):
        if offset:
            pairs = peer_pairs(offset, piece * (length // PIECES), width, count, columns)
            received[place] = lax.ppermute(chunks[place], axes, pairs)

    unit = length // UNITS
    near_starts = [0] + [cut * unit for cut in NEAR_CUTS]
    far_starts = [0] + [cut * unit for cut in FAR_CUTS]
    near_count = len(near_starts)
    halves = [
        jax.ShapeDtypeStruct((half, end - start), jnp.float32)
        for starts in (far_starts, near_starts)
        for start, end in zip(starts, starts[1:] + [length])
    ]
    moved = pl.pallas_call(
        functools.partial(first_kernel, order, near_count),
        in_specs=in_vmem(pieces),
        out_specs=in_vmem(len(halves)),
        out_shape=halves,
        scratch_shapes=[split],
        compiler_params=params,
        name="first_round",
    )(*received)
    far, near = list(moved[:-near_count]), list(moved[-near_count:])

    def swapped(value, first_row, side):
        return lax.ppermute(value, axes, swap_pairs(first_row, width, count, columns)[side])

    far = [swapped(value, start, 1) for value, start in zip(far, far_starts)]
    near = [swapped(value, start, 0) for value, start in zip(near, near_starts)]
    last_starts = [0] + [cut * unit for cut in LAST_CUTS]
    sizes = len(last_starts)
    last_halves = [
        jax.ShapeDtypeStruct((half, end - start), jnp.float32)
        for start, end in zip(last_starts, last_starts[1:] + [length])
    ]
    last = pl.pallas_call(
        functools.partial(middle_kernel, near_count),
        in_specs=in_vmem(2 * len(halves)),
        out_specs=in_vmem(2 * sizes),
        out_shape=last_halves * 2,
        scratch_shapes=[split] * 2,
        compiler_params=more_params,
        name="middle_rounds",
    )(*far, *near, *moved)
    off, on = list(last[:sizes]), list(last[sizes:])
    for place, start in enumerate(last_starts):
        off_pairs, on_pairs = last_pairs(start, width, count, columns)
        off[place] = lax.ppermute(off[place], axes, off_pairs)
        on[place] = lax.ppermute(on[place], axes, on_pairs)
    return pl.pallas_call(
        last_kernel,
        in_specs=in_vmem(2 * sizes),
        out_specs=pl.BlockSpec(memory_space=pltpu.HBM),
        out_shape=jax.ShapeDtypeStruct((length, width), jnp.float32),
        scratch_shapes=[
            split,
            pltpu.VMEM((length, width), jnp.float32),
            pltpu.SemaphoreType.DMA((length // SPAN,)),
        ],
        compiler_params=params,
        name="last_round",
    )(*off, *on)


def solution(mesh):
    return jax.shard_map(
        per_device,
        mesh=mesh,
        in_specs=(P(None, "row", None, "col"),),
        out_specs=P(None, ("row", "col")),
        check_vma=False,
    )
```

```python
import functools

import jax
import jax.numpy as jnp
from jax import lax
from jax.experimental import pallas as pl
from jax.experimental.pallas import tpu as pltpu
from jax.sharding import PartitionSpec as P

LOGB = 7
OUTER = 4
INNER = 8
LANES = 128
SUBLANES = 8
SPAN = 256
DEPTH = 2048
UNROLLED = 4096
UNITS = 32
NEAR_CUTS = (10, 22)
FAR_CUTS = (16, 24)
LAST_CUTS = (18, 26)
PIECES = 2

damping_ratio = 0.01
spare_bytes = 2048


def partner_columns(value, stride):
    if 2 * stride == value.shape[-1]:
        return pltpu.roll(value, stride, 1)
    column = lax.broadcasted_iota(jnp.int32, value.shape, 1)
    return jnp.take_along_axis(value, jnp.bitwise_xor(column, stride), axis=1)


def partner_rows(value, stride):
    order = value.shape[0]
    if stride >= 8:
        pieces = [value[start : start + stride] for start in range(0, order, stride)]
        return jnp.concatenate([pieces[place ^ 1] for place in range(len(pieces))], axis=0)
    row = lax.broadcasted_iota(jnp.int32, value.shape, 0)
    is_tail = jnp.bitwise_and(row, stride) != 0
    return jnp.where(is_tail, pltpu.roll(value, stride, 0), pltpu.roll(value, order - stride, 0))


def turn_of(own, other, cross):
    gap = own - other
    total = own + other
    base = gap * gap + damping_ratio * total * total
    tangent = jnp.where(base > 0.0, 2.0 * cross * gap / jnp.where(base > 0.0, base, 1.0), 0.0)
    inverse = lax.rsqrt(1.0 + tangent * tangent)
    square = 0.5 + 0.5 * inverse
    root = lax.rsqrt(square)
    return square * root, 0.5 * tangent * inverse * root


def inner_solve(*grams):
    shape = grams[0].shape
    row = lax.broadcasted_iota(jnp.int32, shape, 0)
    column = lax.broadcasted_iota(jnp.int32, shape, 1)
    mixed = jnp.bitwise_xor(row, column)

    def line_of(lines, place):
        return jnp.broadcast_to(lines[place : place + 1], (SUBLANES, shape[1]))

    def spread(line):
        return jnp.broadcast_to(line[None], (shape[0] // SUBLANES, *line.shape)).reshape(shape)

    state = []
    for gram in grams:
        lines = gram
        for bit in range(LOGB):
            is_set = jnp.bitwise_and(column, 2**bit) != 0
            lines = jnp.where(is_set, partner_rows(lines, 2**bit), lines)
        start = jnp.where(row == column, 1.0, 0.0).astype(jnp.float32)
        state.append((lines, line_of(lines, 0), start))
    for step in range(INNER):
        stride = 2 ** ((LOGB - 1 - step) % LOGB)
        after = []
        for lines, own, turned in state:
            other = partner_columns(own, stride)
            cross = line_of(lines, stride)
            cosine, sine = turn_of(own, other, cross)
            own = cosine * (cosine * own + 2.0 * sine * cross) + sine * sine * other
            cosine, sine = spread(cosine), spread(sine)
            turned = turned * cosine + partner_columns(turned, stride) * sine
            if step + 1 < INNER:
                across = partner_rows(partner_columns(lines, stride), stride)
                lines = lines * cosine + across * sine
                cos_mixed = jnp.take_along_axis(cosine, mixed, axis=1)
                sin_mixed = jnp.take_along_axis(sine, mixed, axis=1)
                lines = lines * cos_mixed + partner_rows(lines, stride) * sin_mixed
            after.append((lines, own, turned))
        state = after
    return [turned.T for _, _, turned in state]


def three_parts(value):
    high = value.astype(jnp.bfloat16)
    rest = value - high.astype(jnp.float32)
    middle = rest.astype(jnp.bfloat16)
    return high, middle, (rest - middle.astype(jnp.float32)).astype(jnp.bfloat16)


def split_store(split_ref, value, start, lane):
    order = split_ref.shape[0] // 3
    rows, lanes = value.shape
    high, middle, low = three_parts(value)
    for place, part in enumerate((middle, high, low)):
        split_ref[pl.ds(place * order + start, rows), pl.ds(lane, lanes)] = part


def gram_of(split_ref):
    order = split_ref.shape[0] // 3
    total = split_ref.shape[1]

    def body(place, acc):
        lanes = pl.ds(pl.multiple_of(place * DEPTH, DEPTH), DEPTH)
        return acc + lax.dot_general(
            split_ref[:, lanes],
            split_ref[: 2 * order, lanes],
            (((1,), (1,)), ((), ())),
            preferred_element_type=jnp.float32,
        )

    acc = lax.fori_loop(0, total // DEPTH, body, jnp.zeros((3 * order, 2 * order), jnp.float32))
    outer = acc[2 * order :, order:]
    inner = acc[:order, order:] + acc[order : 2 * order, :order] + acc[:order, :order]
    return acc[order : 2 * order, order:] + (inner + (outer + outer.T))


def product(turned, split_ref, lanes, terms=6):
    order = split_ref.shape[0] // 3
    rows = turned.shape[0]
    high, middle, low = three_parts(turned)

    def dot(weights, start):
        return lax.dot_general(
            jnp.concatenate([jnp.concatenate(pair, axis=1) for pair in weights], axis=0),
            split_ref[start : start + 2 * order, lanes],
            (((1,), (0,)), ((), ())),
            preferred_element_type=jnp.float32,
        )

    both = dot(((high, high), (middle, middle)), 0)
    if terms == 4:
        return both[:rows] + both[rows:]
    return both[:rows] + (both[rows:] + dot(((low, high),), order))


def spans(length, body):
    whole = length // SPAN * SPAN
    if length <= UNROLLED:
        for lane in range(0, whole, SPAN):
            body(lane, SPAN)
    else:

        def step(place, carry):
            body(pl.multiple_of(place * SPAN, SPAN), SPAN)
            return carry

        lax.fori_loop(0, length // SPAN, step, 0)
    if whole < length:
        body(whole, length - whole)


def load_rows(split_ref, refs, start):
    done = 0
    for ref in refs:

        def body(lane, size):
            split_store(split_ref, ref[:, pl.ds(lane, size)], start, done + lane)

        spans(ref.shape[1], body)
        done += ref.shape[1]


def cuts_of(refs):
    cuts = [0]
    for ref in refs:
        cuts.append(cuts[-1] + ref.shape[1])
    return cuts


def send_out(turned, split_ref, first_refs, second_refs, swap, terms=6):
    half = split_ref.shape[0] // 6
    swapped = jnp.concatenate([turned[half:], turned[:half]], axis=0)
    arranged = jnp.where(swap, swapped, turned)
    first_cuts, second_cuts = cuts_of(first_refs), cuts_of(second_refs)
    cuts = sorted(set(first_cuts + second_cuts))
    for begin, end in zip(cuts[:-1], cuts[1:]):
        first = max(place for place, cut in enumerate(first_cuts) if cut <= begin)
        second = max(place for place, cut in enumerate(second_cuts) if cut <= begin)
        first_lane, second_lane = begin - first_cuts[first], begin - second_cuts[second]

        def body(lane, size):
            lines = product(arranged, split_ref, pl.ds(begin + lane, size), terms)
            first_refs[first][:, pl.ds(first_lane + lane, size)] = lines[:half]
            second_refs[second][:, pl.ds(second_lane + lane, size)] = lines[half:]

        spans(end - begin, body)


def run_of(column, row, row_count, column_count):
    last = jnp.where(row == row_count - 1, row, row_count - 2 - row)
    odd = jnp.where(column == column_count - 1, last, row_count - 1 - row)
    return jnp.where(jnp.bitwise_and(column, 1) == 0, row, odd)


def hosted_slot():
    column, columns = lax.axis_index("col"), lax.axis_size("col")
    run = run_of(column, lax.axis_index("row"), lax.axis_size("row"), columns)
    return run * columns + column


def slot_count():
    return lax.axis_size("row") * lax.axis_size("col")


def prepare_kernel(order, in_ref, *refs):
    count = lax.axis_size("row")
    out_refs, buffer, ready = refs[:-2], refs[-2], refs[-1]
    cycles, rows = in_ref.shape[0], in_ref.shape[1] // count
    copies = [
        pltpu.make_async_copy(in_ref.at[cycle], buffer.at[cycle], ready.at[cycle])
        for cycle in range(cycles)
    ]
    for copy in copies:
        copy.start()
    me = lax.axis_index("row")
    column, columns = lax.axis_index("col"), lax.axis_size("col")
    per_piece = cycles // PIECES
    for cycle, copy in enumerate(copies):
        copy.wait()
        piece, place = divmod(cycle, per_piece)
        for offset in range(count):
            tile = run_of(column, jnp.bitwise_xor(me, offset), count, columns)
            out_ref = out_refs[order.index((offset, piece))]
            out_ref[:, place * rows : (place + 1) * rows] = buffer[
                cycle, pl.ds(tile, rows, stride=count), :
            ].T


def odd_chip(slot):
    return jnp.bitwise_and(slot // 2, 1)


def first_kernel(order, near_count, *refs):
    chunk_refs, out_refs, split_ref = refs[: len(order)], refs[len(order) : -1], refs[-1]
    me, count = lax.axis_index("row"), lax.axis_size("row")
    total = split_ref.shape[1]
    rows = split_ref.shape[0] // 3
    per_piece = total // (PIECES * count * rows)
    for (offset, piece), chunk_ref in zip(order, chunk_refs):
        peer = jnp.bitwise_xor(me, offset)
        for place in range(per_piece):
            lane = ((piece * per_piece + place) * count + peer) * rows
            split_store(
                split_ref,
                chunk_ref[:, place * rows : (place + 1) * rows],
                0,
                pl.multiple_of(lane, rows),
            )
    (turned,) = inner_solve(gram_of(split_ref))
    slot = hosted_slot()
    bottom_first = jnp.logical_or(odd_chip(slot) == 1, slot == 0)
    send_out(turned, split_ref, out_refs[-near_count:], out_refs[:-near_count], bottom_first)


def middle_kernel(near_count, *refs):
    sizes = len(LAST_CUTS) + 1
    near_ref, far_ref = refs[-2:]
    off_outs, on_outs = refs[-2 - 2 * sizes : -2 - sizes], refs[-2 - sizes : -2]
    halves = refs[: -2 - 2 * sizes]
    in_refs, own_refs = halves[: len(halves) // 2], halves[len(halves) // 2 :]
    far_in, near_in = in_refs[:-near_count], in_refs[-near_count:]
    second, first = own_refs[:-near_count], own_refs[-near_count:]
    slot, slots = hosted_slot(), slot_count()
    half = off_outs[0].shape[0]
    odd = odd_chip(slot)
    at_end = jnp.logical_or(slot == 0, slot == slots - 1).astype(jnp.int32)
    near_own = pl.multiple_of(odd * half, half)
    near_other = pl.multiple_of((1 - odd) * half, half)
    far_own = pl.multiple_of(jnp.bitwise_xor(1 - odd, at_end) * half, half)
    far_other = pl.multiple_of(jnp.bitwise_xor(odd, at_end) * half, half)
    load_rows(near_ref, first, near_own)
    load_rows(near_ref, near_in, near_other)
    load_rows(far_ref, second, far_own)
    load_rows(far_ref, far_in, far_other)
    near, far = inner_solve(gram_of(near_ref), gram_of(far_ref))
    near_half = jnp.where(odd == 0, near[half:], near[:half])
    flipped = jnp.logical_or(slot == 1, slot == slots - 1)
    far_bottom = jnp.logical_xor(odd == 1, flipped)
    far_half = jnp.where(far_bottom, far[half:], far[:half])

    def body(lane, size):
        near_lines = product(near_half, near_ref, pl.ds(lane, size))
        far_lines = product(far_half, far_ref, pl.ds(lane, size))
        split_store(near_ref, near_lines, near_other, lane)
        split_store(near_ref, far_lines, near_own, lane)

    spans(near_ref.shape[1], body)
    (turned,) = inner_solve(gram_of(near_ref))
    swap = jnp.logical_and(jnp.bitwise_and(slot, 1) == 0, slot != 0)
    send_out(turned, near_ref, off_outs, on_outs, swap, terms=4)


def last_kernel(*refs):
    out_ref, split_ref, buffer, done = refs[-4:]
    sizes = (len(refs) - 4) // 2
    off_in, on_in = refs[:sizes], refs[sizes:-4]
    half = off_in[0].shape[0]
    odd = jnp.bitwise_and(lax.axis_index("col"), 1)
    load_rows(split_ref, off_in, pl.multiple_of(odd * half, half))
    load_rows(split_ref, on_in, pl.multiple_of((1 - odd) * half, half))
    (turned,) = inner_solve(gram_of(split_ref))
    total = split_ref.shape[1]

    def copy_of(lane):
        rows = pl.ds(lane, SPAN)
        return pltpu.make_async_copy(buffer.at[rows], out_ref.at[rows], done.at[lane // SPAN])

    def body(lane, size):
        lines = product(turned, split_ref, pl.ds(lane, size), terms=4)
        for place in range(0, size, LANES):
            buffer[pl.ds(lane + place, LANES), :] = lines[:, place : place + LANES].T
        copy_of(lane).start()

    spans(total, body)
    spans(total, lambda lane, size: copy_of(lane).wait())


def in_vmem(count):
    return [pl.BlockSpec(memory_space=pltpu.VMEM)] * count


def host_of(slot, row_count, column_count):
    run, column = divmod(slot, column_count)
    row = run
    if column == column_count - 1:
        row = run if run == row_count - 1 else row_count - 2 - run
    elif column % 2:
        row = row_count - 1 - run
    return row * column_count + column


def peer_pairs(offset, first_row, width, row_count, column_count):
    pairs = []
    for row in range(row_count):
        for column in range(column_count):
            peer = (row ^ offset) * column_count + column
            slot = host_of(peer, row_count, column_count)
            if (slot + 1) * width > first_row:
                pairs.append((row * column_count + column, peer))
    return pairs


def swap_pairs(first_row, width, row_count, column_count):
    slots = row_count * column_count
    near_pairs, far_pairs = [], []
    for slot in range(slots):
        if (slot + 1) * width <= first_row:
            continue
        source = host_of(slot, row_count, column_count)
        step = -2 if slot // 2 % 2 else 2
        near_pairs.append((source, host_of(slot + step, row_count, column_count)))
        target = slot - step if 0 <= slot - step < slots else slot ^ 1
        far_pairs.append((source, host_of(target, row_count, column_count)))
    return near_pairs, far_pairs


def last_pairs(first_row, width, row_count, column_count):
    slots = row_count * column_count
    off_pairs, on_pairs = [], []
    for slot in range(slots):
        if (slot + OUTER - 1) * width > first_row:
            target = slot + 1 if slot % 2 else slot - 1
            source = host_of(slot, row_count, column_count)
            off_pairs.append((source, target if 0 <= target < slots else slot))
            on_pairs.append((source, slot ^ 1))
    return off_pairs, on_pairs


def per_device(factor_tiles):
    cycles, rows, tiles, width = factor_tiles.shape
    count, columns = lax.axis_size("row"), lax.axis_size("col")
    half = width // 2
    length = cycles * rows * count
    axes = ("row", "col")
    split_bytes, spare = 6 * width * length, spare_bytes * length
    params = pltpu.CompilerParams(vmem_limit_bytes=split_bytes + spare)
    more_params = pltpu.CompilerParams(vmem_limit_bytes=2 * split_bytes + spare)
    split = pltpu.VMEM((3 * width, length), jnp.bfloat16)

    order = [(peer, part) for peer in range(tiles - 1, -1, -1) for part in range(PIECES - 1, -1, -1)]
    pieces = len(order)
    chunks = pl.pallas_call(
        functools.partial(prepare_kernel, order),
        in_specs=[pl.BlockSpec(memory_space=pltpu.HBM)],
        out_specs=in_vmem(pieces),
        out_shape=[jax.ShapeDtypeStruct((width, cycles * rows // PIECES), jnp.float32)] * pieces,
        scratch_shapes=[
            pltpu.VMEM((cycles, rows * tiles, width), jnp.float32),
            pltpu.SemaphoreType.DMA((cycles,)),
        ],
        compiler_params=params,
        name="prepare",
    )(pltpu.with_memory_space_constraint(factor_tiles.reshape(cycles, rows * tiles, width), pltpu.HBM))
    received = list(chunks)
    for place, (offset, piece) in enumerate(order):
        if offset:
            pairs = peer_pairs(offset, piece * (length // PIECES), width, count, columns)
            received[place] = lax.ppermute(chunks[place], axes, pairs)

    unit = length // UNITS
    near_starts = [0] + [cut * unit for cut in NEAR_CUTS]
    far_starts = [0] + [cut * unit for cut in FAR_CUTS]
    near_count = len(near_starts)
    halves = [
        jax.ShapeDtypeStruct((half, end - start), jnp.float32)
        for starts in (far_starts, near_starts)
        for start, end in zip(starts, starts[1:] + [length])
    ]
    moved = pl.pallas_call(
        functools.partial(first_kernel, order, near_count),
        in_specs=in_vmem(pieces),
        out_specs=in_vmem(len(halves)),
        out_shape=halves,
        scratch_shapes=[split],
        compiler_params=params,
        name="first_round",
    )(*received)
    far, near = list(moved[:-near_count]), list(moved[-near_count:])

    def swapped(value, first_row, side):
        return lax.ppermute(value, axes, swap_pairs(first_row, width, count, columns)[side])

    far = [swapped(value, start, 1) for value, start in zip(far, far_starts)]
    near = [swapped(value, start, 0) for value, start in zip(near, near_starts)]
    last_starts = [0] + [cut * unit for cut in LAST_CUTS]
    sizes = len(last_starts)
    last_halves = [
        jax.ShapeDtypeStruct((half, end - start), jnp.float32)
        for start, end in zip(last_starts, last_starts[1:] + [length])
    ]
    last = pl.pallas_call(
        functools.partial(middle_kernel, near_count),
        in_specs=in_vmem(2 * len(halves)),
        out_specs=in_vmem(2 * sizes),
        out_shape=last_halves * 2,
        scratch_shapes=[split] * 2,
        compiler_params=more_params,
        name="middle_rounds",
    )(*far, *near, *moved)
    off, on = list(last[:sizes]), list(last[sizes:])
    for place, start in enumerate(last_starts):
        off_pairs, on_pairs = last_pairs(start, width, count, columns)
        off[place] = lax.ppermute(off[place], axes, off_pairs)
        on[place] = lax.ppermute(on[place], axes, on_pairs)
    return pl.pallas_call(
        last_kernel,
        in_specs=in_vmem(2 * sizes),
        out_specs=pl.BlockSpec(memory_space=pltpu.HBM),
        out_shape=jax.ShapeDtypeStruct((length, width), jnp.float32),
        scratch_shapes=[
            split,
            pltpu.VMEM((length, width), jnp.float32),
            pltpu.SemaphoreType.DMA((length // SPAN,)),
        ],
        compiler_params=params,
        name="last_round",
    )(*off, *on)


def solution(mesh):
    return jax.shard_map(
        per_device,
        mesh=mesh,
        in_specs=(P(None, "row", None, "col"),),
        out_specs=P(None, ("row", "col")),
        check_vma=False,
    )
```

```python
import functools

import jax
import jax.numpy as jnp
from jax import lax
from jax.experimental import pallas as pl
from jax.experimental.pallas import tpu as pltpu
from jax.sharding import PartitionSpec as P

LOGB = 7
OUTER = 4
INNER = 8
LANES = 128
SUBLANES = 8
SPAN = 512
DEPTH = 2048
UNROLLED = 4096
UNITS = 32
NEAR_CUTS = (10, 22)
FAR_CUTS = (16, 24)
LAST_CUTS = (18, 26)
ON_CUTS = (18,)
PIECES = 2

damping_ratio = 0.01
spare_bytes = 2048


def partner_columns(value, stride):
    if 2 * stride == value.shape[-1]:
        return pltpu.roll(value, stride, 1)
    column = lax.broadcasted_iota(jnp.int32, value.shape, 1)
    return jnp.take_along_axis(value, jnp.bitwise_xor(column, stride), axis=1)


def partner_rows(value, stride):
    order = value.shape[0]
    if stride >= 8:
        pieces = [value[start : start + stride] for start in range(0, order, stride)]
        return jnp.concatenate([pieces[place ^ 1] for place in range(len(pieces))], axis=0)
    row = lax.broadcasted_iota(jnp.int32, value.shape, 0)
    is_tail = jnp.bitwise_and(row, stride) != 0
    return jnp.where(is_tail, pltpu.roll(value, stride, 0), pltpu.roll(value, order - stride, 0))


def turn_of(own, other, cross):
    gap = own - other
    total = own + other
    base = gap * gap + damping_ratio * total * total
    tangent = jnp.where(base > 0.0, 2.0 * cross * gap / jnp.where(base > 0.0, base, 1.0), 0.0)
    inverse = lax.rsqrt(1.0 + tangent * tangent)
    square = 0.5 + 0.5 * inverse
    root = lax.rsqrt(square)
    return square * root, 0.5 * tangent * inverse * root


def inner_solve(*grams):
    shape = grams[0].shape
    row = lax.broadcasted_iota(jnp.int32, shape, 0)
    column = lax.broadcasted_iota(jnp.int32, shape, 1)
    mixed = jnp.bitwise_xor(row, column)

    def line_of(lines, place):
        return jnp.broadcast_to(lines[place : place + 1], (SUBLANES, shape[1]))

    def spread(line):
        return jnp.broadcast_to(line[None], (shape[0] // SUBLANES, *line.shape)).reshape(shape)

    state = []
    for gram in grams:
        lines = gram
        for bit in range(LOGB):
            is_set = jnp.bitwise_and(column, 2**bit) != 0
            lines = jnp.where(is_set, partner_rows(lines, 2**bit), lines)
        start = jnp.where(row == column, 1.0, 0.0).astype(jnp.float32)
        state.append((lines, line_of(lines, 0), start))
    for step in range(INNER):
        stride = 2 ** ((LOGB - 1 - step) % LOGB)
        after = []
        for lines, own, turned in state:
            other = partner_columns(own, stride)
            cross = line_of(lines, stride)
            cosine, sine = turn_of(own, other, cross)
            own = cosine * (cosine * own + 2.0 * sine * cross) + sine * sine * other
            cosine, sine = spread(cosine), spread(sine)
            turned = turned * cosine + partner_columns(turned, stride) * sine
            if step + 1 < INNER:
                across = partner_rows(partner_columns(lines, stride), stride)
                lines = lines * cosine + across * sine
                cos_mixed = jnp.take_along_axis(cosine, mixed, axis=1)
                sin_mixed = jnp.take_along_axis(sine, mixed, axis=1)
                lines = lines * cos_mixed + partner_rows(lines, stride) * sin_mixed
            after.append((lines, own, turned))
        state = after
    return [turned.T for _, _, turned in state]


def three_parts(value):
    high = value.astype(jnp.bfloat16)
    rest = value - high.astype(jnp.float32)
    middle = rest.astype(jnp.bfloat16)
    return high, middle, (rest - middle.astype(jnp.float32)).astype(jnp.bfloat16)


def split_store(split_ref, value, start, lane):
    order = split_ref.shape[0] // 3
    rows, lanes = value.shape
    high, middle, low = three_parts(value)
    for place, part in enumerate((middle, high, low)):
        split_ref[pl.ds(place * order + start, rows), pl.ds(lane, lanes)] = part


def gram_of(split_ref):
    order = split_ref.shape[0] // 3
    total = split_ref.shape[1]

    def body(place, acc):
        lanes = pl.ds(pl.multiple_of(place * DEPTH, DEPTH), DEPTH)
        return acc + lax.dot_general(
            split_ref[:, lanes],
            split_ref[: 2 * order, lanes],
            (((1,), (1,)), ((), ())),
            preferred_element_type=jnp.float32,
        )

    acc = lax.fori_loop(0, total // DEPTH, body, jnp.zeros((3 * order, 2 * order), jnp.float32))
    outer = acc[2 * order :, order:]
    inner = acc[:order, order:] + acc[order : 2 * order, :order] + acc[:order, :order]
    return acc[order : 2 * order, order:] + (inner + (outer + outer.T))


def product(turned, split_ref, lanes, terms=6):
    order = split_ref.shape[0] // 3
    rows = turned.shape[0]
    high, middle, low = three_parts(turned)

    def dot(weights, start):
        return lax.dot_general(
            jnp.concatenate([jnp.concatenate(pair, axis=1) for pair in weights], axis=0),
            split_ref[start : start + 2 * order, lanes],
            (((1,), (0,)), ((), ())),
            preferred_element_type=jnp.float32,
        )

    both = dot(((high, high), (middle, middle)), 0)
    if terms == 4:
        return both[:rows] + both[rows:]
    return both[:rows] + (both[rows:] + dot(((low, high),), order))


def spans(length, body):
    whole = length // SPAN * SPAN
    if length <= UNROLLED:
        for lane in range(0, whole, SPAN):
            body(lane, SPAN)
    else:

        def step(place, carry):
            body(pl.multiple_of(place * SPAN, SPAN), SPAN)
            return carry

        lax.fori_loop(0, length // SPAN, step, 0)
    if whole < length:
        body(whole, length - whole)


def load_rows(split_ref, refs, start):
    done = 0
    for ref in refs:

        def body(lane, size):
            split_store(split_ref, ref[:, pl.ds(lane, size)], start, done + lane)

        spans(ref.shape[1], body)
        done += ref.shape[1]


def cuts_of(refs):
    cuts = [0]
    for ref in refs:
        cuts.append(cuts[-1] + ref.shape[1])
    return cuts


def send_out(turned, split_ref, first_refs, second_refs, swap, terms=6):
    half = split_ref.shape[0] // 6
    swapped = jnp.concatenate([turned[half:], turned[:half]], axis=0)
    arranged = jnp.where(swap, swapped, turned)
    first_cuts, second_cuts = cuts_of(first_refs), cuts_of(second_refs)
    cuts = sorted(set(first_cuts + second_cuts))
    for begin, end in zip(cuts[:-1], cuts[1:]):
        first = max(place for place, cut in enumerate(first_cuts) if cut <= begin)
        second = max(place for place, cut in enumerate(second_cuts) if cut <= begin)
        first_lane, second_lane = begin - first_cuts[first], begin - second_cuts[second]

        def body(lane, size):
            lines = product(arranged, split_ref, pl.ds(begin + lane, size), terms)
            first_refs[first][:, pl.ds(first_lane + lane, size)] = lines[:half]
            second_refs[second][:, pl.ds(second_lane + lane, size)] = lines[half:]

        spans(end - begin, body)


def run_of(column, row, row_count, column_count):
    last = jnp.where(row == row_count - 1, row, row_count - 2 - row)
    odd = jnp.where(column == column_count - 1, last, row_count - 1 - row)
    return jnp.where(jnp.bitwise_and(column, 1) == 0, row, odd)


def hosted_slot():
    column, columns = lax.axis_index("col"), lax.axis_size("col")
    run = run_of(column, lax.axis_index("row"), lax.axis_size("row"), columns)
    return run * columns + column


def slot_count():
    return lax.axis_size("row") * lax.axis_size("col")


def prepare_kernel(order, in_ref, *refs):
    count = lax.axis_size("row")
    out_refs, buffer, ready = refs[:-2], refs[-2], refs[-1]
    cycles, rows = in_ref.shape[0], in_ref.shape[1] // count
    copies = [
        pltpu.make_async_copy(in_ref.at[cycle], buffer.at[cycle], ready.at[cycle])
        for cycle in range(cycles)
    ]
    for copy in copies:
        copy.start()
    me = lax.axis_index("row")
    column, columns = lax.axis_index("col"), lax.axis_size("col")
    per_piece = cycles // PIECES
    for cycle, copy in enumerate(copies):
        copy.wait()
        piece, place = divmod(cycle, per_piece)
        for offset in range(count):
            tile = run_of(column, jnp.bitwise_xor(me, offset), count, columns)
            out_ref = out_refs[order.index((offset, piece))]
            out_ref[:, place * rows : (place + 1) * rows] = buffer[
                cycle, pl.ds(tile, rows, stride=count), :
            ].T


def odd_chip(slot):
    return jnp.bitwise_and(slot // 2, 1)


def first_kernel(order, near_count, *refs):
    chunk_refs, out_refs, split_ref = refs[: len(order)], refs[len(order) : -1], refs[-1]
    me, count = lax.axis_index("row"), lax.axis_size("row")
    total = split_ref.shape[1]
    rows = split_ref.shape[0] // 3
    per_piece = total // (PIECES * count * rows)
    for (offset, piece), chunk_ref in zip(order, chunk_refs):
        peer = jnp.bitwise_xor(me, offset)
        for place in range(per_piece):
            lane = ((piece * per_piece + place) * count + peer) * rows
            split_store(
                split_ref,
                chunk_ref[:, place * rows : (place + 1) * rows],
                0,
                pl.multiple_of(lane, rows),
            )
    (turned,) = inner_solve(gram_of(split_ref))
    slot = hosted_slot()
    bottom_first = jnp.logical_or(odd_chip(slot) == 1, slot == 0)
    send_out(turned, split_ref, out_refs[-near_count:], out_refs[:-near_count], bottom_first)


def middle_kernel(near_count, *refs):
    off_count, on_count = len(LAST_CUTS) + 1, len(ON_CUTS) + 1
    near_ref, far_ref = refs[-2:]
    off_outs, on_outs = refs[-2 - on_count - off_count : -2 - on_count], refs[-2 - on_count : -2]
    halves = refs[: -2 - on_count - off_count]
    in_refs, own_refs = halves[: len(halves) // 2], halves[len(halves) // 2 :]
    far_in, near_in = in_refs[:-near_count], in_refs[-near_count:]
    second, first = own_refs[:-near_count], own_refs[-near_count:]
    slot, slots = hosted_slot(), slot_count()
    half = off_outs[0].shape[0]
    odd = odd_chip(slot)
    at_end = jnp.logical_or(slot == 0, slot == slots - 1).astype(jnp.int32)
    near_own = pl.multiple_of(odd * half, half)
    near_other = pl.multiple_of((1 - odd) * half, half)
    far_own = pl.multiple_of(jnp.bitwise_xor(1 - odd, at_end) * half, half)
    far_other = pl.multiple_of(jnp.bitwise_xor(odd, at_end) * half, half)
    load_rows(near_ref, first, near_own)
    load_rows(near_ref, near_in, near_other)
    load_rows(far_ref, second, far_own)
    load_rows(far_ref, far_in, far_other)
    near, far = inner_solve(gram_of(near_ref), gram_of(far_ref))
    near_half = jnp.where(odd == 0, near[half:], near[:half])
    flipped = jnp.logical_or(slot == 1, slot == slots - 1)
    far_bottom = jnp.logical_xor(odd == 1, flipped)
    far_half = jnp.where(far_bottom, far[half:], far[:half])

    def body(lane, size):
        near_lines = product(near_half, near_ref, pl.ds(lane, size))
        far_lines = product(far_half, far_ref, pl.ds(lane, size))
        split_store(near_ref, near_lines, near_other, lane)
        split_store(near_ref, far_lines, near_own, lane)

    spans(near_ref.shape[1], body)
    (turned,) = inner_solve(gram_of(near_ref))
    swap = jnp.logical_and(jnp.bitwise_and(slot, 1) == 0, slot != 0)
    send_out(turned, near_ref, off_outs, on_outs, swap, terms=4)


def last_kernel(*refs):
    out_ref, split_ref, buffer, done = refs[-4:]
    off_count = len(LAST_CUTS) + 1
    off_in, on_in = refs[:off_count], refs[off_count:-4]
    half = off_in[0].shape[0]
    odd = jnp.bitwise_and(lax.axis_index("col"), 1)
    load_rows(split_ref, off_in, pl.multiple_of(odd * half, half))
    load_rows(split_ref, on_in, pl.multiple_of((1 - odd) * half, half))
    (turned,) = inner_solve(gram_of(split_ref))
    total = split_ref.shape[1]

    def copy_of(lane):
        rows = pl.ds(lane, SPAN)
        return pltpu.make_async_copy(buffer.at[rows], out_ref.at[rows], done.at[lane // SPAN])

    def body(lane, size):
        lines = product(turned, split_ref, pl.ds(lane, size), terms=4)
        for place in range(0, size, LANES):
            buffer[pl.ds(lane + place, LANES), :] = lines[:, place : place + LANES].T
        copy_of(lane).start()

    spans(total, body)
    spans(total, lambda lane, size: copy_of(lane).wait())


def in_vmem(count):
    return [pl.BlockSpec(memory_space=pltpu.VMEM)] * count


def host_of(slot, row_count, column_count):
    run, column = divmod(slot, column_count)
    row = run
    if column == column_count - 1:
        row = run if run == row_count - 1 else row_count - 2 - run
    elif column % 2:
        row = row_count - 1 - run
    return row * column_count + column


def peer_pairs(offset, first_row, width, row_count, column_count):
    pairs = []
    for row in range(row_count):
        for column in range(column_count):
            peer = (row ^ offset) * column_count + column
            slot = host_of(peer, row_count, column_count)
            if (slot + 1) * width > first_row:
                pairs.append((row * column_count + column, peer))
    return pairs


def swap_pairs(first_row, width, row_count, column_count):
    slots = row_count * column_count
    near_pairs, far_pairs = [], []
    for slot in range(slots):
        if (slot + 1) * width <= first_row:
            continue
        source = host_of(slot, row_count, column_count)
        step = -2 if slot // 2 % 2 else 2
        near_pairs.append((source, host_of(slot + step, row_count, column_count)))
        target = slot - step if 0 <= slot - step < slots else slot ^ 1
        far_pairs.append((source, host_of(target, row_count, column_count)))
    return near_pairs, far_pairs


def last_pairs(first_row, width, row_count, column_count):
    slots = row_count * column_count
    off_pairs, on_pairs = [], []
    for slot in range(slots):
        if (slot + OUTER - 1) * width > first_row:
            target = slot + 1 if slot % 2 else slot - 1
            source = host_of(slot, row_count, column_count)
            off_pairs.append((source, target if 0 <= target < slots else slot))
            on_pairs.append((source, slot ^ 1))
    return off_pairs, on_pairs


def per_device(factor_tiles):
    cycles, rows, tiles, width = factor_tiles.shape
    count, columns = lax.axis_size("row"), lax.axis_size("col")
    half = width // 2
    length = cycles * rows * count
    axes = ("row", "col")
    split_bytes, spare = 6 * width * length, spare_bytes * length
    params = pltpu.CompilerParams(vmem_limit_bytes=split_bytes + spare)
    more_params = pltpu.CompilerParams(vmem_limit_bytes=2 * split_bytes + spare)
    split = pltpu.VMEM((3 * width, length), jnp.bfloat16)

    order = [(peer, part) for peer in range(tiles - 1, -1, -1) for part in range(PIECES - 1, -1, -1)]
    pieces = len(order)
    chunks = pl.pallas_call(
        functools.partial(prepare_kernel, order),
        in_specs=[pl.BlockSpec(memory_space=pltpu.HBM)],
        out_specs=in_vmem(pieces),
        out_shape=[jax.ShapeDtypeStruct((width, cycles * rows // PIECES), jnp.float32)] * pieces,
        scratch_shapes=[
            pltpu.VMEM((cycles, rows * tiles, width), jnp.float32),
            pltpu.SemaphoreType.DMA((cycles,)),
        ],
        compiler_params=params,
        name="prepare",
    )(pltpu.with_memory_space_constraint(factor_tiles.reshape(cycles, rows * tiles, width), pltpu.HBM))
    received = list(chunks)
    for place, (offset, piece) in enumerate(order):
        if offset:
            pairs = peer_pairs(offset, piece * (length // PIECES), width, count, columns)
            received[place] = lax.ppermute(chunks[place], axes, pairs)

    unit = length // UNITS
    near_starts = [0] + [cut * unit for cut in NEAR_CUTS]
    far_starts = [0] + [cut * unit for cut in FAR_CUTS]
    near_count = len(near_starts)
    halves = [
        jax.ShapeDtypeStruct((half, end - start), jnp.float32)
        for starts in (far_starts, near_starts)
        for start, end in zip(starts, starts[1:] + [length])
    ]
    moved = pl.pallas_call(
        functools.partial(first_kernel, order, near_count),
        in_specs=in_vmem(pieces),
        out_specs=in_vmem(len(halves)),
        out_shape=halves,
        scratch_shapes=[split],
        compiler_params=params,
        name="first_round",
    )(*received)
    far, near = list(moved[:-near_count]), list(moved[-near_count:])

    def swapped(value, first_row, side):
        return lax.ppermute(value, axes, swap_pairs(first_row, width, count, columns)[side])

    far = [swapped(value, start, 1) for value, start in zip(far, far_starts)]
    near = [swapped(value, start, 0) for value, start in zip(near, near_starts)]
    off_starts = [0] + [cut * unit for cut in LAST_CUTS]
    on_starts = [0] + [cut * unit for cut in ON_CUTS]
    off_count = len(off_starts)
    last_halves = [
        jax.ShapeDtypeStruct((half, end - start), jnp.float32)
        for starts in (off_starts, on_starts)
        for start, end in zip(starts, starts[1:] + [length])
    ]
    last = pl.pallas_call(
        functools.partial(middle_kernel, near_count),
        in_specs=in_vmem(2 * len(halves)),
        out_specs=in_vmem(len(last_halves)),
        out_shape=last_halves,
        scratch_shapes=[split] * 2,
        compiler_params=more_params,
        name="middle_rounds",
    )(*far, *near, *moved)
    off, on = list(last[:off_count]), list(last[off_count:])
    for values, starts, side in ((off, off_starts, 0), (on, on_starts, 1)):
        for place, start in enumerate(starts):
            pairs = last_pairs(start, width, count, columns)[side]
            values[place] = lax.ppermute(values[place], axes, pairs)
    return pl.pallas_call(
        last_kernel,
        in_specs=in_vmem(len(last_halves)),
        out_specs=pl.BlockSpec(memory_space=pltpu.HBM),
        out_shape=jax.ShapeDtypeStruct((length, width), jnp.float32),
        scratch_shapes=[
            split,
            pltpu.VMEM((length, width), jnp.float32),
            pltpu.SemaphoreType.DMA((length // SPAN,)),
        ],
        compiler_params=params,
        name="last_round",
    )(*off, *on)


def solution(mesh):
    return jax.shard_map(
        per_device,
        mesh=mesh,
        in_specs=(P(None, "row", None, "col"),),
        out_specs=P(None, ("row", "col")),
        check_vma=False,
    )
```
